256 devices in a mesh: date: 32 (over z_lo, x, core), strip: 8 (over z_hi, y).
Axes of the slice: x: 4, y: 4, z: 8 (z_hi: 2, z_lo: 4; z = z_hi * 4 + z_lo), core: 2. Of those that a mesh axis runs over, the one named last changes fastest.
Arguments:
- slc: bfloat16 [64, 2, 256, 1024], P('date', None, 'strip'), as said below
- partner: int32 [4, 32, 2], P(None, 'date'), may hold values from 0 to 1, each once within a row
- valid: int32 [4, 64, 2], P(None, 'date'), may hold values from 0 to 256, as said below
Outputs:
- coherence: float32 [4, 64, 256, 1024], P(None, 'date', 'strip')
- filtered: float32 [4, 64, 2, 256, 1024], P(None, 'date', None, 'strip')
The draws below stay inside these ranges and needn't reach their ends.
Inputs may be any that keep to these rules, and one draw needn't show every extreme that they name: Each row partner[r, b, :] is a permutation of the 2 positions of a block. valid[r, i, 0] <= 128 < valid[r, i, 1]; date 0 is valid on all 256 rows in every round. `slc`: finite values.
All inputs are finite; a program needn't handle non-finite values.
Results may differ from the reference program's by a relative error of at most 0.0015.
Values may be sent and summed in bfloat16 or wider, within the bound.
A program may use at most 64 MiB of HBM per device.

```python
import math
import jax
import jax.numpy as jnp
import numpy as np
from jax import lax

DATE_DEV = 2
COLS = 1024
ROUNDS = 4
PATCH = 32
LOOK_A = 5
LOOK_R = 19
HALO = 2
DATES = 64
ROWS = 256
N_DATE = 32


def draw_slc(key, part):
    key_list = jax.random.split(key, 6)
    scene_field = jax.random.normal(key_list[0], (2, ROWS, COLS), jnp.float32)
    rotation = jax.random.uniform(key_list[1], (DATES, 1, 1), jnp.float32, -math.pi, math.pi)
    noise_level = jax.random.uniform(key_list[2], (DATES, 1, 1, 1), jnp.float32, 0.3, 1.2)
    cos_part = jnp.cos(rotation)
    sin_part = jnp.sin(rotation)
    real_part = scene_field[0][None] * cos_part - scene_field[1][None] * sin_part
    imag_part = scene_field[0][None] * sin_part + scene_field[1][None] * cos_part
    noise_field = jax.random.normal(key_list[5], (DATES, 2, ROWS, COLS), jnp.float32)
    return (jnp.stack([real_part, imag_part], 1) + noise_level * noise_field).astype(jnp.bfloat16)


def draw_valid(key, part):
    first_key, second_key = jax.random.split(key)
    start_rows = jax.random.randint(first_key, (ROUNDS, DATES), 0, ROWS // 2)
    end_rows = jax.random.randint(second_key, (ROUNDS, DATES), ROWS // 2 + 1, ROWS + 1)
    date_ids = lax.iota(jnp.int32, DATES)[None, :]
    start_rows = jnp.where(date_ids == 0, 0, start_rows)
    end_rows = jnp.where(date_ids == 0, ROWS, end_rows)
    return jnp.stack([start_rows, end_rows], -1).astype(jnp.int32)


def setup_inputs(seed: int = 0) -> dict:
    keys = jax.random.split(jax.random.key(seed), 4)
    return {
        "slc": draw_slc(jax.random.fold_in(keys[3], 71), 0),
        "partner": jax.vmap(lambda own: jax.random.permutation(own, DATE_DEV))(jax.random.split(keys[1], ROUNDS * N_DATE)).reshape((ROUNDS, N_DATE, DATE_DEV)).astype(jnp.int32),
        "valid": draw_valid(jax.random.fold_in(keys[3], 71), 0),
    }


def box_filter(fields):
    row_count = fields.shape[-2]
    col_count = fields.shape[-1]
    col_reach = LOOK_R // 2
    padded = jnp.pad(fields, ((0, 0), (HALO, HALO), (col_reach, col_reach)))
    row_total = padded[:, 0:row_count, :]
    for shift_row in range(1, LOOK_A):
        row_total = row_total + padded[:, shift_row:shift_row + row_count, :]
    col_total = row_total[:, :, 0:col_count]
    for shift_col in range(1, LOOK_R):
        col_total = col_total + row_total[:, :, shift_col:shift_col + col_count]
    return col_total * (1.0 / (LOOK_A * LOOK_R))

def goldstein_ref(ml_real, ml_imag):
    tiles = lax.complex(ml_real, ml_imag).reshape(ROWS // PATCH, PATCH, COLS // PATCH, PATCH)
    spectrum = jnp.fft.fft2(tiles, axes=(1, 3))
    magnitude = jnp.abs(spectrum)
    spread_cols = magnitude + jnp.roll(magnitude, 1, axis=3) + jnp.roll(magnitude, -1, axis=3)
    spread = (spread_cols + jnp.roll(spread_cols, 1, axis=1) + jnp.roll(spread_cols, -1, axis=1)) / 9.0
    tile_mean = lax.optimization_barrier(jnp.mean(spread, axis=(1, 3), keepdims=True))
    weight = jnp.sqrt(spread / (tile_mean + 1e-06))
    result = jnp.fft.ifft2(spectrum * weight, axes=(1, 3)).reshape(ROWS, COLS)
    return (jnp.real(result), jnp.imag(result))

def pair_outputs(primary, secondary, bounds):
    row_index = lax.iota(jnp.int32, ROWS)
    row_mask = ((row_index >= bounds[0]) & (row_index < bounds[1])).astype(jnp.float32)[:, None]
    a_real = primary[0]
    a_imag = primary[1]
    b_real = secondary[0]
    b_imag = secondary[1]
    fields = jnp.stack([(a_real * b_real + a_imag * b_imag) * row_mask, (a_imag * b_real - a_real * b_imag) * row_mask, (a_real * a_real + a_imag * a_imag) * row_mask, (b_real * b_real + b_imag * b_imag) * row_mask])
    boxed = box_filter(fields)
    coherence = row_mask * jnp.sqrt(boxed[0] * boxed[0] + boxed[1] * boxed[1]) / jnp.sqrt(boxed[2] * boxed[3] + 1e-06)
    filt_real, filt_imag = goldstein_ref(boxed[0], boxed[1])
    return (coherence, jnp.stack([filt_real * row_mask, filt_imag * row_mask]))

def reference(slc, partner, valid):
    stack_all = slc.astype(jnp.float32)
    block_ids = np.arange(N_DATE)
    date_ids = lax.iota(jnp.int32, DATES)
    coherence_rounds = []
    filtered_rounds = []
    for round_bit in range(ROUNDS):
        partner_block = jnp.asarray(block_ids ^ 1 << round_bit, dtype=jnp.int32)
        second_index = (partner_block[:, None] * DATE_DEV + partner[round_bit].astype(jnp.int32)).reshape(DATES).astype(jnp.int32)

        def one_pair(pair_item):
            own_index, other_index, bounds = pair_item
            primary = lax.dynamic_index_in_dim(stack_all, own_index, 0, keepdims=False)
            secondary = lax.dynamic_index_in_dim(stack_all, other_index, 0, keepdims=False)
            return pair_outputs(primary, secondary, bounds)
        coherence, filtered = lax.map(one_pair, (date_ids, second_index, valid[round_bit].astype(jnp.int32)))
        coherence_rounds.append(coherence)
        filtered_rounds.append(filtered)
    return (jnp.stack(coherence_rounds), jnp.stack(filtered_rounds))
```

```python
import functools
import math

import jax
import jax.numpy as jnp
import numpy as np
from jax import lax
from jax.experimental import pallas as pl
from jax.experimental.pallas import tpu as pltpu
from jax.sharding import PartitionSpec as P

F32 = jnp.float32
BF16 = jnp.bfloat16
MESH = pl.DeviceIdType.MESH

PATCH = 32
LOOK_A = 5
LOOK_R = 19
HALO = 2
LANES = 128
SUBS = 8
ROWS = 32
EXT = ROWS + 2 * HALO
EDGE = HALO * SUBS
BODY = ROWS * SUBS
FULL = EXT * SUBS
TINY = 1.2e-38

BOX_SCALE = 1.0 / 128.0
BOX_RATIO = LOOK_A * LOOK_R / 128.0


def split_np(table):
    high = table.astype(np.float32).astype(jnp.bfloat16)
    low = (table - high.astype(np.float64)).astype(np.float32).astype(jnp.bfloat16)
    return high, low


def make_tables():
    lane = np.arange(LANES)
    reach = LOOK_R // 2
    centre = np.abs(lane[:, None] - lane[None, :]) <= reach
    to_next = np.abs(lane[None, :] + LANES - lane[:, None]) <= reach
    to_previous = np.abs(lane[None, :] - LANES - lane[:, None]) <= reach
    box = np.concatenate([centre, to_next | to_previous], 1) * BOX_SCALE
    box = np.concatenate([box, box], 0)

    same = lane[:, None] // PATCH == lane[None, :] // PATCH
    angle = (lane[:, None] % PATCH) * (lane[None, :] % PATCH) % PATCH * (2 * math.pi / PATCH)
    cos = np.where(same, np.cos(angle), 0.0)
    sin = np.where(same, np.sin(angle), 0.0)
    forward = np.block([[cos, -sin], [sin, cos]]) / (BOX_RATIO * PATCH * PATCH)
    inverse = np.block([[cos, sin], [-sin, cos]])
    apart = (lane[:, None] - lane[None, :]) % PATCH
    near = same & ((apart <= 1) | (apart == PATCH - 1))

    def triple(table):
        high, low = split_np(table)
        return np.concatenate([high, high, low], 0)

    def twice(table):
        return np.concatenate([table, table], 0).astype(np.float32).astype(jnp.bfloat16)

    return (
        box.astype(np.float32).astype(jnp.bfloat16),
        triple(forward),
        triple(inverse),
        twice(near),
        twice(same),
    )


def cmul(value, angle):
    re, im = value
    c, s = math.cos(angle), math.sin(angle)
    quarter = round(angle / (math.pi / 4), 9)
    if quarter == int(quarter):
        turn = int(quarter) % 8
        h = math.sqrt(0.5)
        return [
            lambda: (re, im),
            lambda: ((re - im) * h, (re + im) * h),
            lambda: (-im, re),
            lambda: (-(re + im) * h, (re - im) * h),
            lambda: (-re, -im),
            lambda: ((im - re) * h, -(re + im) * h),
            lambda: (im, -re),
            lambda: ((re + im) * h, (im - re) * h),
        ][turn]()
    return re * c - im * s, re * s + im * c


def cadd(a, b):
    return a[0] + b[0], a[1] + b[1]


def csub(a, b):
    return a[0] - b[0], a[1] - b[1]


def add_turned(a, b, sign):
    if sign > 0:
        return a[0] - b[1], a[1] + b[0]
    return a[0] + b[1], a[1] - b[0]


def dft4(x, sign):
    s0, d0 = cadd(x[0], x[2]), csub(x[0], x[2])
    s1, d1 = cadd(x[1], x[3]), csub(x[1], x[3])
    return [cadd(s0, s1), add_turned(d0, d1, sign), csub(s0, s1), add_turned(d0, d1, -sign)]


def dft8(x, sign):
    even = dft4(x[0::2], sign)
    odd = dft4(x[1::2], sign)
    out = [None] * 8
    h = math.sqrt(0.5)
    for k in range(4):
        if k == 2:
            out[2] = add_turned(even[2], odd[2], sign)
            out[6] = add_turned(even[2], odd[2], -sign)
            continue
        turned = odd[k] if k == 0 else cmul(odd[k], sign * k * math.pi / 4)
        out[k] = cadd(even[k], turned)
        out[k + 4] = csub(even[k], turned)
    return out


def row(ref_value, r):
    return ref_value[r * SUBS : (r + 1) * SUBS]


def pair_up(a, b):
    return jnp.concatenate([a, b], 0)


def split(x):
    high = x.astype(BF16)
    low = (x - high.astype(F32)).astype(BF16)
    return high, low


def root(x):
    return x * lax.rsqrt(jnp.maximum(x, TINY))


def dot(a, b):
    return jnp.dot(a, b, preferred_element_type=F32)


def prepare_own(own_ref, own32_ref):
    for i in range(2):
        for q in range(EXT // 2):
            at = pl.ds(q * 16, 16)
            re = own_ref[i, 0, at, :].astype(F32)
            im = own_ref[i, 1, at, :].astype(F32)
            own32_ref[i, 0, at, :] = re
            own32_ref[i, 1, at, :] = im
            own32_ref[i, 2, at, :] = re * re + im * im


def compute_pair(
    first, start, end, own32, other, tables, put_coherence, put_filtered, box_in, ml, mid, spec_in, mags, mag_in
):
    box_t, forward_t, inverse_t, near_t, same_t = tables
    sub = lax.broadcasted_iota(jnp.int32, (SUBS, LANES), 0)
    lane = lax.broadcasted_iota(jnp.int32, (SUBS, LANES), 1)
    low_half = lane < LANES // 2
    inner = jnp.where(low_half, jnp.where(sub > 0, 1.0, 0.0), jnp.where(sub < SUBS - 1, 1.0, 0.0))
    masks = []
    for r in range(EXT):
        here = first + (r - HALO)
        masks.append(jnp.where((here >= start) & (here < end), 1.0, 0.0).astype(F32))

    kept = [[], [], [], []]

    def add_products(q):
        at = pl.ds(q * 16, 16)
        c_re2 = other(0, at).astype(F32)
        c_im2 = other(1, at).astype(F32)
        for half in range(2):
            r = 2 * q + half
            m = masks[r]
            one = pl.ds(r * SUBS, SUBS)
            a_re = own32(0, one) * m
            a_im = own32(1, one) * m
            c_re, c_im = row(c_re2, half), row(c_im2, half)
            kept[0].append(a_re * c_re + a_im * c_im)
            kept[1].append(a_im * c_re - a_re * c_im)
            kept[2].append(own32(2, one) * m)
            kept[3].append((c_re * c_re + c_im * c_im) * m)

    add_products(0)
    add_products(1)
    two = [[kept[f][n] + kept[f][n + 1] for n in range(3)] for f in range(4)]
    for g in range(ROWS // SUBS):
        for q in range(4):
            add_products(2 + g * 4 + q)
            for f in range(4):
                sums = []
                for half in range(2):
                    r = g * 8 + q * 2 + half
                    two[f].append(kept[f][r + 3] + kept[f][r + 4])
                    sums.append(kept[f][r] + (two[f][r + 1] + two[f][r + 3]))
                high, low = split(pair_up(*sums))
                at = pl.ds(f * 64 + q * 16, 16)
                box_in[g % 2, at, 0:LANES] = high
                box_in[g % 2, at, LANES : 2 * LANES] = low
        y = dot(box_in[g % 2], box_t[...])
        for n in range(8):
            r = g * 8 + n
            ml_f = []
            for f in range(4):
                base = (f * 8 + n) * SUBS
                own_part = y[base : base + SUBS, 0:LANES]
                side = y[base : base + SUBS, LANES : 2 * LANES]
                side = jnp.where(low_half, pltpu.roll(side, 1, 0), pltpu.roll(side, SUBS - 1, 0))
                ml_f.append(own_part + side * inner)
            re, im, p1, p2 = ml_f
            ml[0, pl.ds(r * SUBS, SUBS), :] = re
            ml[1, pl.ds(r * SUBS, SUBS), :] = im
            size = root(re * re + im * im)
            down = lax.rsqrt(p1 * p2 + 1e-6 * BOX_RATIO * BOX_RATIO)
            put_coherence(r, size * (down * masks[r + HALO]))

    for b in range(8):
        x = [
            (ml[0, pl.ds((b + 8 * a) * SUBS, SUBS), :], ml[1, pl.ds((b + 8 * a) * SUBS, SUBS), :])
            for a in range(4)
        ]
        x = dft4(x, -1)
        for k1 in range(4):
            v = cmul(x[k1], -2 * math.pi * b * k1 / 32)
            mid[0, pl.ds((k1 * 8 + b) * SUBS, SUBS), :] = v[0]
            mid[1, pl.ds((k1 * 8 + b) * SUBS, SUBS), :] = v[1]

    def put_split(place, parts):
        for c in range(2):
            high, low = split(pair_up(parts[0][c], parts[1][c]))
            at = pl.ds(place * SUBS, 16)
            spec_in[at, c * LANES : (c + 1) * LANES] = high
            spec_in[at, (2 + c) * LANES : (3 + c) * LANES] = low

    for k1 in range(4):
        x = [
            (mid[0, pl.ds((k1 * 8 + b) * SUBS, SUBS), :], mid[1, pl.ds((k1 * 8 + b) * SUBS, SUBS), :])
            for b in range(8)
        ]
        x = dft8(x, -1)
        for k2 in range(0, 8, 2):
            put_split(k1 * 8 + k2, x[k2 : k2 + 2])

    both = spec_in[...]
    s = dot(jnp.concatenate([both, both[:, 0 : 2 * LANES]], 1), forward_t[...])
    for p in range(ROWS):
        at = pl.ds(p * SUBS, SUBS)
        re, im = row(s, p)[:, 0:LANES], row(s, p)[:, LANES:]
        mid[0, at, :] = re
        mid[1, at, :] = im
        mags[at, :] = root(re * re + im * im)

    def place(k):
        k = k % PATCH
        return (k % 4) * 8 + k // 4

    total = None
    for p in range(0, ROWS, 2):
        sums = []
        for k in (p // 8 + 4 * (p % 8), p // 8 + 4 * (p % 8 + 1)):
            sums.append(
                mags[pl.ds(place(k - 1) * SUBS, SUBS), :]
                + mags[pl.ds(place(k) * SUBS, SUBS), :]
                + mags[pl.ds(place(k + 1) * SUBS, SUBS), :]
            )
            total = sums[-1] if total is None else total + sums[-1]
        high, low = split(pair_up(*sums))
        mag_in[pl.ds(p * SUBS, 16), 0:LANES] = high
        mag_in[pl.ds(p * SUBS, 16), LANES:] = low
    high, low = split(pair_up(total, total))
    tile_sum = dot(jnp.concatenate([high, low], 1), same_t[...])[0:SUBS]
    inv = (1.0 / 9.0) / (tile_sum * (1.0 / (3 * PATCH * PATCH)) + 1e-6 / (PATCH * PATCH))
    smooth = dot(mag_in[...], near_t[...])
    for p in range(0, ROWS, 2):
        parts = []
        for n in (p, p + 1):
            w = root(row(smooth, n) * inv)
            at = pl.ds(n * SUBS, SUBS)
            parts.append((mid[0, at, :] * w, mid[1, at, :] * w))
        put_split(p, parts)

    both = spec_in[...]
    s = dot(jnp.concatenate([both, both[:, 0 : 2 * LANES]], 1), inverse_t[...])
    for k1 in range(4):
        x = [
            (row(s, k1 * 8 + k2)[:, 0:LANES], row(s, k1 * 8 + k2)[:, LANES:])
            for k2 in range(8)
        ]
        x = dft8(x, 1)
        for b in range(8):
            v = cmul(x[b], 2 * math.pi * b * k1 / 32)
            at = pl.ds((k1 * 8 + b) * SUBS, SUBS)
            mid[0, at, :] = v[0]
            mid[1, at, :] = v[1]
    for b in range(8):
        x = [
            (mid[0, pl.ds((k1 * 8 + b) * SUBS, SUBS), :], mid[1, pl.ds((k1 * 8 + b) * SUBS, SUBS), :])
            for k1 in range(4)
        ]
        x = dft4(x, 1)
        for a in range(4):
            r = b + 8 * a
            put_filtered(0, r, x[a][0] * masks[r + HALO])
            put_filtered(1, r, x[a][1] * masks[r + HALO])


def compute_kernel(
    partner, valid, own, other, box_t, forward_t, inverse_t, near_t, same_t, coherence, filtered,
    own32, box_in, ml, mid, spec_in, mags, mag_in,
):
    rnd = pl.program_id(0)
    first = lax.axis_index("strip") * ROWS
    tables = (box_t, forward_t, inverse_t, near_t, same_t)

    @pl.when(rnd == 0)
    def _():
        prepare_own(own, own32)

    for i in range(2):
        which = partner[rnd, 0, i]

        def put_coherence(r, value, i=i):
            coherence[0, i, r // 8, pl.ds(r % 8, SUBS, stride=8), :] = value

        def put_filtered(c, r, value, i=i):
            filtered[0, i, c, r // 8, pl.ds(r % 8, SUBS, stride=8), :] = value

        compute_pair(
            first,
            valid[rnd, i, 0],
            valid[rnd, i, 1],
            lambda c, at, i=i: own32[i, c, at, :],
            lambda c, at, which=which: other[rnd, which, c, at, :],
            tables,
            put_coherence,
            put_filtered,
            box_in.at[i],
            ml.at[i],
            mid.at[i],
            spec_in.at[i],
            mags.at[i],
            mag_in.at[i],
        )


def compute(partner, valid, own, other):
    tables = [jnp.asarray(t) for t in make_tables()]
    vmem = pl.BlockSpec(memory_space=pltpu.VMEM)
    smem = pl.BlockSpec(memory_space=pltpu.SMEM)
    rounds = other.shape[0]
    return pl.pallas_call(
        compute_kernel,
        grid=(rounds,),
        out_shape=(
            jax.ShapeDtypeStruct((rounds, 2, 4, 64, LANES), F32),
            jax.ShapeDtypeStruct((rounds, 2, 2, 4, 64, LANES), F32),
        ),
        in_specs=[smem, smem] + [vmem] * 7,
        out_specs=(
            pl.BlockSpec((1, 2, 4, 64, LANES), lambda r: (r, 0, 0, 0, 0)),
            pl.BlockSpec((1, 2, 2, 4, 64, LANES), lambda r: (r, 0, 0, 0, 0, 0)),
        ),
        scratch_shapes=[
            pltpu.VMEM((2, 3, FULL, LANES), F32),
            pltpu.VMEM((2, 2, 256, 2 * LANES), BF16),
            pltpu.VMEM((2, 2, BODY, LANES), F32),
            pltpu.VMEM((2, 2, BODY, LANES), F32),
            pltpu.VMEM((2, BODY, 4 * LANES), BF16),
            pltpu.VMEM((2, BODY, LANES), F32),
            pltpu.VMEM((2, BODY, 2 * LANES), BF16),
        ],
        compiler_params=pltpu.CompilerParams(vmem_limit_bytes=48 * 1024 * 1024),
    )(partner, valid, own, other, *tables)


def exchange_kernel(slc, own, other, lines, halo_send, halo_recv, main_send, main_recv, edge_send, edge_recv, fwd_send, fwd_recv, fwde_send, fwde_recv):
    date = lax.axis_index("date")
    strip = lax.axis_index("strip")
    n_strip = lax.axis_size("strip")
    above = (date, lax.rem(strip + n_strip - 1, n_strip))
    below = (date, lax.rem(strip + 1, n_strip))

    def xor(bits):
        target = date
        for bit in range(4):
            if bits >> bit & 1:
                size = 1 << bit
                target = target + size - 2 * size * lax.rem(lax.div(date, size), 2)
        return (target, strip)

    partners = {0: xor(1), 1: xor(2), 3: xor(8)}
    onward = xor(6)

    barrier = pltpu.get_barrier_semaphore()
    greeted = [above, below, partners[0], partners[1], partners[3], onward]
    for device in greeted:
        pl.semaphore_signal(barrier, inc=1, device_id=device, device_id_type=MESH)

    for i in range(2):
        for c in range(2):
            for g in range(4):
                for j in range(8):
                    lines[i * 2 + c, g, pl.ds(j * 8, 8), :] = slc[
                        i, c, pl.ds(g * 8, 8), pl.ds(j * LANES, LANES)
                    ].astype(F32)
            for g in range(4):
                for s in range(0, 8, 2):
                    pair = jnp.concatenate(
                        [
                            lines[i * 2 + c, g, pl.ds(s, 8, stride=8), :],
                            lines[i * 2 + c, g, pl.ds(s + 1, 8, stride=8), :],
                        ],
                        0,
                    )
                    own[i, c, pl.ds(EDGE + (g * 8 + s) * SUBS, 16), :] = pair.astype(BF16)

    pl.semaphore_wait(barrier, len(greeted))

    top, bottom = pl.ds(0, EDGE), pl.ds(FULL - EDGE, EDGE)
    first_rows, last_rows = pl.ds(EDGE, EDGE), pl.ds(FULL - 2 * EDGE, EDGE)
    body = pl.ds(EDGE, BODY)

    def send(src, dst, send_sem, recv_sem, device):
        copy = pltpu.make_async_remote_copy(
            src_ref=src, dst_ref=dst, send_sem=send_sem, recv_sem=recv_sem, device_id=device, device_id_type=MESH
        )
        copy.start()
        return copy

    to_above = send(own.at[:, :, first_rows], own.at[:, :, bottom], halo_send.at[0], halo_recv.at[0], above)
    to_below = send(own.at[:, :, last_rows], own.at[:, :, top], halo_send.at[1], halo_recv.at[1], below)

    mains = {}
    for i in range(2):
        for c in range(2):
            for n, r in enumerate((1, 3, 0)):
                mains[r, i, c] = send(
                    own.at[i, c, body],
                    other.at[r, i, c, body],
                    main_send.at[n, i, c],
                    main_recv.at[n, i, c],
                    partners[r],
                )
    to_above.wait_recv()
    to_below.wait_recv()
    edges = {}
    for n, r in enumerate((1, 3, 0)):
        for side, at in enumerate((top, bottom)):
            edges[r, side] = send(
                own.at[:, :, at], other.at[r, :, :, at], edge_send.at[n, side], edge_recv.at[n, side], partners[r]
            )
    forwards = []
    for i in range(2):
        for c in range(2):
            mains[1, i, c].wait_recv()
            forwards.append(
                send(
                    other.at[1, i, c, body], other.at[2, i, c, body], fwd_send.at[i, c], fwd_recv.at[i, c], onward
                )
            )
    for side, at in enumerate((top, bottom)):
        edges[1, side].wait_recv()
        forwards.append(
            send(other.at[1, :, :, at], other.at[2, :, :, at], fwde_send.at[side], fwde_recv.at[side], onward)
        )
    to_above.wait_send()
    to_below.wait_send()
    for (r, _, _), copy in mains.items():
        copy.wait_send()
        if r != 1:
            copy.wait_recv()
    for (r, _), copy in edges.items():
        copy.wait_send()
        if r != 1:
            copy.wait_recv()
    for copy in forwards:
        copy.wait()


def exchange(slc):
    vmem = pl.BlockSpec(memory_space=pltpu.VMEM)
    dma = pltpu.SemaphoreType.DMA
    return pl.pallas_call(
        exchange_kernel,
        out_shape=(
            jax.ShapeDtypeStruct((2, 2, FULL, LANES), BF16),
            jax.ShapeDtypeStruct((4, 2, 2, FULL, LANES), BF16),
        ),
        in_specs=[vmem],
        out_specs=(vmem, vmem),
        scratch_shapes=[
            pltpu.VMEM((4, 4, 64, LANES), F32),
            dma((2,)),
            dma((2,)),
            dma((3, 2, 2)),
            dma((3, 2, 2)),
            dma((3, 2)),
            dma((3, 2)),
            dma((2, 2)),
            dma((2, 2)),
            dma((2,)),
            dma((2,)),
        ],
        compiler_params=pltpu.CompilerParams(
            collective_id=0, has_side_effects=True, vmem_limit_bytes=32 * 1024 * 1024
        ),
    )(slc)


def untile(array):
    lead = array.shape[:-3]
    array = array.reshape(lead + (4, 8, 8, LANES))
    n = len(lead)
    array = array.transpose(tuple(range(n)) + (n, n + 2, n + 1, n + 3))
    return array.reshape(lead + (ROWS, 8 * LANES))


def shards(slc, partner, valid):
    own, other = exchange(slc)
    coherence, filtered = compute(partner, valid, own, other)
    return untile(coherence), untile(filtered)


def solution(mesh):
    in_specs = (P("date", None, "strip", None), P(None, "date", None), P(None, "date", None))
    out_specs = (P(None, "date", "strip", None), P(None, "date", None, "strip", None))
    return jax.shard_map(shards, mesh=mesh, in_specs=in_specs, out_specs=out_specs, check_vma=False)
```

```python
import functools
import math

import jax
import jax.numpy as jnp
import numpy as np
from jax import lax
from jax.experimental import pallas as pl
from jax.experimental.pallas import tpu as pltpu
from jax.sharding import PartitionSpec as P

F32 = jnp.float32
BF16 = jnp.bfloat16
MESH = pl.DeviceIdType.MESH

PATCH = 32
LOOK_A = 5
LOOK_R = 19
HALO = 2
LANES = 128
SUBS = 8
ROWS = 32
EXT = ROWS + 2 * HALO
EDGE = HALO * SUBS
BODY = ROWS * SUBS
FULL = EXT * SUBS
TINY = 1.2e-38

BOX_SCALE = 1.0 / 128.0
BOX_RATIO = LOOK_A * LOOK_R / 128.0


def split_np(table):
    high = table.astype(np.float32).astype(jnp.bfloat16)
    low = (table - high.astype(np.float64)).astype(np.float32).astype(jnp.bfloat16)
    return high, low


def make_tables():
    lane = np.arange(LANES)
    reach = LOOK_R // 2
    centre = np.abs(lane[:, None] - lane[None, :]) <= reach
    to_next = np.abs(lane[None, :] + LANES - lane[:, None]) <= reach
    to_previous = np.abs(lane[None, :] - LANES - lane[:, None]) <= reach
    box = np.concatenate([centre, to_next | to_previous], 1) * BOX_SCALE
    box = np.concatenate([box, box], 0)

    same = lane[:, None] // PATCH == lane[None, :] // PATCH
    angle = (lane[:, None] % PATCH) * (lane[None, :] % PATCH) % PATCH * (2 * math.pi / PATCH)
    cos = np.where(same, np.cos(angle), 0.0)
    sin = np.where(same, np.sin(angle), 0.0)
    forward = np.block([[cos, -sin], [sin, cos]]) / (BOX_RATIO * PATCH * PATCH)
    inverse = np.block([[cos, sin], [-sin, cos]])
    apart = (lane[:, None] - lane[None, :]) % PATCH
    near = same & ((apart <= 1) | (apart == PATCH - 1))

    def triple(table):
        high, low = split_np(table)
        return np.concatenate([high, high, low], 0)

    def twice(table):
        return np.concatenate([table, table], 0).astype(np.float32).astype(jnp.bfloat16)

    return (
        box.astype(np.float32).astype(jnp.bfloat16),
        triple(forward),
        triple(inverse),
        twice(near),
        twice(same),
    )


def cmul(value, angle):
    re, im = value
    c, s = math.cos(angle), math.sin(angle)
    quarter = round(angle / (math.pi / 4), 9)
    if quarter == int(quarter):
        turn = int(quarter) % 8
        h = math.sqrt(0.5)
        return [
            lambda: (re, im),
            lambda: ((re - im) * h, (re + im) * h),
            lambda: (-im, re),
            lambda: (-(re + im) * h, (re - im) * h),
            lambda: (-re, -im),
            lambda: ((im - re) * h, -(re + im) * h),
            lambda: (im, -re),
            lambda: ((re + im) * h, (im - re) * h),
        ][turn]()
    return re * c - im * s, re * s + im * c


def cadd(a, b):
    return a[0] + b[0], a[1] + b[1]


def csub(a, b):
    return a[0] - b[0], a[1] - b[1]


def add_turned(a, b, sign):
    if sign > 0:
        return a[0] - b[1], a[1] + b[0]
    return a[0] + b[1], a[1] - b[0]


def dft4(x, sign):
    s0, d0 = cadd(x[0], x[2]), csub(x[0], x[2])
    s1, d1 = cadd(x[1], x[3]), csub(x[1], x[3])
    return [cadd(s0, s1), add_turned(d0, d1, sign), csub(s0, s1), add_turned(d0, d1, -sign)]


def dft8(x, sign):
    even = dft4(x[0::2], sign)
    odd = dft4(x[1::2], sign)
    out = [None] * 8
    h = math.sqrt(0.5)
    for k in range(4):
        if k == 2:
            out[2] = add_turned(even[2], odd[2], sign)
            out[6] = add_turned(even[2], odd[2], -sign)
            continue
        turned = odd[k] if k == 0 else cmul(odd[k], sign * k * math.pi / 4)
        out[k] = cadd(even[k], turned)
        out[k + 4] = csub(even[k], turned)
    return out


def row(ref_value, r):
    return ref_value[r * SUBS : (r + 1) * SUBS]


def pair_up(a, b):
    return jnp.concatenate([a, b], 0)


def split(x):
    high = x.astype(BF16)
    low = (x - high.astype(F32)).astype(BF16)
    return high, low


def root(x):
    return x * lax.rsqrt(jnp.maximum(x, TINY))


def dot(a, b):
    return jnp.dot(a, b, preferred_element_type=F32)


def compute_pair(
    first, start, end, own32, other, tables, put_coherence, put_filtered, box_in, ml, mid, spec_in, mags, mag_in
):
    box_t, forward_t, inverse_t, near_t, same_t = tables
    sub = lax.broadcasted_iota(jnp.int32, (SUBS, LANES), 0)
    lane = lax.broadcasted_iota(jnp.int32, (SUBS, LANES), 1)
    low_half = lane < LANES // 2
    inner = jnp.where(low_half, jnp.where(sub > 0, 1.0, 0.0), jnp.where(sub < SUBS - 1, 1.0, 0.0))
    masks = []
    for r in range(EXT):
        here = first + (r - HALO)
        masks.append(jnp.where((here >= start) & (here < end), 1.0, 0.0).astype(F32))

    kept = [[], [], [], []]

    def add_products(q):
        at = pl.ds(q * 16, 16)
        c_re2 = other(0, at).astype(F32)
        c_im2 = other(1, at).astype(F32)
        for half in range(2):
            r = 2 * q + half
            m = masks[r]
            one = pl.ds(r * SUBS, SUBS)
            a_re = own32(0, one) * m
            a_im = own32(1, one) * m
            c_re, c_im = row(c_re2, half), row(c_im2, half)
            kept[0].append(a_re * c_re + a_im * c_im)
            kept[1].append(a_im * c_re - a_re * c_im)
            kept[2].append(own32(2, one) * m)
            kept[3].append((c_re * c_re + c_im * c_im) * m)

    add_products(0)
    add_products(1)
    two = [[kept[f][n] + kept[f][n + 1] for n in range(3)] for f in range(4)]
    for g in range(ROWS // SUBS):
        for q in range(4):
            add_products(2 + g * 4 + q)
            for f in range(4):
                sums = []
                for half in range(2):
                    r = g * 8 + q * 2 + half
                    two[f].append(kept[f][r + 3] + kept[f][r + 4])
                    sums.append(kept[f][r] + (two[f][r + 1] + two[f][r + 3]))
                high, low = split(pair_up(*sums))
                at = pl.ds(f * 64 + q * 16, 16)
                box_in[g % 2, at, 0:LANES] = high
                box_in[g % 2, at, LANES : 2 * LANES] = low
        y = dot(box_in[g % 2], box_t[...])
        for n in range(8):
            r = g * 8 + n
            ml_f = []
            for f in range(4):
                base = (f * 8 + n) * SUBS
                own_part = y[base : base + SUBS, 0:LANES]
                side = y[base : base + SUBS, LANES : 2 * LANES]
                side = jnp.where(low_half, pltpu.roll(side, 1, 0), pltpu.roll(side, SUBS - 1, 0))
                ml_f.append(own_part + side * inner)
            re, im, p1, p2 = ml_f
            ml[0, pl.ds(r * SUBS, SUBS), :] = re
            ml[1, pl.ds(r * SUBS, SUBS), :] = im
            size = root(re * re + im * im)
            down = lax.rsqrt(p1 * p2 + 1e-6 * BOX_RATIO * BOX_RATIO)
            put_coherence(r, size * (down * masks[r + HALO]))

    for b in range(8):
        x = [
            (ml[0, pl.ds((b + 8 * a) * SUBS, SUBS), :], ml[1, pl.ds((b + 8 * a) * SUBS, SUBS), :])
            for a in range(4)
        ]
        x = dft4(x, -1)
        for k1 in range(4):
            v = cmul(x[k1], -2 * math.pi * b * k1 / 32)
            mid[0, pl.ds((k1 * 8 + b) * SUBS, SUBS), :] = v[0]
            mid[1, pl.ds((k1 * 8 + b) * SUBS, SUBS), :] = v[1]

    def put_split(place, parts):
        for c in range(2):
            high, low = split(pair_up(parts[0][c], parts[1][c]))
            at = pl.ds(place * SUBS, 16)
            spec_in[at, c * LANES : (c + 1) * LANES] = high
            spec_in[at, (2 + c) * LANES : (3 + c) * LANES] = low

    for k1 in range(4):
        x = [
            (mid[0, pl.ds((k1 * 8 + b) * SUBS, SUBS), :], mid[1, pl.ds((k1 * 8 + b) * SUBS, SUBS), :])
            for b in range(8)
        ]
        x = dft8(x, -1)
        for k2 in range(0, 8, 2):
            put_split(k1 * 8 + k2, x[k2 : k2 + 2])

    both = spec_in[...]
    s = dot(jnp.concatenate([both, both[:, 0 : 2 * LANES]], 1), forward_t[...])
    for p in range(ROWS):
        at = pl.ds(p * SUBS, SUBS)
        re, im = row(s, p)[:, 0:LANES], row(s, p)[:, LANES:]
        mid[0, at, :] = re
        mid[1, at, :] = im
        mags[at, :] = root(re * re + im * im)

    def place(k):
        k = k % PATCH
        return (k % 4) * 8 + k // 4

    total = None
    for p in range(0, ROWS, 2):
        sums = []
        for k in (p // 8 + 4 * (p % 8), p // 8 + 4 * (p % 8 + 1)):
            sums.append(
                mags[pl.ds(place(k - 1) * SUBS, SUBS), :]
                + mags[pl.ds(place(k) * SUBS, SUBS), :]
                + mags[pl.ds(place(k + 1) * SUBS, SUBS), :]
            )
            total = sums[-1] if total is None else total + sums[-1]
        high, low = split(pair_up(*sums))
        mag_in[pl.ds(p * SUBS, 16), 0:LANES] = high
        mag_in[pl.ds(p * SUBS, 16), LANES:] = low
    high, low = split(pair_up(total, total))
    tile_sum = dot(jnp.concatenate([high, low], 1), same_t[...])[0:SUBS]
    inv = (1.0 / 9.0) / (tile_sum * (1.0 / (3 * PATCH * PATCH)) + 1e-6 / (PATCH * PATCH))
    smooth = dot(mag_in[...], near_t[...])
    for p in range(0, ROWS, 2):
        parts = []
        for n in (p, p + 1):
            w = root(row(smooth, n) * inv)
            at = pl.ds(n * SUBS, SUBS)
            parts.append((mid[0, at, :] * w, mid[1, at, :] * w))
        put_split(p, parts)

    both = spec_in[...]
    s = dot(jnp.concatenate([both, both[:, 0 : 2 * LANES]], 1), inverse_t[...])
    for k1 in range(4):
        x = [
            (row(s, k1 * 8 + k2)[:, 0:LANES], row(s, k1 * 8 + k2)[:, LANES:])
            for k2 in range(8)
        ]
        x = dft8(x, 1)
        for b in range(8):
            v = cmul(x[b], 2 * math.pi * b * k1 / 32)
            at = pl.ds((k1 * 8 + b) * SUBS, SUBS)
            mid[0, at, :] = v[0]
            mid[1, at, :] = v[1]
    for b in range(8):
        x = [
            (mid[0, pl.ds((k1 * 8 + b) * SUBS, SUBS), :], mid[1, pl.ds((k1 * 8 + b) * SUBS, SUBS), :])
            for k1 in range(4)
        ]
        x = dft4(x, 1)
        for a in range(4):
            r = b + 8 * a
            put_filtered(0, r, x[a][0] * masks[r + HALO])
            put_filtered(1, r, x[a][1] * masks[r + HALO])


def compute_round(rnd, first, partner, valid, own32, other, tables, coherence, filtered, scratch):
    for i in range(2):
        which = partner[0, i, rnd]

        def put_coherence(r, value, i=i):
            coherence[i, r // 8, pl.ds(r % 8, SUBS, stride=8), :] = value

        def put_filtered(c, r, value, i=i):
            filtered[i, c, r // 8, pl.ds(r % 8, SUBS, stride=8), :] = value

        compute_pair(
            first,
            valid[i, 0, rnd],
            valid[i, 1, rnd],
            lambda c, at, i=i: own32[i, c, at, :],
            lambda c, at, which=which: jnp.where(which == 0, other[rnd, 0, c, at, :], other[rnd, 1, c, at, :]),
            tables,
            put_coherence,
            put_filtered,
            *[ref.at[i] for ref in scratch],
        )


def work_shapes():
    return [
        pltpu.VMEM((2, 2, 256, 2 * LANES), BF16),
        pltpu.VMEM((2, 2, BODY, LANES), F32),
        pltpu.VMEM((2, 2, BODY, LANES), F32),
        pltpu.VMEM((2, BODY, 4 * LANES), BF16),
        pltpu.VMEM((2, BODY, LANES), F32),
        pltpu.VMEM((2, BODY, 2 * LANES), BF16),
    ]


def exchange_kernel(
    partner_hbm, valid_hbm, slc_hbm, box_h, forward_h, inverse_h, near_h, same_h,
    coherence_hbm, filtered_hbm,
    own32, other, coherence, filtered, box_t, forward_t, inverse_t, near_t, same_t,
    slc, own, lines, partner, valid, load_sem, out_sem,
    halo_send, halo_recv, main_send, main_recv, edge_send, edge_recv, fwd_send, fwd_recv, *work,
):
    date = lax.axis_index("date")
    strip = lax.axis_index("strip")
    n_strip = lax.axis_size("strip")

    def xor(bits):
        target = date
        for bit in range(4):
            if bits >> bit & 1:
                size = 1 << bit
                target = target + size - 2 * size * lax.rem(lax.div(date, size), 2)
        return target

    mate, onward = xor(1), xor(6)
    partners = {0: mate, 1: xor(2), 2: xor(4), 3: xor(8)}
    has_above, has_below = strip > 0, strip < n_strip - 1

    loads = []
    for n, (src, dst) in enumerate(
        [
            (slc_hbm, slc),
            (partner_hbm, partner),
            (valid_hbm, valid),
            (box_h, box_t),
            (forward_h, forward_t),
            (near_h, near_t),
            (same_h, same_t),
            (inverse_h, inverse_t),
        ]
    ):
        loads.append(pltpu.make_async_copy(src, dst, load_sem.at[n]))
        loads[-1].start()

    barrier = pltpu.get_barrier_semaphore()

    def greet(device):
        pl.semaphore_signal(barrier, inc=1, device_id=device, device_id_type=MESH)

    @pl.when(has_above)
    def _():
        greet((date, strip - 1))
        greet((mate, strip - 1))

    @pl.when(has_below)
    def _():
        greet((date, strip + 1))
        greet((mate, strip + 1))

    for device in (*partners.values(), onward):
        greet((device, strip))

    loads[0].wait()
    for i in range(2):
        for c in range(2):
            for g in range(4):
                for j in range(8):
                    lines[i * 2 + c, g, pl.ds(j * 8, 8), :] = slc[
                        i, c, pl.ds(g * 8, 8), pl.ds(j * LANES, LANES)
                    ].astype(F32)
            for g in range(4):
                for s in range(0, 8, 2):
                    pair = jnp.concatenate(
                        [
                            lines[i * 2 + c, g, pl.ds(s, 8, stride=8), :],
                            lines[i * 2 + c, g, pl.ds(s + 1, 8, stride=8), :],
                        ],
                        0,
                    )
                    own[i, c, pl.ds(EDGE + (g * 8 + s) * SUBS, 16), :] = pair.astype(BF16)

    top, bottom = pl.ds(0, EDGE), pl.ds(FULL - EDGE, EDGE)
    first_rows, last_rows = pl.ds(EDGE, EDGE), pl.ds(FULL - 2 * EDGE, EDGE)
    body = pl.ds(EDGE, BODY)
    blank = jnp.zeros((EDGE, LANES), BF16)

    @pl.when(jnp.logical_not(has_above))
    def _():
        for i in range(2):
            for c in range(2):
                own[i, c, top, :] = blank
                other[0, i, c, top, :] = blank

    @pl.when(jnp.logical_not(has_below))
    def _():
        for i in range(2):
            for c in range(2):
                own[i, c, bottom, :] = blank
                other[0, i, c, bottom, :] = blank

    def remote(src, dst, send_sem, recv_sem, device):
        return pltpu.make_async_remote_copy(
            src_ref=src, dst_ref=dst, send_sem=send_sem, recv_sem=recv_sem, device_id=device, device_id_type=MESH
        )

    up = [
        remote(own.at[:, :, first_rows], own.at[:, :, bottom], halo_send.at[0], halo_recv.at[0], (date, strip - 1)),
        remote(
            own.at[:, :, first_rows], other.at[0, :, :, bottom], halo_send.at[2], halo_recv.at[2], (mate, strip - 1)
        ),
    ]
    down = [
        remote(own.at[:, :, last_rows], own.at[:, :, top], halo_send.at[1], halo_recv.at[1], (date, strip + 1)),
        remote(own.at[:, :, last_rows], other.at[0, :, :, top], halo_send.at[3], halo_recv.at[3], (mate, strip + 1)),
    ]
    inside = has_above & has_below

    @pl.when(inside)
    def _():
        pl.semaphore_wait(barrier, 9)

    @pl.when(jnp.logical_not(inside))
    def _():
        pl.semaphore_wait(barrier, 7)

    @pl.when(has_above)
    def _():
        for copy in up:
            copy.start()

    @pl.when(has_below)
    def _():
        for copy in down:
            copy.start()

    mains = {}
    for i in range(2):
        for c in range(2):
            for n, r in enumerate((1, 3, 0)):
                mains[r, i, c] = remote(
                    own.at[i, c, body],
                    other.at[r, i, c, body],
                    main_send.at[n, i, c],
                    main_recv.at[n, i, c],
                    (partners[r], strip),
                )
                mains[r, i, c].start()

    def widen(i, q):
        at = pl.ds(q * 16, 16)
        re = own[i, 0, at, :].astype(F32)
        im = own[i, 1, at, :].astype(F32)
        own32[i, 0, at, :] = re
        own32[i, 1, at, :] = im
        own32[i, 2, at, :] = re * re + im * im

    for i in range(2):
        for q in range(1, EXT // 2 - 1):
            widen(i, q)

    @pl.when(has_below)
    def _():
        up[0].wait_recv()

    @pl.when(has_above)
    def _():
        down[0].wait_recv()

    edges = {}
    for n, r in enumerate((1, 2, 3)):
        for side, at in enumerate((top, bottom)):
            edges[r, side] = remote(
                own.at[:, :, at],
                other.at[r, :, :, at],
                edge_send.at[n, side],
                edge_recv.at[n, side],
                (partners[r], strip),
            )
            edges[r, side].start()
    for i in range(2):
        for q in (0, EXT // 2 - 1):
            widen(i, q)

    forwards = []
    for i in range(2):
        for c in range(2):
            mains[1, i, c].wait_recv()
            forwards.append(
                remote(
                    other.at[1, i, c, body],
                    other.at[2, i, c, body],
                    fwd_send.at[i, c],
                    fwd_recv.at[i, c],
                    (onward, strip),
                )
            )
            forwards[-1].start()
    for i in range(2):
        for c in range(2):
            mains[0, i, c].wait_recv()

    @pl.when(has_below)
    def _():
        up[1].wait_recv()

    @pl.when(has_above)
    def _():
        down[1].wait_recv()

    for copy in loads[1:]:
        copy.wait()
    tables = (box_t, forward_t, inverse_t, near_t, same_t)

    def outputs(rnd):
        return [
            pltpu.make_async_copy(coherence.at[rnd], coherence_hbm.at[rnd], out_sem.at[rnd, 0]),
            pltpu.make_async_copy(filtered.at[rnd], filtered_hbm.at[rnd], out_sem.at[rnd, 1]),
        ]

    def one_round(rnd, carry):
        @pl.when(rnd == 1)
        def _():
            edges[1, 0].wait_recv()
            edges[1, 1].wait_recv()

        @pl.when(rnd == 2)
        def _():
            for copy in forwards:
                copy.wait_recv()
            edges[2, 0].wait_recv()
            edges[2, 1].wait_recv()

        @pl.when(rnd == 3)
        def _():
            for i in range(2):
                for c in range(2):
                    mains[3, i, c].wait_recv()
            edges[3, 0].wait_recv()
            edges[3, 1].wait_recv()

        compute_round(
            rnd, strip * ROWS, partner, valid, own32, other, tables, coherence.at[rnd], filtered.at[rnd], work
        )
        for copy in outputs(rnd):
            copy.start()
        return carry

    lax.fori_loop(0, 4, one_round, 0)

    @pl.when(has_above)
    def _():
        for copy in up:
            copy.wait_send()

    @pl.when(has_below)
    def _():
        for copy in down:
            copy.wait_send()

    for copy in (*mains.values(), *edges.values(), *forwards):
        copy.wait_send()
    for rnd in range(4):
        for copy in outputs(rnd):
            copy.wait()


def exchange(partner, valid, slc):
    tables = [jnp.asarray(t) for t in make_tables()]
    hbm = pl.BlockSpec(memory_space=pltpu.HBM)
    dma = pltpu.SemaphoreType.DMA
    return pl.pallas_call(
        exchange_kernel,
        out_shape=(
            jax.ShapeDtypeStruct((4, 2, 4, 64, LANES), F32),
            jax.ShapeDtypeStruct((4, 2, 2, 4, 64, LANES), F32),
        ),
        in_specs=[hbm] * 8,
        out_specs=(hbm, hbm),
        scratch_shapes=[
            pltpu.VMEM((2, 3, FULL, LANES), F32),
            pltpu.VMEM((4, 2, 2, FULL, LANES), BF16),
            pltpu.VMEM((4, 2, 4, 64, LANES), F32),
            pltpu.VMEM((4, 2, 2, 4, 64, LANES), F32),
        ]
        + [pltpu.VMEM(t.shape, t.dtype) for t in tables]
        + [
            pltpu.VMEM(slc.shape, BF16),
            pltpu.VMEM((2, 2, FULL, LANES), BF16),
            pltpu.VMEM((4, 4, 64, LANES), F32),
            pltpu.SMEM(partner.shape, jnp.int32),
            pltpu.SMEM(valid.shape, jnp.int32),
            dma((8,)),
            dma((4, 2)),
            dma((4,)),
            dma((4,)),
            dma((3, 2, 2)),
            dma((3, 2, 2)),
            dma((3, 2)),
            dma((3, 2)),
            dma((2, 2)),
            dma((2, 2)),
        ]
        + work_shapes(),
        compiler_params=pltpu.CompilerParams(
            collective_id=0, has_side_effects=True, vmem_limit_bytes=60 * 1024 * 1024
        ),
        name="interferograms",
    )(partner, valid, slc, *tables)


def untile(array):
    lead = array.shape[:-3]
    array = array.reshape(lead + (4, 8, 8, LANES))
    n = len(lead)
    array = array.transpose(tuple(range(n)) + (n, n + 2, n + 1, n + 3))
    return array.reshape(lead + (ROWS, 8 * LANES))


def shards(slc, partner, valid):
    partner = partner.transpose(1, 2, 0)
    valid = valid.transpose(1, 2, 0)
    coherence, filtered = exchange(partner, valid, slc)
    return untile(coherence), untile(filtered)


def solution(mesh):
    in_specs = (P("date", None, "strip", None), P(None, "date", None), P(None, "date", None))
    out_specs = (P(None, "date", "strip", None), P(None, "date", None, "strip", None))
    return jax.shard_map(shards, mesh=mesh, in_specs=in_specs, out_specs=out_specs, check_vma=False)
```

```python
import functools
import math

import jax
import jax.numpy as jnp
import numpy as np
from jax import lax
from jax.experimental import pallas as pl
from jax.experimental.pallas import tpu as pltpu
from jax.sharding import PartitionSpec as P

F32 = jnp.float32
BF16 = jnp.bfloat16
MESH = pl.DeviceIdType.MESH

PATCH = 32
LOOK_A = 5
LOOK_R = 19
HALO = 2
LANES = 128
SUBS = 8
ROWS = 32
EXT = ROWS + 2 * HALO
EDGE = HALO * SUBS
BODY = ROWS * SUBS
FULL = EXT * SUBS
TINY = 1.2e-38
PAIRS = 8

BOX_SCALE = 1.0 / 128.0
BOX_RATIO = LOOK_A * LOOK_R / 128.0


def split_np(table):
    high = table.astype(np.float32).astype(jnp.bfloat16)
    low = (table - high.astype(np.float64)).astype(np.float32).astype(jnp.bfloat16)
    return high, low


def make_tables():
    lane = np.arange(LANES)
    reach = LOOK_R // 2
    centre = np.abs(lane[:, None] - lane[None, :]) <= reach
    to_next = np.abs(lane[None, :] + LANES - lane[:, None]) <= reach
    to_previous = np.abs(lane[None, :] - LANES - lane[:, None]) <= reach
    box = np.concatenate([centre, to_next | to_previous], 1) * BOX_SCALE
    box = np.concatenate([box, box], 0)

    same = lane[:, None] // PATCH == lane[None, :] // PATCH
    angle = (lane[:, None] % PATCH) * (lane[None, :] % PATCH) % PATCH * (2 * math.pi / PATCH)
    cos = np.where(same, np.cos(angle), 0.0)
    sin = np.where(same, np.sin(angle), 0.0)
    forward = np.block([[cos, -sin], [sin, cos]]) / (BOX_RATIO * PATCH * PATCH)
    inverse = np.block([[cos, sin], [-sin, cos]])
    apart = (lane[:, None] - lane[None, :]) % PATCH
    near = same & ((apart <= 1) | (apart == PATCH - 1))

    def triple(table):
        high, low = split_np(table)
        return np.concatenate([high, high, low], 0)

    def twice(table):
        return np.concatenate([table, table], 0).astype(np.float32).astype(jnp.bfloat16)

    return (
        box.astype(np.float32).astype(jnp.bfloat16),
        triple(forward),
        triple(inverse),
        twice(near),
        twice(same),
    )


def cmul(value, angle):
    re, im = value
    c, s = math.cos(angle), math.sin(angle)
    quarter = round(angle / (math.pi / 4), 9)
    if quarter == int(quarter):
        turn = int(quarter) % 8
        h = math.sqrt(0.5)
        return [
            lambda: (re, im),
            lambda: ((re - im) * h, (re + im) * h),
            lambda: (-im, re),
            lambda: (-(re + im) * h, (re - im) * h),
            lambda: (-re, -im),
            lambda: ((im - re) * h, -(re + im) * h),
            lambda: (im, -re),
            lambda: ((re + im) * h, (im - re) * h),
        ][turn]()
    return re * c - im * s, re * s + im * c


def cadd(a, b):
    return a[0] + b[0], a[1] + b[1]


def csub(a, b):
    return a[0] - b[0], a[1] - b[1]


def add_turned(a, b, sign):
    if sign > 0:
        return a[0] - b[1], a[1] + b[0]
    return a[0] + b[1], a[1] - b[0]


def dft4(x, sign):
    s0, d0 = cadd(x[0], x[2]), csub(x[0], x[2])
    s1, d1 = cadd(x[1], x[3]), csub(x[1], x[3])
    return [cadd(s0, s1), add_turned(d0, d1, sign), csub(s0, s1), add_turned(d0, d1, -sign)]


def dft8(x, sign):
    even = dft4(x[0::2], sign)
    odd = dft4(x[1::2], sign)
    out = [None] * 8
    h = math.sqrt(0.5)
    for k in range(4):
        if k == 2:
            out[2] = add_turned(even[2], odd[2], sign)
            out[6] = add_turned(even[2], odd[2], -sign)
            continue
        turned = odd[k] if k == 0 else cmul(odd[k], sign * k * math.pi / 4)
        out[k] = cadd(even[k], turned)
        out[k + 4] = csub(even[k], turned)
    return out


def row(ref_value, r):
    return ref_value[r * SUBS : (r + 1) * SUBS]


def pair_up(a, b):
    return jnp.concatenate([a, b], 0)


def split(x):
    high = x.astype(BF16)
    low = (x - high.astype(F32)).astype(BF16)
    return high, low


def root(x):
    return x * lax.rsqrt(jnp.maximum(x, TINY))


def dot(a, b):
    return jnp.dot(a, b, preferred_element_type=F32)


def row_masks(first, start, end):
    masks = []
    for r in range(EXT):
        here = first + (r - HALO)
        masks.append(jnp.where((here >= start) & (here < end), 1.0, 0.0).astype(F32))
    return masks


def multilook(first, start, end, own32, other, box_t, coherence, ml, box_in):
    masks = row_masks(first, start, end)
    sub = lax.broadcasted_iota(jnp.int32, (SUBS, LANES), 0)
    lane = lax.broadcasted_iota(jnp.int32, (SUBS, LANES), 1)
    low_half = lane < LANES // 2
    inner = jnp.where(low_half, jnp.where(sub > 0, 1.0, 0.0), jnp.where(sub < SUBS - 1, 1.0, 0.0))

    kept = [[], [], [], []]

    def add_products(q):
        at = pl.ds(q * 16, 16)
        c_re2 = other(0, at).astype(F32)
        c_im2 = other(1, at).astype(F32)
        for half in range(2):
            r = 2 * q + half
            m = masks[r]
            one = pl.ds(r * SUBS, SUBS)
            a_re = own32[0, one, :] * m
            a_im = own32[1, one, :] * m
            c_re, c_im = row(c_re2, half), row(c_im2, half)
            kept[0].append(a_re * c_re + a_im * c_im)
            kept[1].append(a_im * c_re - a_re * c_im)
            kept[2].append(own32[2, one, :] * m)
            kept[3].append((c_re * c_re + c_im * c_im) * m)

    add_products(0)
    add_products(1)
    two = [[kept[f][n] + kept[f][n + 1] for n in range(3)] for f in range(4)]
    for g in range(ROWS // SUBS):
        for q in range(4):
            add_products(2 + g * 4 + q)
            for f in range(4):
                sums = []
                for half in range(2):
                    r = g * 8 + q * 2 + half
                    two[f].append(kept[f][r + 3] + kept[f][r + 4])
                    sums.append(kept[f][r] + (two[f][r + 1] + two[f][r + 3]))
                high, low = split(pair_up(*sums))
                at = pl.ds(f * 64 + q * 16, 16)
                box_in[g % 2, at, 0:LANES] = high
                box_in[g % 2, at, LANES : 2 * LANES] = low
        y = dot(box_in[g % 2], box_t[...])
        for n in range(8):
            r = g * 8 + n
            ml_f = []
            for f in range(4):
                both = row(y, f * 8 + n)
                side = both[:, LANES:]
                side = jnp.where(low_half, pltpu.roll(side, 1, 0), pltpu.roll(side, SUBS - 1, 0))
                ml_f.append(both[:, 0:LANES] + side * inner)
            re, im, p1, p2 = ml_f
            ml[0, pl.ds(r * SUBS, SUBS), :] = re
            ml[1, pl.ds(r * SUBS, SUBS), :] = im
            size = root(re * re + im * im)
            down = lax.rsqrt(p1 * p2 + 1e-6 * BOX_RATIO * BOX_RATIO)
            coherence[g, pl.ds(n, SUBS, stride=8), :] = size * (down * masks[r + HALO])


def goldstein(first, start, end, tables, ml, filtered, mid, spec_in, mags, mag_in):
    forward_t, inverse_t, near_t, same_t = tables
    masks = row_masks(first, start, end)

    for b in range(8):
        x = [
            (ml[0, pl.ds((b + 8 * a) * SUBS, SUBS), :], ml[1, pl.ds((b + 8 * a) * SUBS, SUBS), :])
            for a in range(4)
        ]
        x = dft4(x, -1)
        for k1 in range(4):
            v = cmul(x[k1], -2 * math.pi * b * k1 / 32)
            mid[0, pl.ds((k1 * 8 + b) * SUBS, SUBS), :] = v[0]
            mid[1, pl.ds((k1 * 8 + b) * SUBS, SUBS), :] = v[1]

    def put_split(place, parts):
        for c in range(2):
            high, low = split(pair_up(parts[0][c], parts[1][c]))
            at = pl.ds(place * SUBS, 16)
            spec_in[at, c * LANES : (c + 1) * LANES] = high
            spec_in[at, (2 + c) * LANES : (3 + c) * LANES] = low

    for k1 in range(4):
        x = [
            (mid[0, pl.ds((k1 * 8 + b) * SUBS, SUBS), :], mid[1, pl.ds((k1 * 8 + b) * SUBS, SUBS), :])
            for b in range(8)
        ]
        x = dft8(x, -1)
        for k2 in range(0, 8, 2):
            put_split(k1 * 8 + k2, x[k2 : k2 + 2])

    both = spec_in[...]
    s = dot(jnp.concatenate([both, both[:, 0 : 2 * LANES]], 1), forward_t[...])
    for p in range(ROWS):
        at = pl.ds(p * SUBS, SUBS)
        re, im = row(s, p)[:, 0:LANES], row(s, p)[:, LANES:]
        mid[0, at, :] = re
        mid[1, at, :] = im
        mags[at, :] = root(re * re + im * im)

    def place(k):
        k = k % PATCH
        return (k % 4) * 8 + k // 4

    total = None
    for p in range(0, ROWS, 2):
        sums = []
        for k in (p // 8 + 4 * (p % 8), p // 8 + 4 * (p % 8 + 1)):
            sums.append(
                mags[pl.ds(place(k - 1) * SUBS, SUBS), :]
                + mags[pl.ds(place(k) * SUBS, SUBS), :]
                + mags[pl.ds(place(k + 1) * SUBS, SUBS), :]
            )
            total = sums[-1] if total is None else total + sums[-1]
        high, low = split(pair_up(*sums))
        mag_in[pl.ds(p * SUBS, 16), 0:LANES] = high
        mag_in[pl.ds(p * SUBS, 16), LANES:] = low
    high, low = split(pair_up(total, total))
    tile_sum = dot(jnp.concatenate([high, low], 1), same_t[...])[0:SUBS]
    inv = (1.0 / 9.0) / (tile_sum * (1.0 / (3 * PATCH * PATCH)) + 1e-6 / (PATCH * PATCH))
    smooth = dot(mag_in[...], near_t[...])
    for p in range(0, ROWS, 2):
        parts = []
        for n in (p, p + 1):
            w = root(row(smooth, n) * inv)
            at = pl.ds(n * SUBS, SUBS)
            parts.append((mid[0, at, :] * w, mid[1, at, :] * w))
        put_split(p, parts)

    both = spec_in[...]
    s = dot(jnp.concatenate([both, both[:, 0 : 2 * LANES]], 1), inverse_t[...])
    for k1 in range(4):
        x = [
            (row(s, k1 * 8 + k2)[:, 0:LANES], row(s, k1 * 8 + k2)[:, LANES:])
            for k2 in range(8)
        ]
        x = dft8(x, 1)
        for b in range(8):
            v = cmul(x[b], 2 * math.pi * b * k1 / 32)
            at = pl.ds((k1 * 8 + b) * SUBS, SUBS)
            mid[0, at, :] = v[0]
            mid[1, at, :] = v[1]
    for b in range(8):
        x = [
            (mid[0, pl.ds((k1 * 8 + b) * SUBS, SUBS), :], mid[1, pl.ds((k1 * 8 + b) * SUBS, SUBS), :])
            for k1 in range(4)
        ]
        x = dft4(x, 1)
        for a in range(4):
            r = b + 8 * a
            filtered[0, a, pl.ds(b, SUBS, stride=8), :] = x[a][0] * masks[r + HALO]
            filtered[1, a, pl.ds(b, SUBS, stride=8), :] = x[a][1] * masks[r + HALO]


def place_of(pair):
    turn = lax.div(pair, 2)
    return turn + lax.div(turn, 2) * (5 - 2 * turn), lax.rem(pair, 2)


def compute_most(first, partner, valid, own32, other, tables, coherence, filtered, work, before, after):
    box_in, ml, *rest = work
    box_t, *filter_t = tables

    def start(pair):
        rnd, i = place_of(pair)
        which = partner[0, i, rnd]

        def image(c, at):
            return jnp.where(which == 0, other[rnd, 0, c, at, :], other[rnd, 1, c, at, :])

        multilook(
            first, valid[i, 0, rnd], valid[i, 1, rnd], own32.at[i], image, box_t, coherence.at[rnd, i],
            ml.at[lax.rem(pair, 3)], box_in,
        )

    def finish(pair):
        rnd, i = place_of(pair)
        goldstein(
            first, valid[i, 0, rnd], valid[i, 1, rnd], filter_t, ml.at[lax.rem(pair, 3)], filtered.at[rnd, i], *rest
        )

    def step(pair, carry):
        before(pair)
        finish(pair - 1)
        start(pair)
        after(pair - 1)
        return carry

    before(jnp.int32(0))
    start(jnp.int32(0))
    lax.fori_loop(1, PAIRS - 1, step, 0)
    start(jnp.int32(PAIRS - 1))


def work_shapes():
    return [
        pltpu.VMEM((2, 256, 2 * LANES), BF16),
        pltpu.VMEM((3, 2, BODY, LANES), F32),
        *filter_shapes(),
    ]


def filter_shapes():
    return [
        pltpu.VMEM((2, BODY, LANES), F32),
        pltpu.VMEM((BODY, 4 * LANES), BF16),
        pltpu.VMEM((BODY, LANES), F32),
        pltpu.VMEM((BODY, 2 * LANES), BF16),
    ]


def exchange_kernel(
    partner_hbm, valid_hbm, slc_hbm, box_h, forward_h, inverse_h, near_h, same_h,
    coherence_hbm, filtered_hbm, ml_hbm,
    own32, other, coherence, filtered, box_t, forward_t, inverse_t, near_t, same_t,
    slc, own, lines, partner, valid, load_sem, out_sem,
    halo_send, halo_recv, main_send, main_recv, edge_send, edge_recv, fwd_send, fwd_recv, *work,
):
    date = lax.axis_index("date")
    strip = lax.axis_index("strip")
    n_strip = lax.axis_size("strip")

    def xor(bits):
        target = date
        for bit in range(4):
            if bits >> bit & 1:
                size = 1 << bit
                target = target + size - 2 * size * lax.rem(lax.div(date, size), 2)
        return target

    mate, onward = xor(1), xor(6)
    partners = {0: mate, 1: xor(2), 2: xor(4), 3: xor(8)}
    has_above, has_below = strip > 0, strip < n_strip - 1

    loads = []
    for n, (src, dst) in enumerate(
        [
            (slc_hbm, slc),
            (partner_hbm, partner),
            (valid_hbm, valid),
            (box_h, box_t),
            (forward_h, forward_t),
            (near_h, near_t),
            (same_h, same_t),
            (inverse_h, inverse_t),
        ]
    ):
        loads.append(pltpu.make_async_copy(src, dst, load_sem.at[n]))
        loads[-1].start()

    barrier = pltpu.get_barrier_semaphore()

    def greet(device):
        pl.semaphore_signal(barrier, inc=1, device_id=device, device_id_type=MESH)

    @pl.when(has_above)
    def _():
        greet((date, strip - 1))
        greet((mate, strip - 1))

    @pl.when(has_below)
    def _():
        greet((date, strip + 1))
        greet((mate, strip + 1))

    for device in (*partners.values(), onward):
        greet((device, strip))

    loads[0].wait()
    for i in range(2):
        for c in range(2):
            for g in range(4):
                for j in range(8):
                    lines[i * 2 + c, g, pl.ds(j * 8, 8), :] = slc[
                        i, c, pl.ds(g * 8, 8), pl.ds(j * LANES, LANES)
                    ].astype(F32)
            for g in range(4):
                for s in range(0, 8, 2):
                    pair = jnp.concatenate(
                        [
                            lines[i * 2 + c, g, pl.ds(s, 8, stride=8), :],
                            lines[i * 2 + c, g, pl.ds(s + 1, 8, stride=8), :],
                        ],
                        0,
                    )
                    own[i, c, pl.ds(EDGE + (g * 8 + s) * SUBS, 16), :] = pair.astype(BF16)

    top, bottom = pl.ds(0, EDGE), pl.ds(FULL - EDGE, EDGE)
    first_rows, last_rows = pl.ds(EDGE, EDGE), pl.ds(FULL - 2 * EDGE, EDGE)
    body = pl.ds(EDGE, BODY)
    blank = jnp.zeros((EDGE, LANES), BF16)

    @pl.when(jnp.logical_not(has_above))
    def _():
        for i in range(2):
            for c in range(2):
                own[i, c, top, :] = blank
                other[0, i, c, top, :] = blank

    @pl.when(jnp.logical_not(has_below))
    def _():
        for i in range(2):
            for c in range(2):
                own[i, c, bottom, :] = blank
                other[0, i, c, bottom, :] = blank

    def remote(src, dst, send_sem, recv_sem, device):
        return pltpu.make_async_remote_copy(
            src_ref=src, dst_ref=dst, send_sem=send_sem, recv_sem=recv_sem, device_id=device, device_id_type=MESH
        )

    up = [
        remote(own.at[:, :, first_rows], own.at[:, :, bottom], halo_send.at[0], halo_recv.at[0], (date, strip - 1)),
        remote(
            own.at[:, :, first_rows], other.at[0, :, :, bottom], halo_send.at[2], halo_recv.at[2], (mate, strip - 1)
        ),
    ]
    down = [
        remote(own.at[:, :, last_rows], own.at[:, :, top], halo_send.at[1], halo_recv.at[1], (date, strip + 1)),
        remote(own.at[:, :, last_rows], other.at[0, :, :, top], halo_send.at[3], halo_recv.at[3], (mate, strip + 1)),
    ]
    inside = has_above & has_below

    @pl.when(inside)
    def _():
        pl.semaphore_wait(barrier, 9)

    @pl.when(jnp.logical_not(inside))
    def _():
        pl.semaphore_wait(barrier, 7)

    @pl.when(has_above)
    def _():
        for copy in up:
            copy.start()

    @pl.when(has_below)
    def _():
        for copy in down:
            copy.start()

    mains = {}
    for i in range(2):
        for c in range(2):
            for n, r in enumerate((1, 3, 0)):
                mains[r, i, c] = remote(
                    own.at[i, c, body],
                    other.at[r, i, c, body],
                    main_send.at[n, i, c],
                    main_recv.at[n, i, c],
                    (partners[r], strip),
                )
                mains[r, i, c].start()

    def widen(i, q):
        at = pl.ds(q * 16, 16)
        re = own[i, 0, at, :].astype(F32)
        im = own[i, 1, at, :].astype(F32)
        own32[i, 0, at, :] = re
        own32[i, 1, at, :] = im
        own32[i, 2, at, :] = re * re + im * im

    for i in range(2):
        for q in range(1, EXT // 2 - 1):
            widen(i, q)

    @pl.when(has_below)
    def _():
        up[0].wait_recv()

    @pl.when(has_above)
    def _():
        down[0].wait_recv()

    edges = {}
    for n, r in enumerate((1, 2, 3)):
        for side, at in enumerate((top, bottom)):
            edges[r, side] = remote(
                own.at[:, :, at],
                other.at[r, :, :, at],
                edge_send.at[n, side],
                edge_recv.at[n, side],
                (partners[r], strip),
            )
            edges[r, side].start()
    for i in range(2):
        for q in (0, EXT // 2 - 1):
            widen(i, q)

    forwards = {}
    for i in range(2):
        for c in range(2):
            forwards[i, c] = remote(
                other.at[1, i, c, body],
                other.at[2, i, c, body],
                fwd_send.at[i, c],
                fwd_recv.at[i, c],
                (onward, strip),
            )
    for i in range(2):
        for c in range(2):
            mains[0, i, c].wait_recv()

    @pl.when(has_below)
    def _():
        up[1].wait_recv()

    @pl.when(has_above)
    def _():
        down[1].wait_recv()

    for copy in loads[1:]:
        copy.wait()
    tables = (box_t, forward_t, inverse_t, near_t, same_t)

    def outputs(pair):
        rnd, i = place_of(pair)
        return [
            pltpu.make_async_copy(coherence.at[rnd, i], coherence_hbm.at[rnd, i], out_sem.at[0, pair]),
            pltpu.make_async_copy(filtered.at[rnd, i], filtered_hbm.at[rnd, i], out_sem.at[1, pair]),
        ]

    def left_over(pair):
        rnd, i = place_of(jnp.int32(pair))
        return [
            pltpu.make_async_copy(coherence.at[rnd, i], coherence_hbm.at[rnd, i], out_sem.at[0, pair]),
            pltpu.make_async_copy(ml.at[pair % 3], ml_hbm.at[pair - PAIRS + 2], out_sem.at[1, pair]),
        ]

    def before(pair):
        @pl.when(pair == 2)
        def _():
            for i in range(2):
                for c in range(2):
                    mains[1, i, c].wait_recv()
                    forwards[i, c].start()
            edges[1, 0].wait_recv()
            edges[1, 1].wait_recv()

        @pl.when(pair == 4)
        def _():
            for i in range(2):
                for c in range(2):
                    mains[3, i, c].wait_recv()
            edges[3, 0].wait_recv()
            edges[3, 1].wait_recv()

        @pl.when(pair == 6)
        def _():
            for i in range(2):
                for c in range(2):
                    forwards[i, c].wait_recv()
            edges[2, 0].wait_recv()
            edges[2, 1].wait_recv()

    def after(pair):
        for copy in outputs(pair):
            copy.start()

    ml = work[1]
    compute_most(
        strip * ROWS, partner, valid, own32, other, tables, coherence, filtered, work, before, after
    )
    for pair in (PAIRS - 2, PAIRS - 1):
        for copy in left_over(pair):
            copy.start()

    @pl.when(has_above)
    def _():
        for copy in up:
            copy.wait_send()

    @pl.when(has_below)
    def _():
        for copy in down:
            copy.wait_send()

    for copy in (*mains.values(), *edges.values(), *forwards.values()):
        copy.wait_send()
    for pair in range(PAIRS - 2):
        for copy in outputs(jnp.int32(pair)):
            copy.wait()
    for pair in (PAIRS - 2, PAIRS - 1):
        for copy in left_over(pair):
            copy.wait()


def exchange(partner, valid, slc, tables):
    hbm = pl.BlockSpec(memory_space=pltpu.HBM)
    dma = pltpu.SemaphoreType.DMA
    return pl.pallas_call(
        exchange_kernel,
        out_shape=(
            jax.ShapeDtypeStruct((4, 2, 4, 64, LANES), F32),
            jax.ShapeDtypeStruct((4, 2, 2, 4, 64, LANES), F32),
            jax.ShapeDtypeStruct((2, 2, BODY, LANES), F32),
        ),
        in_specs=[hbm] * 8,
        out_specs=(hbm, hbm, hbm),
        scratch_shapes=[
            pltpu.VMEM((2, 3, FULL, LANES), F32),
            pltpu.VMEM((4, 2, 2, FULL, LANES), BF16),
            pltpu.VMEM((4, 2, 4, 64, LANES), F32),
            pltpu.VMEM((4, 2, 2, 4, 64, LANES), F32),
        ]
        + [pltpu.VMEM(t.shape, t.dtype) for t in tables]
        + [
            pltpu.VMEM(slc.shape, BF16),
            pltpu.VMEM((2, 2, FULL, LANES), BF16),
            pltpu.VMEM((4, 4, 64, LANES), F32),
            pltpu.SMEM(partner.shape, jnp.int32),
            pltpu.SMEM(valid.shape, jnp.int32),
            dma((8,)),
            dma((2, PAIRS)),
            dma((4,)),
            dma((4,)),
            dma((3, 2, 2)),
            dma((3, 2, 2)),
            dma((3, 2)),
            dma((3, 2)),
            dma((2, 2)),
            dma((2, 2)),
        ]
        + work_shapes(),
        compiler_params=pltpu.CompilerParams(
            collective_id=0, has_side_effects=True, vmem_limit_bytes=60 * 1024 * 1024
        ),
        name="interferograms",
    )(partner, valid, slc, *tables)


def rest_kernel(
    valid_hbm, done_coherence, done_filtered, ml_hbm, forward_h, inverse_h, near_h, same_h, coherence_hbm, filtered_hbm,
    coherence, filtered, valid, ml, forward_t, inverse_t, near_t, same_t, load_sem, in_sem, out_sem, *work,
):
    first = lax.axis_index("strip") * ROWS
    loads = []
    for n, (src, dst) in enumerate(
        [
            (ml_hbm, ml),
            (forward_h, forward_t),
            (valid_hbm, valid),
            (near_h, near_t),
            (same_h, same_t),
            (inverse_h, inverse_t),
        ]
    ):
        loads.append(pltpu.make_async_copy(src, dst, load_sem.at[n]))
        loads[-1].start()
    ins, outs = [], []
    for pair in range(PAIRS):
        turn, i = pair // 2, pair % 2
        rnd = (0, 1, 3, 2)[turn]
        ins.append(pltpu.make_async_copy(done_coherence.at[rnd, i], coherence.at[rnd, i], in_sem.at[0, pair]))
        outs.append(pltpu.make_async_copy(coherence.at[rnd, i], coherence_hbm.at[rnd, i], out_sem.at[0, pair]))
        if pair < PAIRS - 2:
            ins.append(pltpu.make_async_copy(done_filtered.at[rnd, i], filtered.at[rnd, i], in_sem.at[1, pair]))
            outs.append(pltpu.make_async_copy(filtered.at[rnd, i], filtered_hbm.at[rnd, i], out_sem.at[1, pair]))
    for copy in ins:
        copy.start()
    for copy in loads:
        copy.wait()

    def made(n):
        rnd, i = place_of(n + PAIRS - 2)
        return pltpu.make_async_copy(filtered.at[rnd, i], filtered_hbm.at[rnd, i], out_sem.at[1, n + PAIRS - 2])

    def finish(n, carry):
        @pl.when(n == 1)
        def _():
            for copy_in, copy_out in zip(ins, outs):
                copy_in.wait()
                copy_out.start()

        rnd, i = place_of(n + PAIRS - 2)
        goldstein(
            first,
            valid[i, 0, rnd],
            valid[i, 1, rnd],
            (forward_t, inverse_t, near_t, same_t),
            ml.at[n],
            filtered.at[rnd, i],
            *work,
        )
        made(n).start()
        return carry

    lax.fori_loop(0, 2, finish, 0)
    for copy in outs:
        copy.wait()
    for n in range(2):
        made(jnp.int32(n)).wait()


def rest(valid, coherence, filtered, ml, tables):
    hbm = pl.BlockSpec(memory_space=pltpu.HBM)
    dma = pltpu.SemaphoreType.DMA
    return pl.pallas_call(
        rest_kernel,
        out_shape=(
            jax.ShapeDtypeStruct(coherence.shape, F32),
            jax.ShapeDtypeStruct(filtered.shape, F32),
        ),
        in_specs=[hbm] * 8,
        out_specs=(hbm, hbm),
        scratch_shapes=[
            pltpu.VMEM(coherence.shape, F32),
            pltpu.VMEM(filtered.shape, F32),
            pltpu.SMEM(valid.shape, jnp.int32),
            pltpu.VMEM(ml.shape, F32),
        ]
        + [pltpu.VMEM(t.shape, t.dtype) for t in tables]
        + [dma((6,)), dma((2, PAIRS)), dma((2, PAIRS))]
        + filter_shapes(),
        compiler_params=pltpu.CompilerParams(vmem_limit_bytes=60 * 1024 * 1024),
        name="rest",
    )(valid, coherence, filtered, ml, *tables)


def untile(array):
    lead = array.shape[:-3]
    array = array.reshape(lead + (4, 8, 8, LANES))
    n = len(lead)
    array = array.transpose(tuple(range(n)) + (n, n + 2, n + 1, n + 3))
    return array.reshape(lead + (ROWS, 8 * LANES))


def shards(slc, partner, valid):
    partner = partner.transpose(1, 2, 0)
    valid = valid.transpose(1, 2, 0)
    tables = [jnp.asarray(t) for t in make_tables()]
    coherence, filtered, ml = exchange(partner, valid, slc, tables)
    coherence, filtered = rest(valid, coherence, filtered, ml, tables[1:])
    return untile(coherence), untile(filtered)


def solution(mesh):
    in_specs = (P("date", None, "strip", None), P(None, "date", None), P(None, "date", None))
    out_specs = (P(None, "date", "strip", None), P(None, "date", None, "strip", None))
    return jax.shard_map(shards, mesh=mesh, in_specs=in_specs, out_specs=out_specs, check_vma=False)
```

```python
import functools
import math

import jax
import jax.numpy as jnp
import numpy as np
from jax import lax
from jax.experimental import pallas as pl
from jax.experimental.pallas import tpu as pltpu
from jax.sharding import PartitionSpec as P

F32 = jnp.float32
BF16 = jnp.bfloat16
MESH = pl.DeviceIdType.MESH

PATCH = 32
LOOK_A = 5
LOOK_R = 19
HALO = 2
LANES = 128
SUBS = 8
ROWS = 32
EXT = ROWS + 2 * HALO
EDGE = HALO * SUBS
BODY = ROWS * SUBS
FULL = EXT * SUBS
TINY = 1.2e-38

BOX_SCALE = 1.0 / 128.0
BOX_RATIO = LOOK_A * LOOK_R / 128.0


def split_np(table):
    high = table.astype(np.float32).astype(jnp.bfloat16)
    low = (table - high.astype(np.float64)).astype(np.float32).astype(jnp.bfloat16)
    return high, low


def make_tables():
    lane = np.arange(LANES)
    reach = LOOK_R // 2
    centre = np.abs(lane[:, None] - lane[None, :]) <= reach
    to_next = np.abs(lane[None, :] + LANES - lane[:, None]) <= reach
    to_previous = np.abs(lane[None, :] - LANES - lane[:, None]) <= reach
    box = np.concatenate([centre, to_next | to_previous], 1) * BOX_SCALE
    box = np.concatenate([box, box], 0)

    same = lane[:, None] // PATCH == lane[None, :] // PATCH
    angle = (lane[:, None] % PATCH) * (lane[None, :] % PATCH) % PATCH * (2 * math.pi / PATCH)
    cos = np.where(same, np.cos(angle), 0.0)
    sin = np.where(same, np.sin(angle), 0.0)
    forward = np.block([[cos, -sin], [sin, cos]]) / (BOX_RATIO * PATCH * PATCH)
    inverse = np.block([[cos, sin], [-sin, cos]])
    apart = (lane[:, None] - lane[None, :]) % PATCH
    near = same & ((apart <= 1) | (apart == PATCH - 1))

    def triple(table):
        high, low = split_np(table)
        return np.concatenate([high, high, low], 0)

    def twice(table):
        return np.concatenate([table, table], 0).astype(np.float32).astype(jnp.bfloat16)

    return (
        box.astype(np.float32).astype(jnp.bfloat16),
        triple(forward),
        triple(inverse),
        twice(near),
        twice(same),
    )


def cmul(value, angle):
    re, im = value
    c, s = math.cos(angle), math.sin(angle)
    quarter = round(angle / (math.pi / 4), 9)
    if quarter == int(quarter):
        turn = int(quarter) % 8
        h = math.sqrt(0.5)
        return [
            lambda: (re, im),
            lambda: ((re - im) * h, (re + im) * h),
            lambda: (-im, re),
            lambda: (-(re + im) * h, (re - im) * h),
            lambda: (-re, -im),
            lambda: ((im - re) * h, -(re + im) * h),
            lambda: (im, -re),
            lambda: ((re + im) * h, (im - re) * h),
        ][turn]()
    return re * c - im * s, re * s + im * c


def cadd(a, b):
    return a[0] + b[0], a[1] + b[1]


def csub(a, b):
    return a[0] - b[0], a[1] - b[1]


def add_turned(a, b, sign):
    if sign > 0:
        return a[0] - b[1], a[1] + b[0]
    return a[0] + b[1], a[1] - b[0]


def dft4(x, sign):
    s0, d0 = cadd(x[0], x[2]), csub(x[0], x[2])
    s1, d1 = cadd(x[1], x[3]), csub(x[1], x[3])
    return [cadd(s0, s1), add_turned(d0, d1, sign), csub(s0, s1), add_turned(d0, d1, -sign)]


def dft8(x, sign):
    even = dft4(x[0::2], sign)
    odd = dft4(x[1::2], sign)
    out = [None] * 8
    h = math.sqrt(0.5)
    for k in range(4):
        if k == 2:
            out[2] = add_turned(even[2], odd[2], sign)
            out[6] = add_turned(even[2], odd[2], -sign)
            continue
        turned = odd[k] if k == 0 else cmul(odd[k], sign * k * math.pi / 4)
        out[k] = cadd(even[k], turned)
        out[k + 4] = csub(even[k], turned)
    return out


def row(ref_value, r):
    return ref_value[r * SUBS : (r + 1) * SUBS]


def pair_up(a, b):
    return jnp.concatenate([a, b], 0)


def split(x):
    high = x.astype(BF16)
    low = (x - high.astype(F32)).astype(BF16)
    return high, low


def root(x):
    return x * lax.rsqrt(jnp.maximum(x, TINY))


def dot(a, b):
    return jnp.dot(a, b, preferred_element_type=F32)


def row_masks(first, start, end):
    masks = []
    for r in range(EXT):
        here = first + (r - HALO)
        masks.append(jnp.where((here >= start) & (here < end), 1.0, 0.0).astype(F32))
    return masks


def added(*terms):
    total = None
    for term in terms:
        if term is not None:
            total = term if total is None else total + term
    return total


class Look:
    def __init__(self, first, start, end, own32, other, box_t, coherence, ml, part):
        self.masks = row_masks(first, start, end)
        self.own32, self.other, self.box_t = own32, other, box_t
        self.coherence, self.ml, self.part = coherence, ml, part
        sub = lax.broadcasted_iota(jnp.int32, (SUBS, LANES), 0)
        lane = lax.broadcasted_iota(jnp.int32, (SUBS, LANES), 1)
        self.low_half = lane < LANES // 2
        self.inner = jnp.where(
            self.low_half, jnp.where(sub > 0, 1.0, 0.0), jnp.where(sub < SUBS - 1, 1.0, 0.0)
        )

    def products(self, q):
        at = pl.ds(q * 16, 16)
        c_re2 = self.other(0, at).astype(F32)
        c_im2 = self.other(1, at).astype(F32)
        rows = []
        for half in range(2):
            m = self.masks[2 * q + half]
            one = pl.ds((2 * q + half) * SUBS, SUBS)
            a_re = self.own32[0, one, :] * m
            a_im = self.own32[1, one, :] * m
            c_re, c_im = row(c_re2, half), row(c_im2, half)
            rows.append(
                (
                    a_re * c_re + a_im * c_im,
                    a_im * c_re - a_re * c_im,
                    self.own32[2, one, :] * m,
                    (c_re * c_re + c_im * c_im) * m,
                )
            )
        return rows

    def boxed(self, y, place):
        both = row(y, place)
        side = both[:, LANES:]
        side = jnp.where(self.low_half, pltpu.roll(side, 1, 0), pltpu.roll(side, SUBS - 1, 0))
        return both[:, 0:LANES] + side * self.inner

    def put(self, r, re, im, p1, p2):
        self.ml[0, pl.ds(r * SUBS, SUBS), :] = re
        self.ml[1, pl.ds(r * SUBS, SUBS), :] = im
        size = root(re * re + im * im)
        down = lax.rsqrt(p1 * p2 + 1e-6 * BOX_RATIO * BOX_RATIO)
        self.coherence[r // 8, pl.ds(r % 8, SUBS, stride=8), :] = size * (down * self.masks[r + HALO])


EDGE_ROWS = (0, 1, ROWS - 2, ROWS - 1)


def multilook(look, box_in):
    kept = [[None, None] for _ in range(4)]

    def add_products(q):
        for fields in look.products(q):
            for f in range(4):
                kept[f].append(fields[f])

    add_products(1)
    two = [[None, kept[f][2], kept[f][2] + kept[f][3]] for f in range(4)]
    for g in range(ROWS // SUBS):
        for q in range(4):
            tile = 2 + g * 4 + q
            if tile < EXT // 2 - 1:
                add_products(tile)
            else:
                for f in range(4):
                    kept[f] += [None, None]
            for f in range(4):
                sums = []
                for half in range(2):
                    r = g * 8 + q * 2 + half
                    two[f].append(added(kept[f][r + 3], kept[f][r + 4]))
                    sums.append(added(kept[f][r], added(two[f][r + 1], two[f][r + 3])))
                high, low = split(pair_up(*sums))
                at = pl.ds(f * 64 + q * 16, 16)
                box_in[g % 2, at, 0:LANES] = high
                box_in[g % 2, at, LANES : 2 * LANES] = low
        y = dot(box_in[g % 2], look.box_t[...])
        for n in range(8):
            r = g * 8 + n
            fields = [look.boxed(y, f * 8 + n) for f in range(4)]
            if r in EDGE_ROWS:
                at = pl.ds(EDGE_ROWS.index(r) * SUBS, SUBS)
                look.ml[0, pl.ds(r * SUBS, SUBS), :] = fields[0]
                look.ml[1, pl.ds(r * SUBS, SUBS), :] = fields[1]
                look.part[0, at, :] = fields[2]
                look.part[1, at, :] = fields[3]
            else:
                look.put(r, *fields)


def add_halo(look, halo_in):
    before = look.products(0)
    after = look.products(EXT // 2 - 1)
    for f in range(4):
        for n, rows in enumerate(
            [(before[0][f] + before[1][f], before[1][f]), (after[0][f], after[0][f] + after[1][f])]
        ):
            high, low = split(pair_up(*rows))
            at = pl.ds(f * 32 + n * 16, 16)
            halo_in[at, 0:LANES] = high
            halo_in[at, LANES : 2 * LANES] = low
    y = dot(halo_in[...], look.box_t[...])
    for n, r in enumerate(EDGE_ROWS):
        at, here = pl.ds(n * SUBS, SUBS), pl.ds(r * SUBS, SUBS)
        held = [look.ml[0, here, :], look.ml[1, here, :], look.part[0, at, :], look.part[1, at, :]]
        look.put(r, *[held[f] + look.boxed(y, f * 4 + n) for f in range(4)])


def goldstein(first, start, end, tables, ml, filtered, mid, spec_in, mags, mag_in):
    forward_t, inverse_t, near_t, same_t = tables
    masks = row_masks(first, start, end)

    for b in range(8):
        x = [
            (ml[0, pl.ds((b + 8 * a) * SUBS, SUBS), :], ml[1, pl.ds((b + 8 * a) * SUBS, SUBS), :])
            for a in range(4)
        ]
        x = dft4(x, -1)
        for k1 in range(4):
            v = cmul(x[k1], -2 * math.pi * b * k1 / 32)
            mid[0, pl.ds((k1 * 8 + b) * SUBS, SUBS), :] = v[0]
            mid[1, pl.ds((k1 * 8 + b) * SUBS, SUBS), :] = v[1]

    def put_split(place, parts):
        for c in range(2):
            high, low = split(pair_up(parts[0][c], parts[1][c]))
            at = pl.ds(place * SUBS, 16)
            spec_in[at, c * LANES : (c + 1) * LANES] = high
            spec_in[at, (2 + c) * LANES : (3 + c) * LANES] = low

    for k1 in range(4):
        x = [
            (mid[0, pl.ds((k1 * 8 + b) * SUBS, SUBS), :], mid[1, pl.ds((k1 * 8 + b) * SUBS, SUBS), :])
            for b in range(8)
        ]
        x = dft8(x, -1)
        for k2 in range(0, 8, 2):
            put_split(k1 * 8 + k2, x[k2 : k2 + 2])

    both = spec_in[...]
    s = dot(jnp.concatenate([both, both[:, 0 : 2 * LANES]], 1), forward_t[...])
    for p in range(ROWS):
        at = pl.ds(p * SUBS, SUBS)
        re, im = row(s, p)[:, 0:LANES], row(s, p)[:, LANES:]
        mid[0, at, :] = re
        mid[1, at, :] = im
        mags[at, :] = root(re * re + im * im)

    def place(k):
        k = k % PATCH
        return (k % 4) * 8 + k // 4

    total = None
    for p in range(0, ROWS, 2):
        sums = []
        for k in (p // 8 + 4 * (p % 8), p // 8 + 4 * (p % 8 + 1)):
            sums.append(
                mags[pl.ds(place(k - 1) * SUBS, SUBS), :]
                + mags[pl.ds(place(k) * SUBS, SUBS), :]
                + mags[pl.ds(place(k + 1) * SUBS, SUBS), :]
            )
            total = sums[-1] if total is None else total + sums[-1]
        high, low = split(pair_up(*sums))
        mag_in[pl.ds(p * SUBS, 16), 0:LANES] = high
        mag_in[pl.ds(p * SUBS, 16), LANES:] = low
    high, low = split(pair_up(total, total))
    tile_sum = dot(jnp.concatenate([high, low], 1), same_t[...])[0:SUBS]
    inv = (1.0 / 9.0) / (tile_sum * (1.0 / (3 * PATCH * PATCH)) + 1e-6 / (PATCH * PATCH))
    smooth = dot(mag_in[...], near_t[...])
    for p in range(0, ROWS, 2):
        parts = []
        for n in (p, p + 1):
            w = root(row(smooth, n) * inv)
            at = pl.ds(n * SUBS, SUBS)
            parts.append((mid[0, at, :] * w, mid[1, at, :] * w))
        put_split(p, parts)

    both = spec_in[...]
    s = dot(jnp.concatenate([both, both[:, 0 : 2 * LANES]], 1), inverse_t[...])
    for k1 in range(4):
        x = [
            (row(s, k1 * 8 + k2)[:, 0:LANES], row(s, k1 * 8 + k2)[:, LANES:])
            for k2 in range(8)
        ]
        x = dft8(x, 1)
        for b in range(8):
            v = cmul(x[b], 2 * math.pi * b * k1 / 32)
            at = pl.ds((k1 * 8 + b) * SUBS, SUBS)
            mid[0, at, :] = v[0]
            mid[1, at, :] = v[1]
    for b in range(8):
        x = [
            (mid[0, pl.ds((k1 * 8 + b) * SUBS, SUBS), :], mid[1, pl.ds((k1 * 8 + b) * SUBS, SUBS), :])
            for k1 in range(4)
        ]
        x = dft4(x, 1)
        for a in range(4):
            r = b + 8 * a
            filtered[0, a, pl.ds(b, SUBS, stride=8), :] = x[a][0] * masks[r + HALO]
            filtered[1, a, pl.ds(b, SUBS, stride=8), :] = x[a][1] * masks[r + HALO]


def place_of(turn):
    return turn + lax.div(turn, 2) * (5 - 2 * turn)


def compute_all(
    first, partner, valid, own32, other, tables, coherence, filtered, work, before_look, before_halo, after
):
    box_in, halo_in, ml, part, *rest = work
    box_t, *filter_t = tables
    turns = 4

    def look_of(rnd, i):
        which = partner[0, i, rnd]

        def image(c, at):
            return jnp.where(which == 0, other[rnd, 0, c, at, :], other[rnd, 1, c, at, :])

        return Look(
            first, valid[i, 0, rnd], valid[i, 1, rnd], own32.at[i], image, box_t, coherence.at[rnd, i],
            ml.at[rnd, i], part.at[rnd, i],
        )

    def look_turn(turn):
        before_look(turn)
        rnd = place_of(turn)
        for i in range(2):
            multilook(look_of(rnd, i), box_in.at[i])

    def halo_turn(turn):
        before_halo(turn)
        rnd = place_of(turn)
        for i in range(2):
            add_halo(look_of(rnd, i), halo_in.at[i])

    def filter_turn(turn):
        halo_turn(turn)
        rnd = place_of(turn)
        for i in range(2):
            goldstein(
                first, valid[i, 0, rnd], valid[i, 1, rnd], filter_t, ml.at[rnd, i], filtered.at[rnd, i],
                *[ref.at[i] for ref in rest],
            )
        after(turn)

    def step(n, carry):
        looks = (n < turns - 1) | (n == turns + 1)

        @pl.when(looks)
        def _():
            look_turn(jnp.minimum(n, turns - 1))

        @pl.when(jnp.logical_not(looks))
        def _():
            filter_turn(n - (turns - 1) - lax.div(n, turns + 1))

        return carry

    lax.fori_loop(0, 2 * turns, step, 0)


def work_shapes():
    return [
        pltpu.VMEM((2, 2, 256, 2 * LANES), BF16),
        pltpu.VMEM((2, 128, 2 * LANES), BF16),
        pltpu.VMEM((4, 2, 2, BODY, LANES), F32),
        pltpu.VMEM((4, 2, 2, 4 * SUBS, LANES), F32),
        pltpu.VMEM((2, 2, BODY, LANES), F32),
        pltpu.VMEM((2, BODY, 4 * LANES), BF16),
        pltpu.VMEM((2, BODY, LANES), F32),
        pltpu.VMEM((2, BODY, 2 * LANES), BF16),
    ]


def exchange_kernel(
    partner_hbm, valid_hbm, slc_hbm, box_h, forward_h, inverse_h, near_h, same_h,
    coherence_hbm, filtered_hbm,
    own32, other, coherence, filtered, box_t, forward_t, inverse_t, near_t, same_t,
    slc, own, lines, partner, valid, load_sem, out_sem,
    far_sem, halo_send, halo_recv, main_send, main_recv, edge_send, edge_recv, fwd_send, fwd_recv, *work,
):
    date = lax.axis_index("date")
    strip = lax.axis_index("strip")
    n_strip = lax.axis_size("strip")

    def xor(bits):
        target = date
        for bit in range(4):
            if bits >> bit & 1:
                size = 1 << bit
                target = target + size - 2 * size * lax.rem(lax.div(date, size), 2)
        return target

    mate, onward = xor(1), xor(6)
    partners = {0: mate, 1: xor(2), 2: xor(4), 3: xor(8)}
    has_above, has_below = strip > 0, strip < n_strip - 1
    far_upper, far_lower = strip == n_strip // 2 - 1, strip == n_strip // 2
    upper_asks = date < lax.axis_size("date") * 3 // 4
    upper_answers = jnp.logical_not(upper_asks)
    asks = (far_upper & upper_asks) | (far_lower & upper_answers)

    loads = []
    for n, (src, dst) in enumerate(
        [
            (slc_hbm, slc),
            (partner_hbm, partner),
            (valid_hbm, valid),
            (box_h, box_t),
            (forward_h, forward_t),
            (near_h, near_t),
            (same_h, same_t),
            (inverse_h, inverse_t),
        ]
    ):
        loads.append(pltpu.make_async_copy(src, dst, load_sem.at[n]))
        loads[-1].start()

    barrier = pltpu.get_barrier_semaphore()

    def greet(device):
        pl.semaphore_signal(barrier, inc=1, device_id=device, device_id_type=MESH)

    @pl.when(has_above & jnp.logical_not(far_lower & upper_asks))
    def _():
        greet((date, strip - 1))
        greet((mate, strip - 1))

    @pl.when(has_below & jnp.logical_not(far_upper & upper_answers))
    def _():
        greet((date, strip + 1))
        greet((mate, strip + 1))

    for device in (*partners.values(), onward):
        greet((device, strip))

    loads[0].wait()
    for i in range(2):
        for c in range(2):
            for g in range(4):
                for j in range(8):
                    lines[i * 2 + c, g, pl.ds(j * 8, 8), :] = slc[
                        i, c, pl.ds(g * 8, 8), pl.ds(j * LANES, LANES)
                    ].astype(F32)
            for g in range(4):
                for s in range(0, 8, 2):
                    pair = jnp.concatenate(
                        [
                            lines[i * 2 + c, g, pl.ds(s, 8, stride=8), :],
                            lines[i * 2 + c, g, pl.ds(s + 1, 8, stride=8), :],
                        ],
                        0,
                    )
                    own[i, c, pl.ds(EDGE + (g * 8 + s) * SUBS, 16), :] = pair.astype(BF16)

    top, bottom = pl.ds(0, EDGE), pl.ds(FULL - EDGE, EDGE)
    first_rows, last_rows = pl.ds(EDGE, EDGE), pl.ds(FULL - 2 * EDGE, EDGE)
    body = pl.ds(EDGE, BODY)
    blank = jnp.zeros((EDGE, LANES), BF16)

    @pl.when(jnp.logical_not(has_above))
    def _():
        for i in range(2):
            for c in range(2):
                own[i, c, top, :] = blank
                other[0, i, c, top, :] = blank

    @pl.when(jnp.logical_not(has_below))
    def _():
        for i in range(2):
            for c in range(2):
                own[i, c, bottom, :] = blank
                other[0, i, c, bottom, :] = blank

    def remote(src, dst, send_sem, recv_sem, device):
        return pltpu.make_async_remote_copy(
            src_ref=src, dst_ref=dst, send_sem=send_sem, recv_sem=recv_sem, device_id=device, device_id_type=MESH
        )

    up = [
        remote(own.at[:, :, first_rows], own.at[:, :, bottom], halo_send.at[0], halo_recv.at[0], (date, strip - 1)),
        remote(
            own.at[:, :, first_rows], other.at[0, :, :, bottom], halo_send.at[2], halo_recv.at[2], (mate, strip - 1)
        ),
    ]
    down = [
        remote(own.at[:, :, last_rows], own.at[:, :, top], halo_send.at[1], halo_recv.at[1], (date, strip + 1)),
        remote(own.at[:, :, last_rows], other.at[0, :, :, top], halo_send.at[3], halo_recv.at[3], (mate, strip + 1)),
    ]
    inside = has_above & has_below & jnp.logical_not(asks)

    @pl.when(inside)
    def _():
        pl.semaphore_wait(barrier, 9)

    @pl.when(jnp.logical_not(inside))
    def _():
        pl.semaphore_wait(barrier, 7)

    @pl.when(has_above & jnp.logical_not(far_lower & asks))
    def _():
        for copy in up:
            copy.start()

    @pl.when(has_below & jnp.logical_not(far_upper & asks))
    def _():
        for copy in down:
            copy.start()

    @pl.when(far_lower & upper_asks)
    def _():
        for device in (date, mate):
            pl.semaphore_signal(far_sem, inc=1, device_id=(device, strip - 1), device_id_type=MESH)

    @pl.when(far_upper & upper_answers)
    def _():
        for device in (date, mate):
            pl.semaphore_signal(far_sem, inc=1, device_id=(device, strip + 1), device_id_type=MESH)

    mains = {}
    for i in range(2):
        for c in range(2):
            for n, r in enumerate((1, 3, 0)):
                mains[r, i, c] = remote(
                    own.at[i, c, body],
                    other.at[r, i, c, body],
                    main_send.at[n, i, c],
                    main_recv.at[n, i, c],
                    (partners[r], strip),
                )
                mains[r, i, c].start()

    def widen(i, q):
        at = pl.ds(q * 16, 16)
        re = own[i, 0, at, :].astype(F32)
        im = own[i, 1, at, :].astype(F32)
        own32[i, 0, at, :] = re
        own32[i, 1, at, :] = im
        own32[i, 2, at, :] = re * re + im * im

    for i in range(2):
        for q in range(1, EXT // 2 - 1):
            widen(i, q)

    forwards, edges = {}, {}
    for i in range(2):
        for c in range(2):
            forwards[i, c] = remote(
                other.at[1, i, c, body],
                other.at[2, i, c, body],
                fwd_send.at[i, c],
                fwd_recv.at[i, c],
                (onward, strip),
            )
    for n, r in enumerate((1, 2, 3)):
        for side, at in enumerate((top, bottom)):
            edges[r, side] = remote(
                own.at[:, :, at],
                other.at[r, :, :, at],
                edge_send.at[n, side],
                edge_recv.at[n, side],
                (partners[r], strip),
            )

    far = far_upper | far_lower

    def take_halo():
        @pl.when(has_below)
        def _():
            up[0].wait_recv()

        @pl.when(has_above)
        def _():
            down[0].wait_recv()

        for copy in edges.values():
            copy.start()
        for i in range(2):
            for q in (0, EXT // 2 - 1):
                widen(i, q)

    def send_far():
        @pl.when(asks)
        def _():
            pl.semaphore_wait(far_sem, 2)

        @pl.when(far_upper & asks)
        def _():
            for copy in down:
                copy.start()

        @pl.when(far_lower & asks)
        def _():
            for copy in up:
                copy.start()

    def before_look(turn):
        @pl.when(turn == 0)
        def _():
            for i in range(2):
                for c in range(2):
                    mains[0, i, c].wait_recv()
            for copy in loads[1:]:
                copy.wait()

        @pl.when(turn == 1)
        def _():
            @pl.when(jnp.logical_not(far))
            def _():
                take_halo()

            for i in range(2):
                for c in range(2):
                    mains[1, i, c].wait_recv()
                    forwards[i, c].start()
                if i == 0:
                    send_far()

        @pl.when(turn == 2)
        def _():
            for i in range(2):
                for c in range(2):
                    mains[3, i, c].wait_recv()

        @pl.when(turn == 3)
        def _():
            for copy in forwards.values():
                copy.wait_recv()

    def before_halo(turn):
        @pl.when(turn == 0)
        def _():
            @pl.when(far)
            def _():
                take_halo()

            @pl.when(has_below)
            def _():
                up[1].wait_recv()

            @pl.when(has_above)
            def _():
                down[1].wait_recv()

        for n, r in ((1, 1), (2, 3), (3, 2)):

            @pl.when(turn == n)
            def _(r=r):
                edges[r, 0].wait_recv()
                edges[r, 1].wait_recv()

    def outputs(turn):
        rnd = place_of(turn)
        return [
            pltpu.make_async_copy(coherence.at[rnd], coherence_hbm.at[rnd], out_sem.at[0, turn]),
            pltpu.make_async_copy(filtered.at[rnd], filtered_hbm.at[rnd], out_sem.at[1, turn]),
        ]

    def after(turn):
        for copy in outputs(turn):
            copy.start()

    tables = (box_t, forward_t, inverse_t, near_t, same_t)
    compute_all(
        strip * ROWS, partner, valid, own32, other, tables, coherence, filtered, work, before_look, before_halo, after
    )

    @pl.when(has_above)
    def _():
        for copy in up:
            copy.wait_send()

    @pl.when(has_below)
    def _():
        for copy in down:
            copy.wait_send()

    for copy in (*mains.values(), *edges.values(), *forwards.values()):
        copy.wait_send()
    for turn in range(4):
        for copy in outputs(jnp.int32(turn)):
            copy.wait()


def exchange(partner, valid, slc, tables):
    hbm = pl.BlockSpec(memory_space=pltpu.HBM)
    dma = pltpu.SemaphoreType.DMA
    return pl.pallas_call(
        exchange_kernel,
        out_shape=(
            jax.ShapeDtypeStruct((4, 2, 4, 64, LANES), F32),
            jax.ShapeDtypeStruct((4, 2, 2, 4, 64, LANES), F32),
        ),
        in_specs=[hbm] * 8,
        out_specs=(hbm, hbm),
        scratch_shapes=[
            pltpu.VMEM((2, 3, FULL, LANES), F32),
            pltpu.VMEM((4, 2, 2, FULL, LANES), BF16),
            pltpu.VMEM((4, 2, 4, 64, LANES), F32),
            pltpu.VMEM((4, 2, 2, 4, 64, LANES), F32),
        ]
        + [pltpu.VMEM(t.shape, t.dtype) for t in tables]
        + [
            pltpu.VMEM(slc.shape, BF16),
            pltpu.VMEM((2, 2, FULL, LANES), BF16),
            pltpu.VMEM((4, 4, 64, LANES), F32),
            pltpu.SMEM(partner.shape, jnp.int32),
            pltpu.SMEM(valid.shape, jnp.int32),
            dma((8,)),
            dma((2, 4)),
            pltpu.SemaphoreType.REGULAR,
            dma((4,)),
            dma((4,)),
            dma((3, 2, 2)),
            dma((3, 2, 2)),
            dma((3, 2)),
            dma((3, 2)),
            dma((2, 2)),
            dma((2, 2)),
        ]
        + work_shapes(),
        compiler_params=pltpu.CompilerParams(
            collective_id=0, has_side_effects=True, vmem_limit_bytes=60 * 1024 * 1024
        ),
        name="interferograms",
    )(partner, valid, slc, *tables)


def hand_on_kernel(done_coherence, done_filtered, coherence_hbm, filtered_hbm, coherence, filtered, in_sem, out_sem):
    ins, outs = [], []
    for rnd in range(4):
        for i in range(2):
            for n, (src, by, dst) in enumerate(
                [(done_filtered, filtered, filtered_hbm), (done_coherence, coherence, coherence_hbm)]
            ):
                ins.append(pltpu.make_async_copy(src.at[rnd, i], by.at[rnd, i], in_sem.at[n, rnd, i]))
                outs.append(pltpu.make_async_copy(by.at[rnd, i], dst.at[rnd, i], out_sem.at[n, rnd, i]))
    for copy in ins:
        copy.start()
    for copy_in, copy_out in zip(ins, outs):
        copy_in.wait()
        copy_out.start()
    for copy in outs:
        copy.wait()


def hand_on(coherence, filtered):
    hbm = pl.BlockSpec(memory_space=pltpu.HBM)
    dma = pltpu.SemaphoreType.DMA
    return pl.pallas_call(
        hand_on_kernel,
        out_shape=(
            jax.ShapeDtypeStruct(coherence.shape, F32),
            jax.ShapeDtypeStruct(filtered.shape, F32),
        ),
        in_specs=[hbm, hbm],
        out_specs=(hbm, hbm),
        scratch_shapes=[
            pltpu.VMEM(coherence.shape, F32),
            pltpu.VMEM(filtered.shape, F32),
            dma((2, 4, 2)),
            dma((2, 4, 2)),
        ],
        compiler_params=pltpu.CompilerParams(vmem_limit_bytes=60 * 1024 * 1024),
        name="hand_on",
    )(coherence, filtered)


def untile(array):
    lead = array.shape[:-3]
    array = array.reshape(lead + (4, 8, 8, LANES))
    n = len(lead)
    array = array.transpose(tuple(range(n)) + (n, n + 2, n + 1, n + 3))
    return array.reshape(lead + (ROWS, 8 * LANES))


def shards(slc, partner, valid):
    partner = partner.transpose(1, 2, 0)
    valid = valid.transpose(1, 2, 0)
    tables = [jnp.asarray(t) for t in make_tables()]
    coherence, filtered = hand_on(*exchange(partner, valid, slc, tables))
    return untile(coherence), untile(filtered)


def solution(mesh):
    in_specs = (P("date", None, "strip", None), P(None, "date", None), P(None, "date", None))
    out_specs = (P(None, "date", "strip", None), P(None, "date", None, "strip", None))
    return jax.shard_map(shards, mesh=mesh, in_specs=in_specs, out_specs=out_specs, check_vma=False)
```

```python
import functools
import math

import jax
import jax.numpy as jnp
import numpy as np
from jax import lax
from jax.experimental import pallas as pl
from jax.experimental.pallas import tpu as pltpu
from jax.sharding import PartitionSpec as P

F32 = jnp.float32
BF16 = jnp.bfloat16
MESH = pl.DeviceIdType.MESH

PATCH = 32
LOOK_A = 5
LOOK_R = 19
HALO = 2
LANES = 128
SUBS = 8
ROWS = 32
EXT = ROWS + 2 * HALO
EDGE = HALO * SUBS
BODY = ROWS * SUBS
FULL = EXT * SUBS
TINY = 1.2e-38

BOX_SCALE = 1.0 / 128.0
BOX_RATIO = LOOK_A * LOOK_R / 128.0


def split_np(table):
    high = table.astype(np.float32).astype(jnp.bfloat16)
    low = (table - high.astype(np.float64)).astype(np.float32).astype(jnp.bfloat16)
    return high, low


def make_tables():
    lane = np.arange(LANES)
    reach = LOOK_R // 2
    centre = np.abs(lane[:, None] - lane[None, :]) <= reach
    to_next = np.abs(lane[None, :] + LANES - lane[:, None]) <= reach
    to_previous = np.abs(lane[None, :] - LANES - lane[:, None]) <= reach
    box = np.concatenate([centre, to_next | to_previous], 1) * BOX_SCALE
    box = np.concatenate([box, box], 0)

    same = lane[:, None] // PATCH == lane[None, :] // PATCH
    angle = (lane[:, None] % PATCH) * (lane[None, :] % PATCH) % PATCH * (2 * math.pi / PATCH)
    cos = np.where(same, np.cos(angle), 0.0)
    sin = np.where(same, np.sin(angle), 0.0)
    forward = np.block([[cos, -sin], [sin, cos]]) / (BOX_RATIO * PATCH * PATCH)
    inverse = np.block([[cos, sin], [-sin, cos]])
    apart = (lane[:, None] - lane[None, :]) % PATCH
    near = same & ((apart <= 1) | (apart == PATCH - 1))

    def triple(table):
        high, low = split_np(table)
        return np.concatenate([high, high, low], 0)

    def twice(table):
        return np.concatenate([table, table], 0).astype(np.float32).astype(jnp.bfloat16)

    return (
        box.astype(np.float32).astype(jnp.bfloat16),
        triple(forward),
        triple(inverse),
        twice(near),
        twice(same),
    )


def cmul(value, angle):
    re, im = value
    c, s = math.cos(angle), math.sin(angle)
    quarter = round(angle / (math.pi / 4), 9)
    if quarter == int(quarter):
        turn = int(quarter) % 8
        h = math.sqrt(0.5)
        return [
            lambda: (re, im),
            lambda: ((re - im) * h, (re + im) * h),
            lambda: (-im, re),
            lambda: (-(re + im) * h, (re - im) * h),
            lambda: (-re, -im),
            lambda: ((im - re) * h, -(re + im) * h),
            lambda: (im, -re),
            lambda: ((re + im) * h, (im - re) * h),
        ][turn]()
    return re * c - im * s, re * s + im * c


def cadd(a, b):
    return a[0] + b[0], a[1] + b[1]


def csub(a, b):
    return a[0] - b[0], a[1] - b[1]


def add_turned(a, b, sign):
    if sign > 0:
        return a[0] - b[1], a[1] + b[0]
    return a[0] + b[1], a[1] - b[0]


def dft4(x, sign):
    s0, d0 = cadd(x[0], x[2]), csub(x[0], x[2])
    s1, d1 = cadd(x[1], x[3]), csub(x[1], x[3])
    return [cadd(s0, s1), add_turned(d0, d1, sign), csub(s0, s1), add_turned(d0, d1, -sign)]


def dft8(x, sign):
    even = dft4(x[0::2], sign)
    odd = dft4(x[1::2], sign)
    out = [None] * 8
    h = math.sqrt(0.5)
    for k in range(4):
        if k == 2:
            out[2] = add_turned(even[2], odd[2], sign)
            out[6] = add_turned(even[2], odd[2], -sign)
            continue
        turned = odd[k] if k == 0 else cmul(odd[k], sign * k * math.pi / 4)
        out[k] = cadd(even[k], turned)
        out[k + 4] = csub(even[k], turned)
    return out


def row(ref_value, r):
    return ref_value[r * SUBS : (r + 1) * SUBS]


def pair_up(a, b):
    return jnp.concatenate([a, b], 0)


def split(x):
    high = x.astype(BF16)
    low = (x - high.astype(F32)).astype(BF16)
    return high, low


def root(x):
    return x * lax.rsqrt(jnp.maximum(x, TINY))


def dot(a, b):
    return jnp.dot(a, b, preferred_element_type=F32)


def row_masks(first, start, end):
    masks = []
    for r in range(EXT):
        here = first + (r - HALO)
        masks.append(jnp.where((here >= start) & (here < end), 1.0, 0.0).astype(F32))
    return masks


def added(*terms):
    total = None
    for term in terms:
        if term is not None:
            total = term if total is None else total + term
    return total


class Look:
    def __init__(self, first, start, end, own32, other, box_t, coherence, ml, part):
        self.masks = row_masks(first, start, end)
        self.own32, self.other, self.box_t = own32, other, box_t
        self.coherence, self.ml, self.part = coherence, ml, part
        sub = lax.broadcasted_iota(jnp.int32, (SUBS, LANES), 0)
        lane = lax.broadcasted_iota(jnp.int32, (SUBS, LANES), 1)
        self.low_half = lane < LANES // 2
        self.inner = jnp.where(
            self.low_half, jnp.where(sub > 0, 1.0, 0.0), jnp.where(sub < SUBS - 1, 1.0, 0.0)
        )

    def products(self, q):
        at = pl.ds(q * 16, 16)
        c_re2 = self.other(0, at).astype(F32)
        c_im2 = self.other(1, at).astype(F32)
        rows = []
        for half in range(2):
            m = self.masks[2 * q + half]
            one = pl.ds((2 * q + half) * SUBS, SUBS)
            a_re = self.own32[0, one, :] * m
            a_im = self.own32[1, one, :] * m
            c_re, c_im = row(c_re2, half), row(c_im2, half)
            rows.append(
                (
                    a_re * c_re + a_im * c_im,
                    a_im * c_re - a_re * c_im,
                    self.own32[2, one, :] * m,
                    (c_re * c_re + c_im * c_im) * m,
                )
            )
        return rows

    def boxed(self, y, place):
        both = row(y, place)
        side = both[:, LANES:]
        side = jnp.where(self.low_half, pltpu.roll(side, 1, 0), pltpu.roll(side, SUBS - 1, 0))
        return both[:, 0:LANES] + side * self.inner

    def put(self, r, re, im, p1, p2):
        self.ml[0, pl.ds(r * SUBS, SUBS), :] = re
        self.ml[1, pl.ds(r * SUBS, SUBS), :] = im
        size = root(re * re + im * im)
        down = lax.rsqrt(p1 * p2 + 1e-6 * BOX_RATIO * BOX_RATIO)
        self.coherence[r // 8, pl.ds(r % 8, SUBS, stride=8), :] = size * (down * self.masks[r + HALO])


EDGE_ROWS = (0, 1, ROWS - 2, ROWS - 1)


def multilook(look, box_in):
    kept = [[None, None] for _ in range(4)]

    def add_products(q):
        for fields in look.products(q):
            for f in range(4):
                kept[f].append(fields[f])

    add_products(1)
    two = [[None, kept[f][2], kept[f][2] + kept[f][3]] for f in range(4)]
    for g in range(ROWS // SUBS):
        for q in range(4):
            tile = 2 + g * 4 + q
            if tile < EXT // 2 - 1:
                add_products(tile)
            else:
                for f in range(4):
                    kept[f] += [None, None]
            for f in range(4):
                sums = []
                for half in range(2):
                    r = g * 8 + q * 2 + half
                    two[f].append(added(kept[f][r + 3], kept[f][r + 4]))
                    sums.append(added(kept[f][r], added(two[f][r + 1], two[f][r + 3])))
                high, low = split(pair_up(*sums))
                at = pl.ds(f * 64 + q * 16, 16)
                box_in[g % 2, at, 0:LANES] = high
                box_in[g % 2, at, LANES : 2 * LANES] = low
        y = yield box_in[g % 2], look.box_t
        for n in range(8):
            r = g * 8 + n
            fields = [look.boxed(y, f * 8 + n) for f in range(4)]
            if r in EDGE_ROWS:
                at = pl.ds(EDGE_ROWS.index(r) * SUBS, SUBS)
                look.ml[0, pl.ds(r * SUBS, SUBS), :] = fields[0]
                look.ml[1, pl.ds(r * SUBS, SUBS), :] = fields[1]
                look.part[0, at, :] = fields[2]
                look.part[1, at, :] = fields[3]
            else:
                look.put(r, *fields)


def add_halo(look, halo_in):
    before = look.products(0)
    after = look.products(EXT // 2 - 1)
    for f in range(4):
        for n, rows in enumerate(
            [(before[0][f] + before[1][f], before[1][f]), (after[0][f], after[0][f] + after[1][f])]
        ):
            high, low = split(pair_up(*rows))
            at = pl.ds(f * 32 + n * 16, 16)
            halo_in[at, 0:LANES] = high
            halo_in[at, LANES : 2 * LANES] = low
    y = yield halo_in[...], look.box_t
    for n, r in enumerate(EDGE_ROWS):
        at, here = pl.ds(n * SUBS, SUBS), pl.ds(r * SUBS, SUBS)
        held = [look.ml[0, here, :], look.ml[1, here, :], look.part[0, at, :], look.part[1, at, :]]
        look.put(r, *[held[f] + look.boxed(y, f * 4 + n) for f in range(4)])


def goldstein(first, start, end, tables, ml, filtered, mid, spec_in, mags, mag_in):
    forward_t, inverse_t, near_t, same_t = tables
    masks = row_masks(first, start, end)

    for b in range(8):
        x = [
            (ml[0, pl.ds((b + 8 * a) * SUBS, SUBS), :], ml[1, pl.ds((b + 8 * a) * SUBS, SUBS), :])
            for a in range(4)
        ]
        x = dft4(x, -1)
        for k1 in range(4):
            v = cmul(x[k1], -2 * math.pi * b * k1 / 32)
            mid[0, pl.ds((k1 * 8 + b) * SUBS, SUBS), :] = v[0]
            mid[1, pl.ds((k1 * 8 + b) * SUBS, SUBS), :] = v[1]

    def put_split(place, parts):
        for c in range(2):
            high, low = split(pair_up(parts[0][c], parts[1][c]))
            at = pl.ds(place * SUBS, 16)
            spec_in[at, c * LANES : (c + 1) * LANES] = high
            spec_in[at, (2 + c) * LANES : (3 + c) * LANES] = low

    for k1 in range(4):
        x = [
            (mid[0, pl.ds((k1 * 8 + b) * SUBS, SUBS), :], mid[1, pl.ds((k1 * 8 + b) * SUBS, SUBS), :])
            for b in range(8)
        ]
        x = dft8(x, -1)
        for k2 in range(0, 8, 2):
            put_split(k1 * 8 + k2, x[k2 : k2 + 2])

    both = spec_in[...]
    s = yield jnp.concatenate([both, both[:, 0 : 2 * LANES]], 1), forward_t
    for p in range(ROWS):
        at = pl.ds(p * SUBS, SUBS)
        re, im = row(s, p)[:, 0:LANES], row(s, p)[:, LANES:]
        mid[0, at, :] = re
        mid[1, at, :] = im
        mags[at, :] = root(re * re + im * im)

    def place(k):
        k = k % PATCH
        return (k % 4) * 8 + k // 4

    total = None
    for p in range(0, ROWS, 2):
        sums = []
        for k in (p // 8 + 4 * (p % 8), p // 8 + 4 * (p % 8 + 1)):
            sums.append(
                mags[pl.ds(place(k - 1) * SUBS, SUBS), :]
                + mags[pl.ds(place(k) * SUBS, SUBS), :]
                + mags[pl.ds(place(k + 1) * SUBS, SUBS), :]
            )
            total = sums[-1] if total is None else total + sums[-1]
        high, low = split(pair_up(*sums))
        mag_in[pl.ds(p * SUBS, 16), 0:LANES] = high
        mag_in[pl.ds(p * SUBS, 16), LANES:] = low
    high, low = split(pair_up(total, total))
    tile_sum = yield jnp.concatenate([high, low], 1), same_t
    tile_sum = tile_sum[0:SUBS]
    inv = (1.0 / 9.0) / (tile_sum * (1.0 / (3 * PATCH * PATCH)) + 1e-6 / (PATCH * PATCH))
    smooth = yield mag_in[...], near_t
    for p in range(0, ROWS, 2):
        parts = []
        for n in (p, p + 1):
            w = root(row(smooth, n) * inv)
            at = pl.ds(n * SUBS, SUBS)
            parts.append((mid[0, at, :] * w, mid[1, at, :] * w))
        put_split(p, parts)

    both = spec_in[...]
    s = yield jnp.concatenate([both, both[:, 0 : 2 * LANES]], 1), inverse_t
    for k1 in range(4):
        x = [
            (row(s, k1 * 8 + k2)[:, 0:LANES], row(s, k1 * 8 + k2)[:, LANES:])
            for k2 in range(8)
        ]
        x = dft8(x, 1)
        for b in range(8):
            v = cmul(x[b], 2 * math.pi * b * k1 / 32)
            at = pl.ds((k1 * 8 + b) * SUBS, SUBS)
            mid[0, at, :] = v[0]
            mid[1, at, :] = v[1]
    for b in range(8):
        x = [
            (mid[0, pl.ds((k1 * 8 + b) * SUBS, SUBS), :], mid[1, pl.ds((k1 * 8 + b) * SUBS, SUBS), :])
            for k1 in range(4)
        ]
        x = dft4(x, 1)
        for a in range(4):
            r = b + 8 * a
            filtered[0, a, pl.ds(b, SUBS, stride=8), :] = x[a][0] * masks[r + HALO]
            filtered[1, a, pl.ds(b, SUBS, stride=8), :] = x[a][1] * masks[r + HALO]


def place_of(turn):
    return turn + lax.div(turn, 2) * (5 - 2 * turn)


def together(parts):
    asked = [next(part) for part in parts]
    while asked:
        made = dot(jnp.concatenate([left for left, _ in asked], 0), asked[0][1][...])
        rows = made.shape[0] // len(parts)
        following = []
        for n, part in enumerate(parts):
            try:
                following.append(part.send(made[n * rows : (n + 1) * rows]))
            except StopIteration:
                pass
        asked = following


def compute_all(
    first, partner, valid, own32, other, tables, coherence, filtered, work, before_look, before_halo, after
):
    box_in, halo_in, ml, part, *rest = work
    box_t, *filter_t = tables
    turns = 4

    def look_of(rnd, i):
        which = partner[0, i, rnd]

        def image(c, at):
            return jnp.where(which == 0, other[rnd, 0, c, at, :], other[rnd, 1, c, at, :])

        return Look(
            first, valid[i, 0, rnd], valid[i, 1, rnd], own32.at[i], image, box_t, coherence.at[rnd, i],
            ml.at[rnd, i], part.at[rnd, i],
        )

    def look_turn(turn):
        before_look(turn)
        rnd = place_of(turn)
        together([multilook(look_of(rnd, i), box_in.at[i]) for i in range(2)])

    def halo_turn(turn):
        before_halo(turn)
        rnd = place_of(turn)
        together([add_halo(look_of(rnd, i), halo_in.at[i]) for i in range(2)])

    def filter_turn(turn):
        halo_turn(turn)
        rnd = place_of(turn)
        together(
            [
                goldstein(
                    first, valid[i, 0, rnd], valid[i, 1, rnd], filter_t, ml.at[rnd, i], filtered.at[rnd, i],
                    *[ref.at[i] for ref in rest],
                )
                for i in range(2)
            ]
        )
        after(turn)

    def step(n, carry):
        looks = (n < turns - 1) | (n == turns + 1)

        @pl.when(looks)
        def _():
            look_turn(jnp.minimum(n, turns - 1))

        @pl.when(jnp.logical_not(looks))
        def _():
            filter_turn(n - (turns - 1) - lax.div(n, turns + 1))

        return carry

    lax.fori_loop(0, 2 * turns, step, 0)


def work_shapes():
    return [
        pltpu.VMEM((2, 2, 256, 2 * LANES), BF16),
        pltpu.VMEM((2, 128, 2 * LANES), BF16),
        pltpu.VMEM((4, 2, 2, BODY, LANES), F32),
        pltpu.VMEM((4, 2, 2, 4 * SUBS, LANES), F32),
        pltpu.VMEM((2, 2, BODY, LANES), F32),
        pltpu.VMEM((2, BODY, 4 * LANES), BF16),
        pltpu.VMEM((2, BODY, LANES), F32),
        pltpu.VMEM((2, BODY, 2 * LANES), BF16),
    ]


def exchange_kernel(
    partner_hbm, valid_hbm, slc_hbm, box_h, forward_h, inverse_h, near_h, same_h,
    coherence_hbm, filtered_hbm,
    own32, other, coherence, filtered, box_t, forward_t, inverse_t, near_t, same_t,
    slc, own, lines, partner, valid, load_sem, out_sem,
    far_sem, halo_send, halo_recv, main_send, main_recv, edge_send, edge_recv, fwd_send, fwd_recv, *work,
):
    date = lax.axis_index("date")
    strip = lax.axis_index("strip")
    n_strip = lax.axis_size("strip")

    def xor(bits):
        target = date
        for bit in range(4):
            if bits >> bit & 1:
                size = 1 << bit
                target = target + size - 2 * size * lax.rem(lax.div(date, size), 2)
        return target

    mate, onward = xor(1), xor(6)
    partners = {0: mate, 1: xor(2), 2: xor(4), 3: xor(8)}
    has_above, has_below = strip > 0, strip < n_strip - 1
    far_upper, far_lower = strip == n_strip // 2 - 1, strip == n_strip // 2

    barrier = pltpu.get_barrier_semaphore()

    def greet(device):
        pl.semaphore_signal(barrier, inc=1, device_id=device, device_id_type=MESH)

    @pl.when(has_above & jnp.logical_not(far_lower))
    def _():
        greet((date, strip - 1))
        greet((mate, strip - 1))

    @pl.when(has_below)
    def _():
        greet((date, strip + 1))
        greet((mate, strip + 1))

    for device in (*partners.values(), onward):
        greet((device, strip))

    loads = []
    for n, (src, dst) in enumerate(
        [
            (slc_hbm, slc),
            (partner_hbm, partner),
            (valid_hbm, valid),
            (box_h, box_t),
            (forward_h, forward_t),
            (near_h, near_t),
            (same_h, same_t),
            (inverse_h, inverse_t),
        ]
    ):
        loads.append(pltpu.make_async_copy(src, dst, load_sem.at[n]))
        loads[-1].start()

    loads[0].wait()
    for i in range(2):
        for c in range(2):
            for g in range(4):
                for j in range(8):
                    lines[i * 2 + c, g, pl.ds(j * 8, 8), :] = slc[
                        i, c, pl.ds(g * 8, 8), pl.ds(j * LANES, LANES)
                    ].astype(F32)
            for g in range(4):
                for s in range(0, 8, 2):
                    pair = jnp.concatenate(
                        [
                            lines[i * 2 + c, g, pl.ds(s, 8, stride=8), :],
                            lines[i * 2 + c, g, pl.ds(s + 1, 8, stride=8), :],
                        ],
                        0,
                    )
                    own[i, c, pl.ds(EDGE + (g * 8 + s) * SUBS, 16), :] = pair.astype(BF16)

    top, bottom = pl.ds(0, EDGE), pl.ds(FULL - EDGE, EDGE)
    first_rows, last_rows = pl.ds(EDGE, EDGE), pl.ds(FULL - 2 * EDGE, EDGE)
    body = pl.ds(EDGE, BODY)
    blank = jnp.zeros((EDGE, LANES), BF16)

    @pl.when(jnp.logical_not(has_above))
    def _():
        for i in range(2):
            for c in range(2):
                own[i, c, top, :] = blank
                other[0, i, c, top, :] = blank

    @pl.when(jnp.logical_not(has_below))
    def _():
        for i in range(2):
            for c in range(2):
                own[i, c, bottom, :] = blank
                other[0, i, c, bottom, :] = blank

    def remote(src, dst, send_sem, recv_sem, device):
        return pltpu.make_async_remote_copy(
            src_ref=src, dst_ref=dst, send_sem=send_sem, recv_sem=recv_sem, device_id=device, device_id_type=MESH
        )

    up = [
        remote(own.at[:, :, first_rows], own.at[:, :, bottom], halo_send.at[0], halo_recv.at[0], (date, strip - 1)),
        remote(
            own.at[:, :, first_rows], other.at[0, :, :, bottom], halo_send.at[2], halo_recv.at[2], (mate, strip - 1)
        ),
    ]
    down = [
        remote(own.at[:, :, last_rows], own.at[:, :, top], halo_send.at[1], halo_recv.at[1], (date, strip + 1)),
        remote(own.at[:, :, last_rows], other.at[0, :, :, top], halo_send.at[3], halo_recv.at[3], (mate, strip + 1)),
    ]
    inside = has_above & has_below & jnp.logical_not(far_upper)

    @pl.when(inside)
    def _():
        pl.semaphore_wait(barrier, 9)

    @pl.when(jnp.logical_not(inside))
    def _():
        pl.semaphore_wait(barrier, 7)

    @pl.when(far_lower)
    def _():
        for device in (date, mate):
            pl.semaphore_signal(far_sem, inc=1, device_id=(device, strip - 1), device_id_type=MESH)

    @pl.when(has_above)
    def _():
        for copy in up:
            copy.start()

    @pl.when(has_below & jnp.logical_not(far_upper))
    def _():
        for copy in down:
            copy.start()

    mains = {}
    for i in range(2):
        for c in range(2):
            for n, r in enumerate((1, 3, 0)):
                mains[r, i, c] = remote(
                    own.at[i, c, body],
                    other.at[r, i, c, body],
                    main_send.at[n, i, c],
                    main_recv.at[n, i, c],
                    (partners[r], strip),
                )
                mains[r, i, c].start()

    def widen(i, q):
        at = pl.ds(q * 16, 16)
        re = own[i, 0, at, :].astype(F32)
        im = own[i, 1, at, :].astype(F32)
        own32[i, 0, at, :] = re
        own32[i, 1, at, :] = im
        own32[i, 2, at, :] = re * re + im * im

    for i in range(2):
        for q in range(1, EXT // 2 - 1):
            widen(i, q)

    forwards, edges = {}, {}
    for i in range(2):
        for c in range(2):
            forwards[i, c] = remote(
                other.at[1, i, c, body],
                other.at[2, i, c, body],
                fwd_send.at[i, c],
                fwd_recv.at[i, c],
                (onward, strip),
            )
    for n, r in enumerate((1, 2, 3)):
        for side, at in enumerate((top, bottom)):
            edges[r, side] = remote(
                own.at[:, :, at],
                other.at[r, :, :, at],
                edge_send.at[n, side],
                edge_recv.at[n, side],
                (partners[r], strip),
            )

    far = far_upper | far_lower

    def take_halo():
        @pl.when(has_below)
        def _():
            up[0].wait_recv()

        @pl.when(has_above)
        def _():
            down[0].wait_recv()

        for copy in edges.values():
            copy.start()
        for i in range(2):
            for q in (0, EXT // 2 - 1):
                widen(i, q)

    def send_far():
        pl.semaphore_wait(far_sem, 2)
        for copy in down:
            copy.start()

    def before_look(turn):
        @pl.when(turn == 0)
        def _():
            for i in range(2):
                for c in range(2):
                    mains[0, i, c].wait_recv()
            for copy in loads[1:]:
                copy.wait()

        @pl.when(turn == 1)
        def _():
            @pl.when(jnp.logical_not(far))
            def _():
                take_halo()

            for i in range(2):
                for c in range(2):
                    mains[1, i, c].wait_recv()
                    forwards[i, c].start()
                if i == 0:

                    @pl.when(far_upper)
                    def _():
                        send_far()

        @pl.when(turn == 2)
        def _():
            for i in range(2):
                for c in range(2):
                    mains[3, i, c].wait_recv()

        @pl.when(turn == 3)
        def _():
            for copy in forwards.values():
                copy.wait_recv()

    def before_halo(turn):
        @pl.when(turn == 0)
        def _():
            @pl.when(far)
            def _():
                take_halo()

            @pl.when(has_below)
            def _():
                up[1].wait_recv()

            @pl.when(has_above)
            def _():
                down[1].wait_recv()

        for n, r in ((1, 1), (2, 3), (3, 2)):

            @pl.when(turn == n)
            def _(r=r):
                edges[r, 0].wait_recv()
                edges[r, 1].wait_recv()

    def outputs(turn):
        rnd = place_of(turn)
        return [
            pltpu.make_async_copy(coherence.at[rnd], coherence_hbm.at[rnd], out_sem.at[0, turn]),
            pltpu.make_async_copy(filtered.at[rnd], filtered_hbm.at[rnd], out_sem.at[1, turn]),
        ]

    def after(turn):
        for copy in outputs(turn):
            copy.start()

    tables = (box_t, forward_t, inverse_t, near_t, same_t)
    compute_all(
        strip * ROWS, partner, valid, own32, other, tables, coherence, filtered, work, before_look, before_halo, after,
    )

    @pl.when(has_above)
    def _():
        for copy in up:
            copy.wait_send()

    @pl.when(has_below)
    def _():
        for copy in down:
            copy.wait_send()

    for copy in (*mains.values(), *edges.values(), *forwards.values()):
        copy.wait_send()
    for turn in range(4):
        for copy in outputs(jnp.int32(turn)):
            copy.wait()


def exchange(partner, valid, slc, tables):
    hbm = pl.BlockSpec(memory_space=pltpu.HBM)
    dma = pltpu.SemaphoreType.DMA
    return pl.pallas_call(
        exchange_kernel,
        out_shape=(
            jax.ShapeDtypeStruct((4, 2, 4, 64, LANES), F32),
            jax.ShapeDtypeStruct((4, 2, 2, 4, 64, LANES), F32),
        ),
        in_specs=[hbm] * 8,
        out_specs=(hbm, hbm),
        scratch_shapes=[
            pltpu.VMEM((2, 3, FULL, LANES), F32),
            pltpu.VMEM((4, 2, 2, FULL, LANES), BF16),
            pltpu.VMEM((4, 2, 4, 64, LANES), F32),
            pltpu.VMEM((4, 2, 2, 4, 64, LANES), F32),
        ]
        + [pltpu.VMEM(t.shape, t.dtype) for t in tables]
        + [
            pltpu.VMEM(slc.shape, BF16),
            pltpu.VMEM((2, 2, FULL, LANES), BF16),
            pltpu.VMEM((4, 4, 64, LANES), F32),
            pltpu.SMEM(partner.shape, jnp.int32),
            pltpu.SMEM(valid.shape, jnp.int32),
            dma((8,)),
            dma((2, 4)),
            pltpu.SemaphoreType.REGULAR,
            dma((4,)),
            dma((4,)),
            dma((3, 2, 2)),
            dma((3, 2, 2)),
            dma((3, 2)),
            dma((3, 2)),
            dma((2, 2)),
            dma((2, 2)),
        ]
        + work_shapes(),
        compiler_params=pltpu.CompilerParams(
            collective_id=0, has_side_effects=True, vmem_limit_bytes=60 * 1024 * 1024
        ),
        name="interferograms",
    )(partner, valid, slc, *tables)


def hand_on_kernel(done_coherence, done_filtered, coherence_hbm, filtered_hbm, coherence, filtered, in_sem, out_sem):
    ins, outs = [], []
    for rnd in range(4):
        for i in range(2):
            for n, (src, by, dst) in enumerate(
                [(done_filtered, filtered, filtered_hbm), (done_coherence, coherence, coherence_hbm)]
            ):
                ins.append(pltpu.make_async_copy(src.at[rnd, i], by.at[rnd, i], in_sem.at[n, rnd, i]))
                outs.append(pltpu.make_async_copy(by.at[rnd, i], dst.at[rnd, i], out_sem.at[n, rnd, i]))
    for copy in ins:
        copy.start()
    for copy_in, copy_out in zip(ins, outs):
        copy_in.wait()
        copy_out.start()
    for copy in outs:
        copy.wait()


def hand_on(coherence, filtered):
    hbm = pl.BlockSpec(memory_space=pltpu.HBM)
    dma = pltpu.SemaphoreType.DMA
    return pl.pallas_call(
        hand_on_kernel,
        out_shape=(
            jax.ShapeDtypeStruct(coherence.shape, F32),
            jax.ShapeDtypeStruct(filtered.shape, F32),
        ),
        in_specs=[hbm, hbm],
        out_specs=(hbm, hbm),
        scratch_shapes=[
            pltpu.VMEM(coherence.shape, F32),
            pltpu.VMEM(filtered.shape, F32),
            dma((2, 4, 2)),
            dma((2, 4, 2)),
        ],
        compiler_params=pltpu.CompilerParams(vmem_limit_bytes=60 * 1024 * 1024),
        name="hand_on",
    )(coherence, filtered)


def untile(array):
    lead = array.shape[:-3]
    array = array.reshape(lead + (4, 8, 8, LANES))
    n = len(lead)
    array = array.transpose(tuple(range(n)) + (n, n + 2, n + 1, n + 3))
    return array.reshape(lead + (ROWS, 8 * LANES))


def shards(slc, partner, valid):
    partner = partner.transpose(1, 2, 0)
    valid = valid.transpose(1, 2, 0)
    tables = [jnp.asarray(t) for t in make_tables()]
    coherence, filtered = hand_on(*exchange(partner, valid, slc, tables))
    return untile(coherence), untile(filtered)


def solution(mesh):
    in_specs = (P("date", None, "strip", None), P(None, "date", None), P(None, "date", None))
    out_specs = (P(None, "date", "strip", None), P(None, "date", None, "strip", None))
    return jax.shard_map(shards, mesh=mesh, in_specs=in_specs, out_specs=out_specs, check_vma=False)
```

```python
import functools
import math

import jax
import jax.numpy as jnp
import numpy as np
from jax import lax
from jax.experimental import pallas as pl
from jax.experimental.pallas import tpu as pltpu
from jax.sharding import PartitionSpec as P

F32 = jnp.float32
BF16 = jnp.bfloat16
MESH = pl.DeviceIdType.MESH

PATCH = 32
LOOK_A = 5
LOOK_R = 19
HALO = 2
LANES = 128
SUBS = 8
ROWS = 32
EXT = ROWS + 2 * HALO
EDGE = HALO * SUBS
BODY = ROWS * SUBS
FULL = EXT * SUBS
TINY = 1.2e-38

BOX_SCALE = 1.0 / 128.0
BOX_RATIO = LOOK_A * LOOK_R / 128.0


def split_np(table):
    high = table.astype(np.float32).astype(jnp.bfloat16)
    low = (table - high.astype(np.float64)).astype(np.float32).astype(jnp.bfloat16)
    return high, low


def make_tables():
    lane = np.arange(LANES)
    reach = LOOK_R // 2
    centre = np.abs(lane[:, None] - lane[None, :]) <= reach
    to_next = np.abs(lane[None, :] + LANES - lane[:, None]) <= reach
    to_previous = np.abs(lane[None, :] - LANES - lane[:, None]) <= reach
    box = np.concatenate([centre, to_next | to_previous], 1) * BOX_SCALE
    box = np.concatenate([box, box], 0)

    same = lane[:, None] // PATCH == lane[None, :] // PATCH
    angle = (lane[:, None] % PATCH) * (lane[None, :] % PATCH) % PATCH * (2 * math.pi / PATCH)
    cos = np.where(same, np.cos(angle), 0.0)
    sin = np.where(same, np.sin(angle), 0.0)
    forward = np.block([[cos, -sin], [sin, cos]]) / (BOX_RATIO * PATCH * PATCH)
    inverse = np.block([[cos, sin], [-sin, cos]])
    apart = (lane[:, None] - lane[None, :]) % PATCH
    near = same & ((apart <= 1) | (apart == PATCH - 1))

    def triple(table):
        high, low = split_np(table)
        return np.concatenate([high, high, low], 0)

    def twice(table):
        return np.concatenate([table, table], 0).astype(np.float32).astype(jnp.bfloat16)

    return (
        box.astype(np.float32).astype(jnp.bfloat16),
        triple(forward),
        triple(inverse),
        twice(near),
        twice(same),
    )


def cmul(value, angle):
    re, im = value
    c, s = math.cos(angle), math.sin(angle)
    quarter = round(angle / (math.pi / 4), 9)
    if quarter == int(quarter):
        turn = int(quarter) % 8
        h = math.sqrt(0.5)
        return [
            lambda: (re, im),
            lambda: ((re - im) * h, (re + im) * h),
            lambda: (-im, re),
            lambda: (-(re + im) * h, (re - im) * h),
            lambda: (-re, -im),
            lambda: ((im - re) * h, -(re + im) * h),
            lambda: (im, -re),
            lambda: ((re + im) * h, (im - re) * h),
        ][turn]()
    return re * c - im * s, re * s + im * c


def cadd(a, b):
    return a[0] + b[0], a[1] + b[1]


def csub(a, b):
    return a[0] - b[0], a[1] - b[1]


def add_turned(a, b, sign):
    if sign > 0:
        return a[0] - b[1], a[1] + b[0]
    return a[0] + b[1], a[1] - b[0]


def dft4(x, sign):
    s0, d0 = cadd(x[0], x[2]), csub(x[0], x[2])
    s1, d1 = cadd(x[1], x[3]), csub(x[1], x[3])
    return [cadd(s0, s1), add_turned(d0, d1, sign), csub(s0, s1), add_turned(d0, d1, -sign)]


def dft8(x, sign):
    even = dft4(x[0::2], sign)
    odd = dft4(x[1::2], sign)
    out = [None] * 8
    h = math.sqrt(0.5)
    for k in range(4):
        if k == 2:
            out[2] = add_turned(even[2], odd[2], sign)
            out[6] = add_turned(even[2], odd[2], -sign)
            continue
        turned = odd[k] if k == 0 else cmul(odd[k], sign * k * math.pi / 4)
        out[k] = cadd(even[k], turned)
        out[k + 4] = csub(even[k], turned)
    return out


def row(ref_value, r):
    return ref_value[r * SUBS : (r + 1) * SUBS]


def pair_up(a, b):
    return jnp.concatenate([a, b], 0)


def split(x):
    high = x.astype(BF16)
    low = (x - high.astype(F32)).astype(BF16)
    return high, low


def root(x):
    return x * lax.rsqrt(jnp.maximum(x, TINY))


def dot(a, b):
    return jnp.dot(a, b, preferred_element_type=F32)


def row_masks(first, start, end):
    masks = []
    for r in range(EXT):
        here = first + (r - HALO)
        masks.append(jnp.where((here >= start) & (here < end), 1.0, 0.0).astype(F32))
    return masks


def added(*terms):
    total = None
    for term in terms:
        if term is not None:
            total = term if total is None else total + term
    return total


class Look:
    def __init__(self, first, start, end, own32, other, box_t, coherence, ml, part):
        self.masks = row_masks(first, start, end)
        self.own32, self.other, self.box_t = own32, other, box_t
        self.coherence, self.ml, self.part = coherence, ml, part
        sub = lax.broadcasted_iota(jnp.int32, (SUBS, LANES), 0)
        lane = lax.broadcasted_iota(jnp.int32, (SUBS, LANES), 1)
        self.low_half = lane < LANES // 2
        self.inner = jnp.where(
            self.low_half, jnp.where(sub > 0, 1.0, 0.0), jnp.where(sub < SUBS - 1, 1.0, 0.0)
        )

    def products(self, q):
        at = pl.ds(q * 16, 16)
        c_re2 = self.other(0, at).astype(F32)
        c_im2 = self.other(1, at).astype(F32)
        rows = []
        for half in range(2):
            m = self.masks[2 * q + half]
            one = pl.ds((2 * q + half) * SUBS, SUBS)
            a_re = self.own32[0, one, :] * m
            a_im = self.own32[1, one, :] * m
            c_re, c_im = row(c_re2, half), row(c_im2, half)
            rows.append(
                (
                    a_re * c_re + a_im * c_im,
                    a_im * c_re - a_re * c_im,
                    self.own32[2, one, :] * m,
                    (c_re * c_re + c_im * c_im) * m,
                )
            )
        return rows

    def boxed(self, y, place):
        both = row(y, place)
        side = both[:, LANES:]
        side = jnp.where(self.low_half, pltpu.roll(side, 1, 0), pltpu.roll(side, SUBS - 1, 0))
        return both[:, 0:LANES] + side * self.inner

    def put(self, r, re, im, p1, p2):
        self.ml[0, pl.ds(r * SUBS, SUBS), :] = re
        self.ml[1, pl.ds(r * SUBS, SUBS), :] = im
        size = root(re * re + im * im)
        down = lax.rsqrt(p1 * p2 + 1e-6 * BOX_RATIO * BOX_RATIO)
        self.coherence[r // 8, pl.ds(r % 8, SUBS, stride=8), :] = size * (down * self.masks[r + HALO])


EDGE_ROWS = (0, 1, ROWS - 2, ROWS - 1)


def multilook(look, box_in):
    kept = [[None, None] for _ in range(4)]

    def add_products(q):
        for fields in look.products(q):
            for f in range(4):
                kept[f].append(fields[f])

    add_products(1)
    two = [[None, kept[f][2], kept[f][2] + kept[f][3]] for f in range(4)]
    for g in range(ROWS // SUBS):
        for q in range(4):
            tile = 2 + g * 4 + q
            if tile < EXT // 2 - 1:
                add_products(tile)
            else:
                for f in range(4):
                    kept[f] += [None, None]
            for f in range(4):
                sums = []
                for half in range(2):
                    r = g * 8 + q * 2 + half
                    two[f].append(added(kept[f][r + 3], kept[f][r + 4]))
                    sums.append(added(kept[f][r], added(two[f][r + 1], two[f][r + 3])))
                high, low = split(pair_up(*sums))
                at = pl.ds(f * 64 + q * 16, 16)
                box_in[g % 2, at, 0:LANES] = high
                box_in[g % 2, at, LANES : 2 * LANES] = low
        y = yield box_in[g % 2], look.box_t
        for n in range(8):
            r = g * 8 + n
            fields = [look.boxed(y, f * 8 + n) for f in range(4)]
            if r in EDGE_ROWS:
                at = pl.ds(EDGE_ROWS.index(r) * SUBS, SUBS)
                look.ml[0, pl.ds(r * SUBS, SUBS), :] = fields[0]
                look.ml[1, pl.ds(r * SUBS, SUBS), :] = fields[1]
                look.part[0, at, :] = fields[2]
                look.part[1, at, :] = fields[3]
            else:
                look.put(r, *fields)


def add_halo(look, halo_in):
    before = look.products(0)
    after = look.products(EXT // 2 - 1)
    for f in range(4):
        for n, rows in enumerate(
            [(before[0][f] + before[1][f], before[1][f]), (after[0][f], after[0][f] + after[1][f])]
        ):
            high, low = split(pair_up(*rows))
            at = pl.ds(f * 32 + n * 16, 16)
            halo_in[at, 0:LANES] = high
            halo_in[at, LANES : 2 * LANES] = low
    y = yield halo_in[...], look.box_t
    for n, r in enumerate(EDGE_ROWS):
        at, here = pl.ds(n * SUBS, SUBS), pl.ds(r * SUBS, SUBS)
        held = [look.ml[0, here, :], look.ml[1, here, :], look.part[0, at, :], look.part[1, at, :]]
        look.put(r, *[held[f] + look.boxed(y, f * 4 + n) for f in range(4)])


def goldstein(first, start, end, tables, ml, filtered, mid, spec_in, mags, mag_in):
    forward_t, inverse_t, near_t, same_t = tables
    masks = row_masks(first, start, end)

    for b in range(8):
        x = [
            (ml[0, pl.ds((b + 8 * a) * SUBS, SUBS), :], ml[1, pl.ds((b + 8 * a) * SUBS, SUBS), :])
            for a in range(4)
        ]
        x = dft4(x, -1)
        for k1 in range(4):
            v = cmul(x[k1], -2 * math.pi * b * k1 / 32)
            mid[0, pl.ds((k1 * 8 + b) * SUBS, SUBS), :] = v[0]
            mid[1, pl.ds((k1 * 8 + b) * SUBS, SUBS), :] = v[1]

    def put_split(place, parts):
        for c in range(2):
            high, low = split(pair_up(parts[0][c], parts[1][c]))
            at = pl.ds(place * SUBS, 16)
            spec_in[at, c * LANES : (c + 1) * LANES] = high
            spec_in[at, (2 + c) * LANES : (3 + c) * LANES] = low

    for k1 in range(4):
        x = [
            (mid[0, pl.ds((k1 * 8 + b) * SUBS, SUBS), :], mid[1, pl.ds((k1 * 8 + b) * SUBS, SUBS), :])
            for b in range(8)
        ]
        x = dft8(x, -1)
        for k2 in range(0, 8, 2):
            put_split(k1 * 8 + k2, x[k2 : k2 + 2])

    both = spec_in[...]
    s = yield jnp.concatenate([both, both[:, 0 : 2 * LANES]], 1), forward_t
    for p in range(ROWS):
        at = pl.ds(p * SUBS, SUBS)
        re, im = row(s, p)[:, 0:LANES], row(s, p)[:, LANES:]
        mid[0, at, :] = re
        mid[1, at, :] = im
        mags[at, :] = root(re * re + im * im)

    def place(k):
        k = k % PATCH
        return (k % 4) * 8 + k // 4

    total = None
    for p in range(0, ROWS, 2):
        sums = []
        for k in (p // 8 + 4 * (p % 8), p // 8 + 4 * (p % 8 + 1)):
            sums.append(
                mags[pl.ds(place(k - 1) * SUBS, SUBS), :]
                + mags[pl.ds(place(k) * SUBS, SUBS), :]
                + mags[pl.ds(place(k + 1) * SUBS, SUBS), :]
            )
            total = sums[-1] if total is None else total + sums[-1]
        high, low = split(pair_up(*sums))
        mag_in[pl.ds(p * SUBS, 16), 0:LANES] = high
        mag_in[pl.ds(p * SUBS, 16), LANES:] = low
    high, low = split(pair_up(total, total))
    tile_sum = yield jnp.concatenate([high, low], 1), same_t
    tile_sum = tile_sum[0:SUBS]
    inv = (1.0 / 9.0) / (tile_sum * (1.0 / (3 * PATCH * PATCH)) + 1e-6 / (PATCH * PATCH))
    smooth = yield mag_in[...], near_t
    for p in range(0, ROWS, 2):
        parts = []
        for n in (p, p + 1):
            w = root(row(smooth, n) * inv)
            at = pl.ds(n * SUBS, SUBS)
            parts.append((mid[0, at, :] * w, mid[1, at, :] * w))
        put_split(p, parts)

    both = spec_in[...]
    s = yield jnp.concatenate([both, both[:, 0 : 2 * LANES]], 1), inverse_t
    for k1 in range(4):
        x = [
            (row(s, k1 * 8 + k2)[:, 0:LANES], row(s, k1 * 8 + k2)[:, LANES:])
            for k2 in range(8)
        ]
        x = dft8(x, 1)
        for b in range(8):
            v = cmul(x[b], 2 * math.pi * b * k1 / 32)
            at = pl.ds((k1 * 8 + b) * SUBS, SUBS)
            mid[0, at, :] = v[0]
            mid[1, at, :] = v[1]
    for b in range(8):
        x = [
            (mid[0, pl.ds((k1 * 8 + b) * SUBS, SUBS), :], mid[1, pl.ds((k1 * 8 + b) * SUBS, SUBS), :])
            for k1 in range(4)
        ]
        x = dft4(x, 1)
        for a in range(4):
            r = b + 8 * a
            filtered[0, a, pl.ds(b, SUBS, stride=8), :] = x[a][0] * masks[r + HALO]
            filtered[1, a, pl.ds(b, SUBS, stride=8), :] = x[a][1] * masks[r + HALO]


def place_of(turn):
    return turn + lax.div(turn, 2) * (5 - 2 * turn)


def together(parts):
    asked = [next(part) for part in parts]
    while asked:
        made = dot(jnp.concatenate([left for left, _ in asked], 0), asked[0][1][...])
        rows = made.shape[0] // len(parts)
        following = []
        for n, part in enumerate(parts):
            try:
                following.append(part.send(made[n * rows : (n + 1) * rows]))
            except StopIteration:
                pass
        asked = following


def compute_all(
    first, partner, valid, own32, other, tables, coherence, filtered, work, before_look, before_halo, after
):
    box_in, halo_in, ml, part, *rest = work
    box_t, *filter_t = tables
    turns = 4

    def look_of(rnd, i):
        which = partner[0, i, rnd]

        def image(c, at):
            return jnp.where(which == 0, other[rnd, 0, c, at, :], other[rnd, 1, c, at, :])

        return Look(
            first, valid[i, 0, rnd], valid[i, 1, rnd], own32.at[i], image, box_t, coherence.at[rnd, i],
            ml.at[rnd, i], part.at[rnd, i],
        )

    def look_turn(turn):
        before_look(turn)
        rnd = place_of(turn)
        together([multilook(look_of(rnd, i), box_in.at[i]) for i in range(2)])

    def halo_turn(turn):
        before_halo(turn)
        rnd = place_of(turn)
        together([add_halo(look_of(rnd, i), halo_in.at[i]) for i in range(2)])

    def filter_turn(turn):
        halo_turn(turn)
        rnd = place_of(turn)
        together(
            [
                goldstein(
                    first, valid[i, 0, rnd], valid[i, 1, rnd], filter_t, ml.at[rnd, i], filtered.at[rnd, i],
                    *[ref.at[i] for ref in rest],
                )
                for i in range(2)
            ]
        )
        after(turn)

    def step(n, carry):
        looks = (n < turns - 1) | (n == turns)

        @pl.when(looks)
        def _():
            look_turn(jnp.minimum(n, turns - 1))

        @pl.when(jnp.logical_not(looks))
        def _():
            filter_turn(n - (turns - 1) - lax.div(n, turns + 1))

        return carry

    lax.fori_loop(0, 2 * turns, step, 0)


def work_shapes():
    return [
        pltpu.VMEM((2, 2, 256, 2 * LANES), BF16),
        pltpu.VMEM((2, 128, 2 * LANES), BF16),
        pltpu.VMEM((4, 2, 2, BODY, LANES), F32),
        pltpu.VMEM((4, 2, 2, 4 * SUBS, LANES), F32),
        pltpu.VMEM((2, 2, BODY, LANES), F32),
        pltpu.VMEM((2, BODY, 4 * LANES), BF16),
        pltpu.VMEM((2, BODY, LANES), F32),
        pltpu.VMEM((2, BODY, 2 * LANES), BF16),
    ]


def exchange_kernel(
    partner_hbm, valid_hbm, slc_hbm, box_h, forward_h, inverse_h, near_h, same_h,
    coherence_hbm, filtered_hbm,
    own32, other, coherence, filtered, box_t, forward_t, inverse_t, near_t, same_t,
    slc, own, lines, partner, valid, load_sem, out_sem,
    far_sem, halo_send, halo_recv, main_send, main_recv, edge_send, edge_recv, fwd_send, fwd_recv, *work,
):
    date = lax.axis_index("date")
    strip = lax.axis_index("strip")
    n_strip = lax.axis_size("strip")

    def xor(bits):
        target = date
        for bit in range(4):
            if bits >> bit & 1:
                size = 1 << bit
                target = target + size - 2 * size * lax.rem(lax.div(date, size), 2)
        return target

    mate, onward = xor(1), xor(6)
    partners = {0: mate, 1: xor(2), 2: xor(4), 3: xor(8)}
    has_above, has_below = strip > 0, strip < n_strip - 1
    far_upper, far_lower = strip == n_strip // 2 - 1, strip == n_strip // 2

    barrier = pltpu.get_barrier_semaphore()

    def greet(device):
        pl.semaphore_signal(barrier, inc=1, device_id=device, device_id_type=MESH)

    @pl.when(has_above & jnp.logical_not(far_lower))
    def _():
        greet((date, strip - 1))
        greet((mate, strip - 1))

    @pl.when(has_below)
    def _():
        greet((date, strip + 1))
        greet((mate, strip + 1))

    for device in (*partners.values(), onward):
        greet((device, strip))

    loads = []
    for n, (src, dst) in enumerate(
        [
            (slc_hbm, slc),
            (partner_hbm, partner),
            (valid_hbm, valid),
            (box_h, box_t),
            (forward_h, forward_t),
            (near_h, near_t),
            (same_h, same_t),
            (inverse_h, inverse_t),
        ]
    ):
        loads.append(pltpu.make_async_copy(src, dst, load_sem.at[n]))
        loads[-1].start()

    loads[0].wait()
    for i in range(2):
        for c in range(2):
            for g in range(4):
                for j in range(8):
                    lines[i * 2 + c, g, pl.ds(j * 8, 8), :] = slc[
                        i, c, pl.ds(g * 8, 8), pl.ds(j * LANES, LANES)
                    ].astype(F32)
            for g in range(4):
                for s in range(0, 8, 2):
                    pair = jnp.concatenate(
                        [
                            lines[i * 2 + c, g, pl.ds(s, 8, stride=8), :],
                            lines[i * 2 + c, g, pl.ds(s + 1, 8, stride=8), :],
                        ],
                        0,
                    )
                    own[i, c, pl.ds(EDGE + (g * 8 + s) * SUBS, 16), :] = pair.astype(BF16)

    top, bottom = pl.ds(0, EDGE), pl.ds(FULL - EDGE, EDGE)
    first_rows, last_rows = pl.ds(EDGE, EDGE), pl.ds(FULL - 2 * EDGE, EDGE)
    body = pl.ds(EDGE, BODY)
    blank = jnp.zeros((EDGE, LANES), BF16)

    @pl.when(jnp.logical_not(has_above))
    def _():
        for i in range(2):
            for c in range(2):
                own[i, c, top, :] = blank
                other[0, i, c, top, :] = blank

    @pl.when(jnp.logical_not(has_below))
    def _():
        for i in range(2):
            for c in range(2):
                own[i, c, bottom, :] = blank
                other[0, i, c, bottom, :] = blank

    def remote(src, dst, send_sem, recv_sem, device):
        return pltpu.make_async_remote_copy(
            src_ref=src, dst_ref=dst, send_sem=send_sem, recv_sem=recv_sem, device_id=device, device_id_type=MESH
        )

    up = [
        remote(own.at[:, :, first_rows], own.at[:, :, bottom], halo_send.at[0], halo_recv.at[0], (date, strip - 1)),
        remote(
            own.at[:, :, first_rows], other.at[0, :, :, bottom], halo_send.at[2], halo_recv.at[2], (mate, strip - 1)
        ),
    ]
    down = [
        remote(own.at[:, :, last_rows], own.at[:, :, top], halo_send.at[1], halo_recv.at[1], (date, strip + 1)),
        remote(own.at[:, :, last_rows], other.at[0, :, :, top], halo_send.at[3], halo_recv.at[3], (mate, strip + 1)),
    ]
    inside = has_above & has_below & jnp.logical_not(far_upper)

    @pl.when(inside)
    def _():
        pl.semaphore_wait(barrier, 9)

    @pl.when(jnp.logical_not(inside))
    def _():
        pl.semaphore_wait(barrier, 7)

    @pl.when(far_lower)
    def _():
        for device in (date, mate):
            pl.semaphore_signal(far_sem, inc=1, device_id=(device, strip - 1), device_id_type=MESH)

    @pl.when(has_above)
    def _():
        for copy in up:
            copy.start()

    @pl.when(has_below & jnp.logical_not(far_upper))
    def _():
        for copy in down:
            copy.start()

    mains = {}
    for n, r in enumerate((1, 3, 0)):
        for i in range(2):
            for c in range(2):
                mains[r, i, c] = remote(
                    own.at[i, c, body],
                    other.at[r, i, c, body],
                    main_send.at[n, i, c],
                    main_recv.at[n, i, c],
                    (partners[r], strip),
                )
                mains[r, i, c].start()

    def widen(i, q):
        at = pl.ds(q * 16, 16)
        re = own[i, 0, at, :].astype(F32)
        im = own[i, 1, at, :].astype(F32)
        own32[i, 0, at, :] = re
        own32[i, 1, at, :] = im
        own32[i, 2, at, :] = re * re + im * im

    for i in range(2):
        for q in range(1, EXT // 2 - 1):
            widen(i, q)

    forwards, edges = {}, {}
    for i in range(2):
        for c in range(2):
            forwards[i, c] = remote(
                other.at[1, i, c, body],
                other.at[2, i, c, body],
                fwd_send.at[i, c],
                fwd_recv.at[i, c],
                (onward, strip),
            )
    for n, r in enumerate((1, 2, 3)):
        for side, at in enumerate((top, bottom)):
            edges[r, side] = remote(
                own.at[:, :, at],
                other.at[r, :, :, at],
                edge_send.at[n, side],
                edge_recv.at[n, side],
                (partners[r], strip),
            )

    far = far_upper | far_lower

    def take_halo():
        @pl.when(has_below)
        def _():
            up[0].wait_recv()

        @pl.when(has_above)
        def _():
            down[0].wait_recv()

        for copy in edges.values():
            copy.start()
        for i in range(2):
            for q in (0, EXT // 2 - 1):
                widen(i, q)

    def send_far():
        pl.semaphore_wait(far_sem, 2)
        for copy in down:
            copy.start()

    def before_look(turn):
        @pl.when(turn == 0)
        def _():
            for i in range(2):
                for c in range(2):
                    mains[0, i, c].wait_recv()
            for copy in loads[1:]:
                copy.wait()

        @pl.when(turn == 1)
        def _():
            @pl.when(jnp.logical_not(far))
            def _():
                take_halo()

            for i in range(2):
                for c in range(2):
                    mains[1, i, c].wait_recv()
                    forwards[i, c].start()
                if i == 0:

                    @pl.when(far_upper)
                    def _():
                        send_far()

        @pl.when(turn == 2)
        def _():
            for i in range(2):
                for c in range(2):
                    mains[3, i, c].wait_recv()

        @pl.when(turn == 3)
        def _():
            for copy in forwards.values():
                copy.wait_recv()

    def before_halo(turn):
        @pl.when(turn == 0)
        def _():
            @pl.when(far)
            def _():
                take_halo()

            @pl.when(has_below)
            def _():
                up[1].wait_recv()

            @pl.when(has_above)
            def _():
                down[1].wait_recv()

        for n, r in ((1, 1), (2, 3), (3, 2)):

            @pl.when(turn == n)
            def _(r=r):
                edges[r, 0].wait_recv()
                edges[r, 1].wait_recv()

    def outputs(turn):
        rnd = place_of(turn)
        return [
            pltpu.make_async_copy(coherence.at[rnd], coherence_hbm.at[rnd], out_sem.at[0, turn]),
            pltpu.make_async_copy(filtered.at[rnd], filtered_hbm.at[rnd], out_sem.at[1, turn]),
        ]

    def after(turn):
        for copy in outputs(turn):
            copy.start()

    tables = (box_t, forward_t, inverse_t, near_t, same_t)
    compute_all(
        strip * ROWS, partner, valid, own32, other, tables, coherence, filtered, work, before_look, before_halo, after,
    )

    @pl.when(has_above)
    def _():
        for copy in up:
            copy.wait_send()

    @pl.when(has_below)
    def _():
        for copy in down:
            copy.wait_send()

    for copy in (*mains.values(), *edges.values(), *forwards.values()):
        copy.wait_send()
    for turn in range(4):
        for copy in outputs(jnp.int32(turn)):
            copy.wait()


def exchange(partner, valid, slc, tables):
    hbm = pl.BlockSpec(memory_space=pltpu.HBM)
    dma = pltpu.SemaphoreType.DMA
    return pl.pallas_call(
        exchange_kernel,
        out_shape=(
            jax.ShapeDtypeStruct((4, 2, 4, 64, LANES), F32),
            jax.ShapeDtypeStruct((4, 2, 2, 4, 64, LANES), F32),
        ),
        in_specs=[hbm] * 8,
        out_specs=(hbm, hbm),
        scratch_shapes=[
            pltpu.VMEM((2, 3, FULL, LANES), F32),
            pltpu.VMEM((4, 2, 2, FULL, LANES), BF16),
            pltpu.VMEM((4, 2, 4, 64, LANES), F32),
            pltpu.VMEM((4, 2, 2, 4, 64, LANES), F32),
        ]
        + [pltpu.VMEM(t.shape, t.dtype) for t in tables]
        + [
            pltpu.VMEM(slc.shape, BF16),
            pltpu.VMEM((2, 2, FULL, LANES), BF16),
            pltpu.VMEM((4, 4, 64, LANES), F32),
            pltpu.SMEM(partner.shape, jnp.int32),
            pltpu.SMEM(valid.shape, jnp.int32),
            dma((8,)),
            dma((2, 4)),
            pltpu.SemaphoreType.REGULAR,
            dma((4,)),
            dma((4,)),
            dma((3, 2, 2)),
            dma((3, 2, 2)),
            dma((3, 2)),
            dma((3, 2)),
            dma((2, 2)),
            dma((2, 2)),
        ]
        + work_shapes(),
        compiler_params=pltpu.CompilerParams(
            collective_id=0, has_side_effects=True, vmem_limit_bytes=60 * 1024 * 1024
        ),
        name="interferograms",
    )(partner, valid, slc, *tables)


def hand_on_kernel(done_coherence, done_filtered, coherence_hbm, filtered_hbm, coherence, filtered, in_sem, out_sem):
    ins, outs = [], []
    for rnd in range(4):
        for i in range(2):
            for n, (src, by, dst) in enumerate(
                [(done_filtered, filtered, filtered_hbm), (done_coherence, coherence, coherence_hbm)]
            ):
                ins.append(pltpu.make_async_copy(src.at[rnd, i], by.at[rnd, i], in_sem.at[n, rnd, i]))
                outs.append(pltpu.make_async_copy(by.at[rnd, i], dst.at[rnd, i], out_sem.at[n, rnd, i]))
    for copy in ins:
        copy.start()
    for copy_in, copy_out in zip(ins, outs):
        copy_in.wait()
        copy_out.start()
    for copy in outs:
        copy.wait()


def hand_on(coherence, filtered):
    hbm = pl.BlockSpec(memory_space=pltpu.HBM)
    dma = pltpu.SemaphoreType.DMA
    return pl.pallas_call(
        hand_on_kernel,
        out_shape=(
            jax.ShapeDtypeStruct(coherence.shape, F32),
            jax.ShapeDtypeStruct(filtered.shape, F32),
        ),
        in_specs=[hbm, hbm],
        out_specs=(hbm, hbm),
        scratch_shapes=[
            pltpu.VMEM(coherence.shape, F32),
            pltpu.VMEM(filtered.shape, F32),
            dma((2, 4, 2)),
            dma((2, 4, 2)),
        ],
        compiler_params=pltpu.CompilerParams(vmem_limit_bytes=60 * 1024 * 1024),
        name="hand_on",
    )(coherence, filtered)


def untile(array):
    lead = array.shape[:-3]
    array = array.reshape(lead + (4, 8, 8, LANES))
    n = len(lead)
    array = array.transpose(tuple(range(n)) + (n, n + 2, n + 1, n + 3))
    return array.reshape(lead + (ROWS, 8 * LANES))


def shards(slc, partner, valid):
    partner = partner.transpose(1, 2, 0)
    valid = valid.transpose(1, 2, 0)
    tables = [jnp.asarray(t) for t in make_tables()]
    coherence, filtered = hand_on(*exchange(partner, valid, slc, tables))
    return untile(coherence), untile(filtered)


def solution(mesh):
    in_specs = (P("date", None, "strip", None), P(None, "date", None), P(None, "date", None))
    out_specs = (P(None, "date", "strip", None), P(None, "date", None, "strip", None))
    return jax.shard_map(shards, mesh=mesh, in_specs=in_specs, out_specs=out_specs, check_vma=False)
```

```python
import functools
import math

import jax
import jax.numpy as jnp
import numpy as np
from jax import lax
from jax.experimental import pallas as pl
from jax.experimental.pallas import tpu as pltpu
from jax.sharding import PartitionSpec as P

F32 = jnp.float32
BF16 = jnp.bfloat16
MESH = pl.DeviceIdType.MESH

PATCH = 32
LOOK_A = 5
LOOK_R = 19
HALO = 2
LANES = 128
SUBS = 8
ROWS = 32
EXT = ROWS + 2 * HALO
EDGE = HALO * SUBS
BODY = ROWS * SUBS
FULL = EXT * SUBS
TINY = 1.2e-38

BOX_SCALE = 1.0 / 128.0
BOX_RATIO = LOOK_A * LOOK_R / 128.0


def split_np(table):
    high = table.astype(np.float32).astype(jnp.bfloat16)
    low = (table - high.astype(np.float64)).astype(np.float32).astype(jnp.bfloat16)
    return high, low


def make_tables():
    lane = np.arange(LANES)
    reach = LOOK_R // 2
    centre = np.abs(lane[:, None] - lane[None, :]) <= reach
    to_next = np.abs(lane[None, :] + LANES - lane[:, None]) <= reach
    to_previous = np.abs(lane[None, :] - LANES - lane[:, None]) <= reach
    box = np.concatenate([centre, to_next | to_previous], 1) * BOX_SCALE
    box = np.concatenate([box, box], 0)

    same = lane[:, None] // PATCH == lane[None, :] // PATCH
    angle = (lane[:, None] % PATCH) * (lane[None, :] % PATCH) % PATCH * (2 * math.pi / PATCH)
    cos = np.where(same, np.cos(angle), 0.0)
    sin = np.where(same, np.sin(angle), 0.0)
    forward = np.block([[cos, -sin], [sin, cos]]) / (BOX_RATIO * PATCH * PATCH)
    inverse = np.block([[cos, sin], [-sin, cos]])
    apart = (lane[:, None] - lane[None, :]) % PATCH
    near = same & ((apart <= 1) | (apart == PATCH - 1))

    def triple(table):
        high, low = split_np(table)
        return np.concatenate([high, high, low], 0)

    def twice(table):
        return np.concatenate([table, table], 0).astype(np.float32).astype(jnp.bfloat16)

    return (
        box.astype(np.float32).astype(jnp.bfloat16),
        triple(forward),
        triple(inverse),
        twice(near),
        twice(same),
    )


def cmul(value, angle):
    re, im = value
    c, s = math.cos(angle), math.sin(angle)
    quarter = round(angle / (math.pi / 4), 9)
    if quarter == int(quarter):
        turn = int(quarter) % 8
        h = math.sqrt(0.5)
        return [
            lambda: (re, im),
            lambda: ((re - im) * h, (re + im) * h),
            lambda: (-im, re),
            lambda: (-(re + im) * h, (re - im) * h),
            lambda: (-re, -im),
            lambda: ((im - re) * h, -(re + im) * h),
            lambda: (im, -re),
            lambda: ((re + im) * h, (im - re) * h),
        ][turn]()
    return re * c - im * s, re * s + im * c


def cadd(a, b):
    return a[0] + b[0], a[1] + b[1]


def csub(a, b):
    return a[0] - b[0], a[1] - b[1]


def add_turned(a, b, sign):
    if sign > 0:
        return a[0] - b[1], a[1] + b[0]
    return a[0] + b[1], a[1] - b[0]


def dft4(x, sign):
    s0, d0 = cadd(x[0], x[2]), csub(x[0], x[2])
    s1, d1 = cadd(x[1], x[3]), csub(x[1], x[3])
    return [cadd(s0, s1), add_turned(d0, d1, sign), csub(s0, s1), add_turned(d0, d1, -sign)]


def dft8(x, sign):
    even = dft4(x[0::2], sign)
    odd = dft4(x[1::2], sign)
    out = [None] * 8
    h = math.sqrt(0.5)
    for k in range(4):
        if k == 2:
            out[2] = add_turned(even[2], odd[2], sign)
            out[6] = add_turned(even[2], odd[2], -sign)
            continue
        turned = odd[k] if k == 0 else cmul(odd[k], sign * k * math.pi / 4)
        out[k] = cadd(even[k], turned)
        out[k + 4] = csub(even[k], turned)
    return out


def row(ref_value, r):
    return ref_value[r * SUBS : (r + 1) * SUBS]


def pair_up(a, b):
    return jnp.concatenate([a, b], 0)


def split(x):
    high = x.astype(BF16)
    low = (x - high.astype(F32)).astype(BF16)
    return high, low


def root(x):
    return x * lax.rsqrt(jnp.maximum(x, TINY))


def dot(a, b):
    return jnp.dot(a, b, preferred_element_type=F32)


def row_masks(first, start, end):
    masks = []
    for r in range(EXT):
        here = first + (r - HALO)
        masks.append(jnp.where((here >= start) & (here < end), 1.0, 0.0).astype(F32))
    return masks


def added(*terms):
    total = None
    for term in terms:
        if term is not None:
            total = term if total is None else total + term
    return total


class Look:
    def __init__(self, first, start, end, own32, other, box_t, coherence, ml, part):
        self.masks = row_masks(first, start, end)
        self.own32, self.other, self.box_t = own32, other, box_t
        self.coherence, self.ml, self.part = coherence, ml, part
        sub = lax.broadcasted_iota(jnp.int32, (SUBS, LANES), 0)
        lane = lax.broadcasted_iota(jnp.int32, (SUBS, LANES), 1)
        self.low_half = lane < LANES // 2
        self.inner = jnp.where(
            self.low_half, jnp.where(sub > 0, 1.0, 0.0), jnp.where(sub < SUBS - 1, 1.0, 0.0)
        )

    def products(self, q):
        at = pl.ds(q * 16, 16)
        c_re2 = self.other(0, at).astype(F32)
        c_im2 = self.other(1, at).astype(F32)
        rows = []
        for half in range(2):
            m = self.masks[2 * q + half]
            one = pl.ds((2 * q + half) * SUBS, SUBS)
            a_re = self.own32[0, one, :] * m
            a_im = self.own32[1, one, :] * m
            c_re, c_im = row(c_re2, half), row(c_im2, half)
            rows.append(
                (
                    a_re * c_re + a_im * c_im,
                    a_im * c_re - a_re * c_im,
                    self.own32[2, one, :] * m,
                    (c_re * c_re + c_im * c_im) * m,
                )
            )
        return rows

    def boxed(self, y, place):
        both = row(y, place)
        side = both[:, LANES:]
        side = jnp.where(self.low_half, pltpu.roll(side, 1, 0), pltpu.roll(side, SUBS - 1, 0))
        return both[:, 0:LANES] + side * self.inner

    def put(self, r, re, im, p1, p2):
        self.ml[0, pl.ds(r * SUBS, SUBS), :] = re
        self.ml[1, pl.ds(r * SUBS, SUBS), :] = im
        size = root(re * re + im * im)
        down = lax.rsqrt(p1 * p2 + 1e-6 * BOX_RATIO * BOX_RATIO)
        self.coherence[r // 8, pl.ds(r % 8, SUBS, stride=8), :] = size * (down * self.masks[r + HALO])


EDGE_ROWS = (0, 1, ROWS - 2, ROWS - 1)


def multilook(look, box_in):
    kept = [[None, None] for _ in range(4)]

    def add_products(q):
        for fields in look.products(q):
            for f in range(4):
                kept[f].append(fields[f])

    add_products(1)
    two = [[None, kept[f][2], kept[f][2] + kept[f][3]] for f in range(4)]
    for g in range(ROWS // SUBS):
        for q in range(4):
            tile = 2 + g * 4 + q
            if tile < EXT // 2 - 1:
                add_products(tile)
            else:
                for f in range(4):
                    kept[f] += [None, None]
            for f in range(4):
                sums = []
                for half in range(2):
                    r = g * 8 + q * 2 + half
                    two[f].append(added(kept[f][r + 3], kept[f][r + 4]))
                    sums.append(added(kept[f][r], added(two[f][r + 1], two[f][r + 3])))
                high, low = split(pair_up(*sums))
                at = pl.ds(f * 64 + q * 16, 16)
                box_in[g % 2, at, 0:LANES] = high
                box_in[g % 2, at, LANES : 2 * LANES] = low
        y = yield box_in[g % 2], look.box_t
        for n in range(8):
            r = g * 8 + n
            fields = [look.boxed(y, f * 8 + n) for f in range(4)]
            if r in EDGE_ROWS:
                at = pl.ds(EDGE_ROWS.index(r) * SUBS, SUBS)
                look.ml[0, pl.ds(r * SUBS, SUBS), :] = fields[0]
                look.ml[1, pl.ds(r * SUBS, SUBS), :] = fields[1]
                look.part[0, at, :] = fields[2]
                look.part[1, at, :] = fields[3]
            else:
                look.put(r, *fields)


def add_halo(look, halo_in):
    before = look.products(0)
    after = look.products(EXT // 2 - 1)
    for f in range(4):
        for n, rows in enumerate(
            [(before[0][f] + before[1][f], before[1][f]), (after[0][f], after[0][f] + after[1][f])]
        ):
            high, low = split(pair_up(*rows))
            at = pl.ds(f * 32 + n * 16, 16)
            halo_in[at, 0:LANES] = high
            halo_in[at, LANES : 2 * LANES] = low
    y = yield halo_in[...], look.box_t
    for n, r in enumerate(EDGE_ROWS):
        at, here = pl.ds(n * SUBS, SUBS), pl.ds(r * SUBS, SUBS)
        held = [look.ml[0, here, :], look.ml[1, here, :], look.part[0, at, :], look.part[1, at, :]]
        look.put(r, *[held[f] + look.boxed(y, f * 4 + n) for f in range(4)])


def goldstein(first, start, end, tables, ml, filtered, mid, spec_in, mags, mag_in):
    forward_t, inverse_t, near_t, same_t = tables
    masks = row_masks(first, start, end)

    for b in range(8):
        x = [
            (ml[0, pl.ds((b + 8 * a) * SUBS, SUBS), :], ml[1, pl.ds((b + 8 * a) * SUBS, SUBS), :])
            for a in range(4)
        ]
        x = dft4(x, -1)
        for k1 in range(4):
            v = cmul(x[k1], -2 * math.pi * b * k1 / 32)
            mid[0, pl.ds((k1 * 8 + b) * SUBS, SUBS), :] = v[0]
            mid[1, pl.ds((k1 * 8 + b) * SUBS, SUBS), :] = v[1]

    def put_split(place, parts):
        for c in range(2):
            high, low = split(pair_up(parts[0][c], parts[1][c]))
            at = pl.ds(place * SUBS, 16)
            spec_in[at, c * LANES : (c + 1) * LANES] = high
            spec_in[at, (2 + c) * LANES : (3 + c) * LANES] = low

    for k1 in range(4):
        x = [
            (mid[0, pl.ds((k1 * 8 + b) * SUBS, SUBS), :], mid[1, pl.ds((k1 * 8 + b) * SUBS, SUBS), :])
            for b in range(8)
        ]
        x = dft8(x, -1)
        for k2 in range(0, 8, 2):
            put_split(k1 * 8 + k2, x[k2 : k2 + 2])

    both = spec_in[...]
    s = yield jnp.concatenate([both, both[:, 0 : 2 * LANES]], 1), forward_t
    for p in range(ROWS):
        at = pl.ds(p * SUBS, SUBS)
        re, im = row(s, p)[:, 0:LANES], row(s, p)[:, LANES:]
        mid[0, at, :] = re
        mid[1, at, :] = im
        mags[at, :] = root(re * re + im * im)

    def place(k):
        k = k % PATCH
        return (k % 4) * 8 + k // 4

    total = None
    for p in range(0, ROWS, 2):
        sums = []
        for k in (p // 8 + 4 * (p % 8), p // 8 + 4 * (p % 8 + 1)):
            sums.append(
                mags[pl.ds(place(k - 1) * SUBS, SUBS), :]
                + mags[pl.ds(place(k) * SUBS, SUBS), :]
                + mags[pl.ds(place(k + 1) * SUBS, SUBS), :]
            )
            total = sums[-1] if total is None else total + sums[-1]
        high, low = split(pair_up(*sums))
        mag_in[pl.ds(p * SUBS, 16), 0:LANES] = high
        mag_in[pl.ds(p * SUBS, 16), LANES:] = low
    high, low = split(pair_up(total, total))
    tile_sum = yield jnp.concatenate([high, low], 1), same_t
    tile_sum = tile_sum[0:SUBS]
    inv = (1.0 / 9.0) / (tile_sum * (1.0 / (3 * PATCH * PATCH)) + 1e-6 / (PATCH * PATCH))
    smooth = yield mag_in[...], near_t
    for p in range(0, ROWS, 2):
        parts = []
        for n in (p, p + 1):
            w = root(row(smooth, n) * inv)
            at = pl.ds(n * SUBS, SUBS)
            parts.append((mid[0, at, :] * w, mid[1, at, :] * w))
        put_split(p, parts)

    both = spec_in[...]
    s = yield jnp.concatenate([both, both[:, 0 : 2 * LANES]], 1), inverse_t
    for k1 in range(4):
        x = [
            (row(s, k1 * 8 + k2)[:, 0:LANES], row(s, k1 * 8 + k2)[:, LANES:])
            for k2 in range(8)
        ]
        x = dft8(x, 1)
        for b in range(8):
            v = cmul(x[b], 2 * math.pi * b * k1 / 32)
            at = pl.ds((k1 * 8 + b) * SUBS, SUBS)
            mid[0, at, :] = v[0]
            mid[1, at, :] = v[1]
    for b in range(8):
        x = [
            (mid[0, pl.ds((k1 * 8 + b) * SUBS, SUBS), :], mid[1, pl.ds((k1 * 8 + b) * SUBS, SUBS), :])
            for k1 in range(4)
        ]
        x = dft4(x, 1)
        for a in range(4):
            r = b + 8 * a
            filtered[0, a, pl.ds(b, SUBS, stride=8), :] = x[a][0] * masks[r + HALO]
            filtered[1, a, pl.ds(b, SUBS, stride=8), :] = x[a][1] * masks[r + HALO]


def place_of(turn):
    return turn + lax.div(turn, 2) * (5 - 2 * turn)


def together(parts):
    asked = [next(part) for part in parts]
    while asked:
        made = dot(jnp.concatenate([left for left, _ in asked], 0), asked[0][1][...])
        rows = made.shape[0] // len(parts)
        following = []
        for n, part in enumerate(parts):
            try:
                following.append(part.send(made[n * rows : (n + 1) * rows]))
            except StopIteration:
                pass
        asked = following


def compute_all(
    first, partner, valid, own32, other, tables, coherence, filtered, work, before_look, before_halo, after
):
    box_in, halo_in, ml, part, *rest = work
    box_t, *filter_t = tables
    turns = 4

    def look_of(rnd, i):
        which = partner[0, i, rnd]

        def image(c, at):
            return jnp.where(which == 0, other[rnd, 0, c, at, :], other[rnd, 1, c, at, :])

        return Look(
            first, valid[i, 0, rnd], valid[i, 1, rnd], own32.at[i], image, box_t, coherence.at[rnd, i],
            ml.at[rnd, i], part.at[rnd, i],
        )

    def look_turn(turn):
        before_look(turn)
        rnd = place_of(turn)
        together([multilook(look_of(rnd, i), box_in.at[i]) for i in range(2)])

    def halo_turn(turn):
        before_halo(turn)
        rnd = place_of(turn)
        together([add_halo(look_of(rnd, i), halo_in.at[i]) for i in range(2)])

    def filter_turn(turn):
        halo_turn(turn)
        rnd = place_of(turn)
        together(
            [
                goldstein(
                    first, valid[i, 0, rnd], valid[i, 1, rnd], filter_t, ml.at[rnd, i], filtered.at[rnd, i],
                    *[ref.at[i] for ref in rest],
                )
                for i in range(2)
            ]
        )
        after(turn)

    def step(n, carry):
        looks = (n < turns - 1) | (n == turns)

        @pl.when(looks)
        def _():
            look_turn(jnp.minimum(n, turns - 1))

        @pl.when(jnp.logical_not(looks))
        def _():
            filter_turn(n - (turns - 1) - lax.div(n, turns + 1))

        return carry

    lax.fori_loop(0, 2 * turns, step, 0)


def work_shapes():
    return [
        pltpu.VMEM((2, 2, 256, 2 * LANES), BF16),
        pltpu.VMEM((2, 128, 2 * LANES), BF16),
        pltpu.VMEM((4, 2, 2, BODY, LANES), F32),
        pltpu.VMEM((4, 2, 2, 4 * SUBS, LANES), F32),
        pltpu.VMEM((2, 2, BODY, LANES), F32),
        pltpu.VMEM((2, BODY, 4 * LANES), BF16),
        pltpu.VMEM((2, BODY, LANES), F32),
        pltpu.VMEM((2, BODY, 2 * LANES), BF16),
    ]


def exchange_kernel(
    partner_hbm, valid_hbm, slc_hbm, box_h, forward_h, inverse_h, near_h, same_h,
    coherence_hbm, filtered_hbm,
    own32, other, coherence, filtered, box_t, forward_t, inverse_t, near_t, same_t,
    slc, own, lines, partner, valid, load_sem, out_sem,
    far_sem, halo_send, halo_recv, piece_send, piece_recv, main_send, main_recv, edge_send, edge_recv, fwd_send, fwd_recv, *work,
):
    date = lax.axis_index("date")
    strip = lax.axis_index("strip")
    n_strip = lax.axis_size("strip")

    def xor(bits):
        target = date
        for bit in range(4):
            if bits >> bit & 1:
                size = 1 << bit
                target = target + size - 2 * size * lax.rem(lax.div(date, size), 2)
        return target

    mate, onward = xor(1), xor(6)
    partners = {0: mate, 1: xor(2), 2: xor(4), 3: xor(8)}
    has_above, has_below = strip > 0, strip < n_strip - 1
    far_upper, far_lower = strip == n_strip // 2 - 1, strip == n_strip // 2

    barrier = pltpu.get_barrier_semaphore()

    def greet(device):
        pl.semaphore_signal(barrier, inc=1, device_id=device, device_id_type=MESH)

    @pl.when(has_above & jnp.logical_not(far_lower))
    def _():
        greet((date, strip - 1))
        greet((mate, strip - 1))

    @pl.when(has_below)
    def _():
        greet((date, strip + 1))
        greet((mate, strip + 1))

    for device in (*partners.values(), onward):
        greet((device, strip))

    loads = []
    for n, (src, dst) in enumerate(
        [
            (slc_hbm, slc),
            (partner_hbm, partner),
            (valid_hbm, valid),
            (box_h, box_t),
            (forward_h, forward_t),
            (near_h, near_t),
            (same_h, same_t),
            (inverse_h, inverse_t),
        ]
    ):
        loads.append(pltpu.make_async_copy(src, dst, load_sem.at[n]))
        loads[-1].start()

    loads[0].wait()
    for i in range(2):
        for c in range(2):
            for g in range(4):
                for j in range(8):
                    lines[i * 2 + c, g, pl.ds(j * 8, 8), :] = slc[
                        i, c, pl.ds(g * 8, 8), pl.ds(j * LANES, LANES)
                    ].astype(F32)
            for g in range(4):
                for s in range(0, 8, 2):
                    pair = jnp.concatenate(
                        [
                            lines[i * 2 + c, g, pl.ds(s, 8, stride=8), :],
                            lines[i * 2 + c, g, pl.ds(s + 1, 8, stride=8), :],
                        ],
                        0,
                    )
                    own[i, c, pl.ds(EDGE + (g * 8 + s) * SUBS, 16), :] = pair.astype(BF16)

    top, bottom = pl.ds(0, EDGE), pl.ds(FULL - EDGE, EDGE)
    first_rows, last_rows = pl.ds(EDGE, EDGE), pl.ds(FULL - 2 * EDGE, EDGE)
    body = pl.ds(EDGE, BODY)
    blank = jnp.zeros((EDGE, LANES), BF16)

    @pl.when(jnp.logical_not(has_above))
    def _():
        for i in range(2):
            for c in range(2):
                own[i, c, top, :] = blank
                other[0, i, c, top, :] = blank

    @pl.when(jnp.logical_not(has_below))
    def _():
        for i in range(2):
            for c in range(2):
                own[i, c, bottom, :] = blank
                other[0, i, c, bottom, :] = blank

    def remote(src, dst, send_sem, recv_sem, device):
        return pltpu.make_async_remote_copy(
            src_ref=src, dst_ref=dst, send_sem=send_sem, recv_sem=recv_sem, device_id=device, device_id_type=MESH
        )

    up = [
        remote(own.at[:, :, first_rows], own.at[:, :, bottom], halo_send.at[0], halo_recv.at[0], (date, strip - 1)),
        remote(
            own.at[:, :, first_rows], other.at[0, :, :, bottom], halo_send.at[2], halo_recv.at[2], (mate, strip - 1)
        ),
    ]
    down = [
        remote(own.at[:, :, last_rows], own.at[:, :, top], halo_send.at[1], halo_recv.at[1], (date, strip + 1)),
        remote(own.at[:, :, last_rows], other.at[0, :, :, top], halo_send.at[3], halo_recv.at[3], (mate, strip + 1)),
    ]
    inside = has_above & has_below & jnp.logical_not(far_upper)

    @pl.when(inside)
    def _():
        pl.semaphore_wait(barrier, 9)

    @pl.when(jnp.logical_not(inside))
    def _():
        pl.semaphore_wait(barrier, 7)

    @pl.when(far_lower)
    def _():
        for device in (date, mate):
            pl.semaphore_signal(far_sem, inc=1, device_id=(device, strip - 1), device_id_type=MESH)

    @pl.when(has_above)
    def _():
        for copy in up:
            copy.start()

    @pl.when(has_below & jnp.logical_not(far_upper))
    def _():
        for copy in down:
            copy.start()

    mains, pieces = {}, {}
    halves = [pl.ds(EDGE + h * (BODY // 2), BODY // 2) for h in range(2)]
    for i in range(2):
        for c in range(2):
            for h, at in enumerate(halves):
                pieces[i, c, h] = remote(
                    own.at[i, c, at],
                    other.at[1, i, c, at],
                    piece_send.at[i, c, h],
                    piece_recv.at[i, c, h],
                    (partners[1], strip),
                )
                pieces[i, c, h].start()
            for n, r in ((1, 3), (2, 0)):
                mains[r, i, c] = remote(
                    own.at[i, c, body],
                    other.at[r, i, c, body],
                    main_send.at[n - 1, i, c],
                    main_recv.at[n - 1, i, c],
                    (partners[r], strip),
                )
                mains[r, i, c].start()

    def widen(i, q):
        at = pl.ds(q * 16, 16)
        re = own[i, 0, at, :].astype(F32)
        im = own[i, 1, at, :].astype(F32)
        own32[i, 0, at, :] = re
        own32[i, 1, at, :] = im
        own32[i, 2, at, :] = re * re + im * im

    for i in range(2):
        for q in range(1, EXT // 2 - 1):
            widen(i, q)

    forwards, edges = {}, {}
    for i in range(2):
        for c in range(2):
            for h, at in enumerate(halves):
                forwards[i, c, h] = remote(
                    other.at[1, i, c, at],
                    other.at[2, i, c, at],
                    fwd_send.at[i, c, h],
                    fwd_recv.at[i, c, h],
                    (onward, strip),
                )
    for n, r in enumerate((1, 2, 3)):
        for side, at in enumerate((top, bottom)):
            edges[r, side] = remote(
                own.at[:, :, at],
                other.at[r, :, :, at],
                edge_send.at[n, side],
                edge_recv.at[n, side],
                (partners[r], strip),
            )

    far = far_upper | far_lower

    def take_halo():
        @pl.when(has_below)
        def _():
            up[0].wait_recv()

        @pl.when(has_above)
        def _():
            down[0].wait_recv()

        for copy in edges.values():
            copy.start()
        for i in range(2):
            for q in (0, EXT // 2 - 1):
                widen(i, q)

    def send_far():
        pl.semaphore_wait(far_sem, 2)
        for copy in down:
            copy.start()

    def before_look(turn):
        @pl.when(turn == 0)
        def _():
            for i in range(2):
                for c in range(2):
                    mains[0, i, c].wait_recv()
            for copy in loads[1:]:
                copy.wait()

        @pl.when(turn == 1)
        def _():
            @pl.when(jnp.logical_not(far))
            def _():
                take_halo()

            for i in range(2):
                for c in range(2):
                    for h in range(2):
                        pieces[i, c, h].wait_recv()
                        forwards[i, c, h].start()
                if i == 0:

                    @pl.when(far_upper)
                    def _():
                        send_far()

        @pl.when(turn == 2)
        def _():
            for i in range(2):
                for c in range(2):
                    mains[3, i, c].wait_recv()

        @pl.when(turn == 3)
        def _():
            for copy in forwards.values():
                copy.wait_recv()

    def before_halo(turn):
        @pl.when(turn == 0)
        def _():
            @pl.when(far)
            def _():
                take_halo()

            @pl.when(has_below)
            def _():
                up[1].wait_recv()

            @pl.when(has_above)
            def _():
                down[1].wait_recv()

        for n, r in ((1, 1), (2, 3), (3, 2)):

            @pl.when(turn == n)
            def _(r=r):
                edges[r, 0].wait_recv()
                edges[r, 1].wait_recv()

    def outputs(turn):
        rnd = place_of(turn)
        return [
            pltpu.make_async_copy(coherence.at[rnd], coherence_hbm.at[rnd], out_sem.at[0, turn]),
            pltpu.make_async_copy(filtered.at[rnd], filtered_hbm.at[rnd], out_sem.at[1, turn]),
        ]

    def after(turn):
        for copy in outputs(turn):
            copy.start()

    tables = (box_t, forward_t, inverse_t, near_t, same_t)
    compute_all(
        strip * ROWS, partner, valid, own32, other, tables, coherence, filtered, work, before_look, before_halo, after,
    )

    @pl.when(has_above)
    def _():
        for copy in up:
            copy.wait_send()

    @pl.when(has_below)
    def _():
        for copy in down:
            copy.wait_send()

    for copy in (*pieces.values(), *mains.values(), *edges.values(), *forwards.values()):
        copy.wait_send()
    for turn in range(4):
        for copy in outputs(jnp.int32(turn)):
            copy.wait()


def exchange(partner, valid, slc, tables):
    hbm = pl.BlockSpec(memory_space=pltpu.HBM)
    dma = pltpu.SemaphoreType.DMA
    return pl.pallas_call(
        exchange_kernel,
        out_shape=(
            jax.ShapeDtypeStruct((4, 2, 4, 64, LANES), F32),
            jax.ShapeDtypeStruct((4, 2, 2, 4, 64, LANES), F32),
        ),
        in_specs=[hbm] * 8,
        out_specs=(hbm, hbm),
        scratch_shapes=[
            pltpu.VMEM((2, 3, FULL, LANES), F32),
            pltpu.VMEM((4, 2, 2, FULL, LANES), BF16),
            pltpu.VMEM((4, 2, 4, 64, LANES), F32),
            pltpu.VMEM((4, 2, 2, 4, 64, LANES), F32),
        ]
        + [pltpu.VMEM(t.shape, t.dtype) for t in tables]
        + [
            pltpu.VMEM(slc.shape, BF16),
            pltpu.VMEM((2, 2, FULL, LANES), BF16),
            pltpu.VMEM((4, 4, 64, LANES), F32),
            pltpu.SMEM(partner.shape, jnp.int32),
            pltpu.SMEM(valid.shape, jnp.int32),
            dma((8,)),
            dma((2, 4)),
            pltpu.SemaphoreType.REGULAR,
            dma((4,)),
            dma((4,)),
            dma((2, 2, 2)),
            dma((2, 2, 2)),
            dma((2, 2, 2)),
            dma((2, 2, 2)),
            dma((3, 2)),
            dma((3, 2)),
            dma((2, 2, 2)),
            dma((2, 2, 2)),
        ]
        + work_shapes(),
        compiler_params=pltpu.CompilerParams(
            collective_id=0, has_side_effects=True, vmem_limit_bytes=60 * 1024 * 1024
        ),
        name="interferograms",
    )(partner, valid, slc, *tables)


def hand_on_kernel(done_coherence, done_filtered, coherence_hbm, filtered_hbm, coherence, filtered, in_sem, out_sem):
    ins, outs = [], []
    for rnd in range(4):
        for i in range(2):
            for n, (src, by, dst) in enumerate(
                [(done_filtered, filtered, filtered_hbm), (done_coherence, coherence, coherence_hbm)]
            ):
                ins.append(pltpu.make_async_copy(src.at[rnd, i], by.at[rnd, i], in_sem.at[n, rnd, i]))
                outs.append(pltpu.make_async_copy(by.at[rnd, i], dst.at[rnd, i], out_sem.at[n, rnd, i]))
    for copy in ins:
        copy.start()
    for copy_in, copy_out in zip(ins, outs):
        copy_in.wait()
        copy_out.start()
    for copy in outs:
        copy.wait()


def hand_on(coherence, filtered):
    hbm = pl.BlockSpec(memory_space=pltpu.HBM)
    dma = pltpu.SemaphoreType.DMA
    return pl.pallas_call(
        hand_on_kernel,
        out_shape=(
            jax.ShapeDtypeStruct(coherence.shape, F32),
            jax.ShapeDtypeStruct(filtered.shape, F32),
        ),
        in_specs=[hbm, hbm],
        out_specs=(hbm, hbm),
        scratch_shapes=[
            pltpu.VMEM(coherence.shape, F32),
            pltpu.VMEM(filtered.shape, F32),
            dma((2, 4, 2)),
            dma((2, 4, 2)),
        ],
        compiler_params=pltpu.CompilerParams(vmem_limit_bytes=60 * 1024 * 1024),
        name="hand_on",
    )(coherence, filtered)


def untile(array):
    lead = array.shape[:-3]
    array = array.reshape(lead + (4, 8, 8, LANES))
    n = len(lead)
    array = array.transpose(tuple(range(n)) + (n, n + 2, n + 1, n + 3))
    return array.reshape(lead + (ROWS, 8 * LANES))


def shards(slc, partner, valid):
    partner = partner.transpose(1, 2, 0)
    valid = valid.transpose(1, 2, 0)
    tables = [jnp.asarray(t) for t in make_tables()]
    coherence, filtered = hand_on(*exchange(partner, valid, slc, tables))
    return untile(coherence), untile(filtered)


def solution(mesh):
    in_specs = (P("date", None, "strip", None), P(None, "date", None), P(None, "date", None))
    out_specs = (P(None, "date", "strip", None), P(None, "date", None, "strip", None))
    return jax.shard_map(shards, mesh=mesh, in_specs=in_specs, out_specs=out_specs, check_vma=False)
```

```python
import functools
import math

import jax
import jax.numpy as jnp
import numpy as np
from jax import lax
from jax.experimental import pallas as pl
from jax.experimental.pallas import tpu as pltpu
from jax.sharding import PartitionSpec as P

F32 = jnp.float32
BF16 = jnp.bfloat16
MESH = pl.DeviceIdType.MESH

PATCH = 32
LOOK_A = 5
LOOK_R = 19
HALO = 2
LANES = 128
SUBS = 8
ROWS = 32
EXT = ROWS + 2 * HALO
EDGE = HALO * SUBS
BODY = ROWS * SUBS
FULL = EXT * SUBS
TINY = 1.2e-38

BOX_SCALE = 1.0 / 128.0
BOX_RATIO = LOOK_A * LOOK_R / 128.0


def split_np(table):
    high = table.astype(np.float32).astype(jnp.bfloat16)
    low = (table - high.astype(np.float64)).astype(np.float32).astype(jnp.bfloat16)
    return high, low


def make_tables():
    lane = np.arange(LANES)
    reach = LOOK_R // 2
    centre = np.abs(lane[:, None] - lane[None, :]) <= reach
    to_next = np.abs(lane[None, :] + LANES - lane[:, None]) <= reach
    to_previous = np.abs(lane[None, :] - LANES - lane[:, None]) <= reach
    box = np.concatenate([centre, to_next | to_previous], 1) * BOX_SCALE
    box = np.concatenate([box, box], 0)

    same = lane[:, None] // PATCH == lane[None, :] // PATCH
    angle = (lane[:, None] % PATCH) * (lane[None, :] % PATCH) % PATCH * (2 * math.pi / PATCH)
    cos = np.where(same, np.cos(angle), 0.0)
    sin = np.where(same, np.sin(angle), 0.0)
    forward = np.block([[cos, -sin], [sin, cos]]) / (BOX_RATIO * PATCH * PATCH)
    inverse = np.block([[cos, sin], [-sin, cos]])
    apart = (lane[:, None] - lane[None, :]) % PATCH
    near = same & ((apart <= 1) | (apart == PATCH - 1))

    def triple(table):
        high, low = split_np(table)
        return np.concatenate([high, high, low], 0)

    def twice(table):
        return np.concatenate([table, table], 0).astype(np.float32).astype(jnp.bfloat16)

    return (
        box.astype(np.float32).astype(jnp.bfloat16),
        triple(forward),
        triple(inverse),
        twice(near),
        twice(same),
    )


def cmul(value, angle):
    re, im = value
    c, s = math.cos(angle), math.sin(angle)
    quarter = round(angle / (math.pi / 4), 9)
    if quarter == int(quarter):
        turn = int(quarter) % 8
        h = math.sqrt(0.5)
        return [
            lambda: (re, im),
            lambda: ((re - im) * h, (re + im) * h),
            lambda: (-im, re),
            lambda: (-(re + im) * h, (re - im) * h),
            lambda: (-re, -im),
            lambda: ((im - re) * h, -(re + im) * h),
            lambda: (im, -re),
            lambda: ((re + im) * h, (im - re) * h),
        ][turn]()
    return re * c - im * s, re * s + im * c


def cadd(a, b):
    return a[0] + b[0], a[1] + b[1]


def csub(a, b):
    return a[0] - b[0], a[1] - b[1]


def add_turned(a, b, sign):
    if sign > 0:
        return a[0] - b[1], a[1] + b[0]
    return a[0] + b[1], a[1] - b[0]


def dft4(x, sign):
    s0, d0 = cadd(x[0], x[2]), csub(x[0], x[2])
    s1, d1 = cadd(x[1], x[3]), csub(x[1], x[3])
    return [cadd(s0, s1), add_turned(d0, d1, sign), csub(s0, s1), add_turned(d0, d1, -sign)]


def dft8(x, sign):
    even = dft4(x[0::2], sign)
    odd = dft4(x[1::2], sign)
    out = [None] * 8
    h = math.sqrt(0.5)
    for k in range(4):
        if k == 2:
            out[2] = add_turned(even[2], odd[2], sign)
            out[6] = add_turned(even[2], odd[2], -sign)
            continue
        turned = odd[k] if k == 0 else cmul(odd[k], sign * k * math.pi / 4)
        out[k] = cadd(even[k], turned)
        out[k + 4] = csub(even[k], turned)
    return out


def row(ref_value, r):
    return ref_value[r * SUBS : (r + 1) * SUBS]


def pair_up(a, b):
    return jnp.concatenate([a, b], 0)


def split(x):
    high = x.astype(BF16)
    low = (x - high.astype(F32)).astype(BF16)
    return high, low


def root(x):
    return x * lax.rsqrt(jnp.maximum(x, TINY))


def dot(a, b):
    return jnp.dot(a, b, preferred_element_type=F32)


def row_masks(first, start, end):
    masks = []
    for r in range(EXT):
        here = first + (r - HALO)
        masks.append(jnp.where((here >= start) & (here < end), 1.0, 0.0).astype(F32))
    return masks


def added(*terms):
    total = None
    for term in terms:
        if term is not None:
            total = term if total is None else total + term
    return total


class Look:
    def __init__(self, first, start, end, own32, other, box_t, coherence, ml, part):
        self.masks = row_masks(first, start, end)
        self.own32, self.other, self.box_t = own32, other, box_t
        self.coherence, self.ml, self.part = coherence, ml, part
        sub = lax.broadcasted_iota(jnp.int32, (SUBS, LANES), 0)
        lane = lax.broadcasted_iota(jnp.int32, (SUBS, LANES), 1)
        self.low_half = lane < LANES // 2
        self.inner = jnp.where(
            self.low_half, jnp.where(sub > 0, 1.0, 0.0), jnp.where(sub < SUBS - 1, 1.0, 0.0)
        )

    def products(self, q):
        at = pl.ds(q * 16, 16)
        c_re2 = self.other(0, at).astype(F32)
        c_im2 = self.other(1, at).astype(F32)
        rows = []
        for half in range(2):
            m = self.masks[2 * q + half]
            one = pl.ds((2 * q + half) * SUBS, SUBS)
            a_re = self.own32[0, one, :] * m
            a_im = self.own32[1, one, :] * m
            c_re, c_im = row(c_re2, half), row(c_im2, half)
            rows.append(
                (
                    a_re * c_re + a_im * c_im,
                    a_im * c_re - a_re * c_im,
                    self.own32[2, one, :] * m,
                    (c_re * c_re + c_im * c_im) * m,
                )
            )
        return rows

    def boxed(self, y, place):
        both = row(y, place)
        side = both[:, LANES:]
        side = jnp.where(self.low_half, pltpu.roll(side, 1, 0), pltpu.roll(side, SUBS - 1, 0))
        return both[:, 0:LANES] + side * self.inner

    def put(self, r, re, im, p1, p2):
        self.ml[0, pl.ds(r * SUBS, SUBS), :] = re
        self.ml[1, pl.ds(r * SUBS, SUBS), :] = im
        size = root(re * re + im * im)
        down = lax.rsqrt(p1 * p2 + 1e-6 * BOX_RATIO * BOX_RATIO)
        self.coherence[r // 8, pl.ds(r % 8, SUBS, stride=8), :] = size * (down * self.masks[r + HALO])


EDGE_ROWS = (0, 1, ROWS - 2, ROWS - 1)


def multilook(look, box_in):
    kept = [[None, None] for _ in range(4)]

    def add_products(q):
        for fields in look.products(q):
            for f in range(4):
                kept[f].append(fields[f])

    add_products(1)
    two = [[None, kept[f][2], kept[f][2] + kept[f][3]] for f in range(4)]
    for g in range(ROWS // SUBS):
        for q in range(4):
            tile = 2 + g * 4 + q
            if tile < EXT // 2 - 1:
                add_products(tile)
            else:
                for f in range(4):
                    kept[f] += [None, None]
            for f in range(4):
                sums = []
                for half in range(2):
                    r = g * 8 + q * 2 + half
                    two[f].append(added(kept[f][r + 3], kept[f][r + 4]))
                    sums.append(added(kept[f][r], added(two[f][r + 1], two[f][r + 3])))
                high, low = split(pair_up(*sums))
                at = pl.ds(f * 64 + q * 16, 16)
                box_in[g % 2, at, 0:LANES] = high
                box_in[g % 2, at, LANES : 2 * LANES] = low
        y = yield box_in[g % 2], look.box_t
        for n in range(8):
            r = g * 8 + n
            fields = [look.boxed(y, f * 8 + n) for f in range(4)]
            if r in EDGE_ROWS:
                at = pl.ds(EDGE_ROWS.index(r) * SUBS, SUBS)
                look.ml[0, pl.ds(r * SUBS, SUBS), :] = fields[0]
                look.ml[1, pl.ds(r * SUBS, SUBS), :] = fields[1]
                look.part[0, at, :] = fields[2]
                look.part[1, at, :] = fields[3]
            else:
                look.put(r, *fields)


def add_halo(look, halo_in):
    before = look.products(0)
    after = look.products(EXT // 2 - 1)
    for f in range(4):
        for n, rows in enumerate(
            [(before[0][f] + before[1][f], before[1][f]), (after[0][f], after[0][f] + after[1][f])]
        ):
            high, low = split(pair_up(*rows))
            at = pl.ds(f * 32 + n * 16, 16)
            halo_in[at, 0:LANES] = high
            halo_in[at, LANES : 2 * LANES] = low
    y = yield halo_in[...], look.box_t
    for n, r in enumerate(EDGE_ROWS):
        at, here = pl.ds(n * SUBS, SUBS), pl.ds(r * SUBS, SUBS)
        held = [look.ml[0, here, :], look.ml[1, here, :], look.part[0, at, :], look.part[1, at, :]]
        look.put(r, *[held[f] + look.boxed(y, f * 4 + n) for f in range(4)])


def goldstein(first, start, end, tables, ml, filtered, mid, spec_in, mags, mag_in):
    forward_t, inverse_t, near_t, same_t = tables
    masks = row_masks(first, start, end)

    for b in range(8):
        x = [
            (ml[0, pl.ds((b + 8 * a) * SUBS, SUBS), :], ml[1, pl.ds((b + 8 * a) * SUBS, SUBS), :])
            for a in range(4)
        ]
        x = dft4(x, -1)
        for k1 in range(4):
            v = cmul(x[k1], -2 * math.pi * b * k1 / 32)
            mid[0, pl.ds((k1 * 8 + b) * SUBS, SUBS), :] = v[0]
            mid[1, pl.ds((k1 * 8 + b) * SUBS, SUBS), :] = v[1]

    def put_split(place, parts):
        for c in range(2):
            high, low = split(pair_up(parts[0][c], parts[1][c]))
            at = pl.ds(place * SUBS, 16)
            spec_in[at, c * LANES : (c + 1) * LANES] = high
            spec_in[at, (2 + c) * LANES : (3 + c) * LANES] = low

    for k1 in range(4):
        x = [
            (mid[0, pl.ds((k1 * 8 + b) * SUBS, SUBS), :], mid[1, pl.ds((k1 * 8 + b) * SUBS, SUBS), :])
            for b in range(8)
        ]
        x = dft8(x, -1)
        for k2 in range(0, 8, 2):
            put_split(k1 * 8 + k2, x[k2 : k2 + 2])

    both = spec_in[...]
    s = yield jnp.concatenate([both, both[:, 0 : 2 * LANES]], 1), forward_t
    for p in range(ROWS):
        at = pl.ds(p * SUBS, SUBS)
        re, im = row(s, p)[:, 0:LANES], row(s, p)[:, LANES:]
        mid[0, at, :] = re
        mid[1, at, :] = im
        mags[at, :] = root(re * re + im * im)

    def place(k):
        k = k % PATCH
        return (k % 4) * 8 + k // 4

    total = None
    for p in range(0, ROWS, 2):
        sums = []
        for k in (p // 8 + 4 * (p % 8), p // 8 + 4 * (p % 8 + 1)):
            sums.append(
                mags[pl.ds(place(k - 1) * SUBS, SUBS), :]
                + mags[pl.ds(place(k) * SUBS, SUBS), :]
                + mags[pl.ds(place(k + 1) * SUBS, SUBS), :]
            )
            total = sums[-1] if total is None else total + sums[-1]
        high, low = split(pair_up(*sums))
        mag_in[pl.ds(p * SUBS, 16), 0:LANES] = high
        mag_in[pl.ds(p * SUBS, 16), LANES:] = low
    high, low = split(pair_up(total, total))
    tile_sum = yield jnp.concatenate([high, low], 1), same_t
    tile_sum = tile_sum[0:SUBS]
    inv = (1.0 / 9.0) / (tile_sum * (1.0 / (3 * PATCH * PATCH)) + 1e-6 / (PATCH * PATCH))
    smooth = yield mag_in[...], near_t
    for p in range(0, ROWS, 2):
        parts = []
        for n in (p, p + 1):
            w = root(row(smooth, n) * inv)
            at = pl.ds(n * SUBS, SUBS)
            parts.append((mid[0, at, :] * w, mid[1, at, :] * w))
        put_split(p, parts)

    both = spec_in[...]
    s = yield jnp.concatenate([both, both[:, 0 : 2 * LANES]], 1), inverse_t
    for k1 in range(4):
        x = [
            (row(s, k1 * 8 + k2)[:, 0:LANES], row(s, k1 * 8 + k2)[:, LANES:])
            for k2 in range(8)
        ]
        x = dft8(x, 1)
        for b in range(8):
            v = cmul(x[b], 2 * math.pi * b * k1 / 32)
            at = pl.ds((k1 * 8 + b) * SUBS, SUBS)
            mid[0, at, :] = v[0]
            mid[1, at, :] = v[1]
    for b in range(8):
        x = [
            (mid[0, pl.ds((k1 * 8 + b) * SUBS, SUBS), :], mid[1, pl.ds((k1 * 8 + b) * SUBS, SUBS), :])
            for k1 in range(4)
        ]
        x = dft4(x, 1)
        for a in range(4):
            r = b + 8 * a
            filtered[0, a, pl.ds(b, SUBS, stride=8), :] = x[a][0] * masks[r + HALO]
            filtered[1, a, pl.ds(b, SUBS, stride=8), :] = x[a][1] * masks[r + HALO]


def place_of(turn):
    return turn + lax.div(turn, 2) * (5 - 2 * turn)


def together(parts):
    asked = [next(part) for part in parts]
    while asked:
        made = dot(jnp.concatenate([left for left, _ in asked], 0), asked[0][1][...])
        rows = made.shape[0] // len(parts)
        following = []
        for n, part in enumerate(parts):
            try:
                following.append(part.send(made[n * rows : (n + 1) * rows]))
            except StopIteration:
                pass
        asked = following


def compute_all(
    first, partner, valid, own32, other, tables, coherence, filtered, work, before_look, before_halo, after
):
    box_in, halo_in, ml, part, *rest = work
    box_t, *filter_t = tables
    turns = 4

    def look_of(rnd, i):
        which = partner[0, i, rnd]

        def image(c, at):
            return jnp.where(which == 0, other[rnd, 0, c, at, :], other[rnd, 1, c, at, :])

        return Look(
            first, valid[i, 0, rnd], valid[i, 1, rnd], own32.at[i], image, box_t, coherence.at[rnd, i],
            ml.at[rnd, i], part.at[rnd, i],
        )

    def look_turn(turn):
        before_look(turn)
        rnd = place_of(turn)
        together([multilook(look_of(rnd, i), box_in.at[i]) for i in range(2)])

    def halo_turn(turn):
        before_halo(turn)
        rnd = place_of(turn)
        together([add_halo(look_of(rnd, i), halo_in.at[i]) for i in range(2)])

    def filter_turn(turn):
        halo_turn(turn)
        after(turn, 0)
        rnd = place_of(turn)
        together(
            [
                goldstein(
                    first, valid[i, 0, rnd], valid[i, 1, rnd], filter_t, ml.at[rnd, i], filtered.at[rnd, i],
                    *[ref.at[i] for ref in rest],
                )
                for i in range(2)
            ]
        )
        after(turn, 1)

    def step(n, carry):
        looks = (n < turns - 1) | (n == turns)

        @pl.when(looks)
        def _():
            look_turn(jnp.minimum(n, turns - 1))

        @pl.when(jnp.logical_not(looks))
        def _():
            filter_turn(n - (turns - 1) - lax.div(n, turns + 1))

        return carry

    lax.fori_loop(0, 2 * turns, step, 0)


def work_shapes():
    return [
        pltpu.VMEM((2, 2, 256, 2 * LANES), BF16),
        pltpu.VMEM((2, 128, 2 * LANES), BF16),
        pltpu.VMEM((4, 2, 2, BODY, LANES), F32),
        pltpu.VMEM((4, 2, 2, 4 * SUBS, LANES), F32),
        pltpu.VMEM((2, 2, BODY, LANES), F32),
        pltpu.VMEM((2, BODY, 4 * LANES), BF16),
        pltpu.VMEM((2, BODY, LANES), F32),
        pltpu.VMEM((2, BODY, 2 * LANES), BF16),
    ]


def exchange_kernel(
    partner_hbm, valid_hbm, slc_hbm, box_h, forward_h, inverse_h, near_h, same_h,
    coherence_hbm, filtered_hbm,
    own32, other, coherence, filtered, box_t, forward_t, inverse_t, near_t, same_t,
    slc, own, lines, partner, valid, load_sem, out_sem,
    far_sem, halo_send, halo_recv, piece_send, piece_recv, main_send, main_recv, edge_send, edge_recv, fwd_send, fwd_recv, *work,
):
    date = lax.axis_index("date")
    strip = lax.axis_index("strip")
    n_strip = lax.axis_size("strip")

    def xor(bits):
        target = date
        for bit in range(4):
            if bits >> bit & 1:
                size = 1 << bit
                target = target + size - 2 * size * lax.rem(lax.div(date, size), 2)
        return target

    mate, onward = xor(1), xor(6)
    partners = {0: mate, 1: xor(2), 2: xor(4), 3: xor(8)}
    has_above, has_below = strip > 0, strip < n_strip - 1
    far_upper, far_lower = strip == n_strip // 2 - 1, strip == n_strip // 2

    barrier = pltpu.get_barrier_semaphore()

    def greet(device):
        pl.semaphore_signal(barrier, inc=1, device_id=device, device_id_type=MESH)

    @pl.when(has_above & jnp.logical_not(far_lower))
    def _():
        greet((date, strip - 1))
        greet((mate, strip - 1))

    @pl.when(has_below)
    def _():
        greet((date, strip + 1))
        greet((mate, strip + 1))

    for device in (*partners.values(), onward):
        greet((device, strip))

    loads = []
    for n, (src, dst) in enumerate(
        [
            (slc_hbm, slc),
            (partner_hbm, partner),
            (valid_hbm, valid),
            (box_h, box_t),
            (forward_h, forward_t),
            (near_h, near_t),
            (same_h, same_t),
            (inverse_h, inverse_t),
        ]
    ):
        loads.append(pltpu.make_async_copy(src, dst, load_sem.at[n]))
        loads[-1].start()

    loads[0].wait()
    for i in range(2):
        for c in range(2):
            for g in range(4):
                for j in range(8):
                    lines[i * 2 + c, g, pl.ds(j * 8, 8), :] = slc[
                        i, c, pl.ds(g * 8, 8), pl.ds(j * LANES, LANES)
                    ].astype(F32)
            for g in range(4):
                for s in range(0, 8, 2):
                    pair = jnp.concatenate(
                        [
                            lines[i * 2 + c, g, pl.ds(s, 8, stride=8), :],
                            lines[i * 2 + c, g, pl.ds(s + 1, 8, stride=8), :],
                        ],
                        0,
                    )
                    own[i, c, pl.ds(EDGE + (g * 8 + s) * SUBS, 16), :] = pair.astype(BF16)

    top, bottom = pl.ds(0, EDGE), pl.ds(FULL - EDGE, EDGE)
    first_rows, last_rows = pl.ds(EDGE, EDGE), pl.ds(FULL - 2 * EDGE, EDGE)
    body = pl.ds(EDGE, BODY)
    blank = jnp.zeros((EDGE, LANES), BF16)

    @pl.when(jnp.logical_not(has_above))
    def _():
        for i in range(2):
            for c in range(2):
                own[i, c, top, :] = blank
                other[0, i, c, top, :] = blank

    @pl.when(jnp.logical_not(has_below))
    def _():
        for i in range(2):
            for c in range(2):
                own[i, c, bottom, :] = blank
                other[0, i, c, bottom, :] = blank

    def remote(src, dst, send_sem, recv_sem, device):
        return pltpu.make_async_remote_copy(
            src_ref=src, dst_ref=dst, send_sem=send_sem, recv_sem=recv_sem, device_id=device, device_id_type=MESH
        )

    up = [
        remote(own.at[:, :, first_rows], own.at[:, :, bottom], halo_send.at[0], halo_recv.at[0], (date, strip - 1)),
        remote(
            own.at[:, :, first_rows], other.at[0, :, :, bottom], halo_send.at[2], halo_recv.at[2], (mate, strip - 1)
        ),
    ]
    down = [
        remote(own.at[:, :, last_rows], own.at[:, :, top], halo_send.at[1], halo_recv.at[1], (date, strip + 1)),
        remote(own.at[:, :, last_rows], other.at[0, :, :, top], halo_send.at[3], halo_recv.at[3], (mate, strip + 1)),
    ]
    inside = has_above & has_below & jnp.logical_not(far_upper)

    @pl.when(inside)
    def _():
        pl.semaphore_wait(barrier, 9)

    @pl.when(jnp.logical_not(inside))
    def _():
        pl.semaphore_wait(barrier, 7)

    @pl.when(far_lower)
    def _():
        for device in (date, mate):
            pl.semaphore_signal(far_sem, inc=1, device_id=(device, strip - 1), device_id_type=MESH)

    @pl.when(has_above)
    def _():
        for copy in up:
            copy.start()

    @pl.when(has_below & jnp.logical_not(far_upper))
    def _():
        for copy in down:
            copy.start()

    mains, pieces = {}, {}
    halves = [pl.ds(EDGE + h * (BODY // 2), BODY // 2) for h in range(2)]
    for i in range(2):
        for c in range(2):
            for h, at in enumerate(halves):
                pieces[i, c, h] = remote(
                    own.at[i, c, at],
                    other.at[1, i, c, at],
                    piece_send.at[i, c, h],
                    piece_recv.at[i, c, h],
                    (partners[1], strip),
                )
                pieces[i, c, h].start()
            for n, r in ((1, 3), (2, 0)):
                mains[r, i, c] = remote(
                    own.at[i, c, body],
                    other.at[r, i, c, body],
                    main_send.at[n - 1, i, c],
                    main_recv.at[n - 1, i, c],
                    (partners[r], strip),
                )
                mains[r, i, c].start()

    def widen(i, q):
        at = pl.ds(q * 16, 16)
        re = own[i, 0, at, :].astype(F32)
        im = own[i, 1, at, :].astype(F32)
        own32[i, 0, at, :] = re
        own32[i, 1, at, :] = im
        own32[i, 2, at, :] = re * re + im * im

    for i in range(2):
        for q in range(1, EXT // 2 - 1):
            widen(i, q)

    forwards, edges = {}, {}
    for i in range(2):
        for c in range(2):
            for h, at in enumerate(halves):
                forwards[i, c, h] = remote(
                    other.at[1, i, c, at],
                    other.at[2, i, c, at],
                    fwd_send.at[i, c, h],
                    fwd_recv.at[i, c, h],
                    (onward, strip),
                )
    for n, r in enumerate((1, 2, 3)):
        for side, at in enumerate((top, bottom)):
            edges[r, side] = remote(
                own.at[:, :, at],
                other.at[r, :, :, at],
                edge_send.at[n, side],
                edge_recv.at[n, side],
                (partners[r], strip),
            )

    far = far_upper | far_lower

    def take_halo():
        @pl.when(has_below)
        def _():
            up[0].wait_recv()

        @pl.when(has_above)
        def _():
            down[0].wait_recv()

        for copy in edges.values():
            copy.start()
        for i in range(2):
            for q in (0, EXT // 2 - 1):
                widen(i, q)

    def send_far():
        pl.semaphore_wait(far_sem, 2)
        for copy in down:
            copy.start()

    def before_look(turn):
        @pl.when(turn == 0)
        def _():
            for i in range(2):
                for c in range(2):
                    mains[0, i, c].wait_recv()
            for copy in loads[1:]:
                copy.wait()

        @pl.when(turn == 1)
        def _():
            @pl.when(jnp.logical_not(far))
            def _():
                take_halo()

            for i in range(2):
                for c in range(2):
                    for h in range(2):
                        pieces[i, c, h].wait_recv()
                        forwards[i, c, h].start()
                if i == 0:

                    @pl.when(far_upper)
                    def _():
                        send_far()

        @pl.when(turn == 2)
        def _():
            for i in range(2):
                for c in range(2):
                    mains[3, i, c].wait_recv()

        @pl.when(turn == 3)
        def _():
            for copy in forwards.values():
                copy.wait_recv()

    def before_halo(turn):
        @pl.when(turn == 0)
        def _():
            @pl.when(far)
            def _():
                take_halo()

            @pl.when(has_below)
            def _():
                up[1].wait_recv()

            @pl.when(has_above)
            def _():
                down[1].wait_recv()

        for n, r in ((1, 1), (2, 3), (3, 2)):

            @pl.when(turn == n)
            def _(r=r):
                edges[r, 0].wait_recv()
                edges[r, 1].wait_recv()

    def outputs(turn):
        rnd = place_of(turn)
        return [
            pltpu.make_async_copy(coherence.at[rnd], coherence_hbm.at[rnd], out_sem.at[0, turn]),
            pltpu.make_async_copy(filtered.at[rnd], filtered_hbm.at[rnd], out_sem.at[1, turn]),
        ]

    def after(turn, n):
        outputs(turn)[n].start()

    tables = (box_t, forward_t, inverse_t, near_t, same_t)
    compute_all(
        strip * ROWS, partner, valid, own32, other, tables, coherence, filtered, work, before_look, before_halo, after,
    )

    @pl.when(has_above)
    def _():
        for copy in up:
            copy.wait_send()

    @pl.when(has_below)
    def _():
        for copy in down:
            copy.wait_send()

    for copy in (*pieces.values(), *mains.values(), *edges.values(), *forwards.values()):
        copy.wait_send()
    for turn in range(4):
        for copy in outputs(jnp.int32(turn)):
            copy.wait()


def exchange(partner, valid, slc, tables):
    hbm = pl.BlockSpec(memory_space=pltpu.HBM)
    dma = pltpu.SemaphoreType.DMA
    return pl.pallas_call(
        exchange_kernel,
        out_shape=(
            jax.ShapeDtypeStruct((4, 2, 4, 64, LANES), F32),
            jax.ShapeDtypeStruct((4, 2, 2, 4, 64, LANES), F32),
        ),
        in_specs=[hbm] * 8,
        out_specs=(hbm, hbm),
        scratch_shapes=[
            pltpu.VMEM((2, 3, FULL, LANES), F32),
            pltpu.VMEM((4, 2, 2, FULL, LANES), BF16),
            pltpu.VMEM((4, 2, 4, 64, LANES), F32),
            pltpu.VMEM((4, 2, 2, 4, 64, LANES), F32),
        ]
        + [pltpu.VMEM(t.shape, t.dtype) for t in tables]
        + [
            pltpu.VMEM(slc.shape, BF16),
            pltpu.VMEM((2, 2, FULL, LANES), BF16),
            pltpu.VMEM((4, 4, 64, LANES), F32),
            pltpu.SMEM(partner.shape, jnp.int32),
            pltpu.SMEM(valid.shape, jnp.int32),
            dma((8,)),
            dma((2, 4)),
            pltpu.SemaphoreType.REGULAR,
            dma((4,)),
            dma((4,)),
            dma((2, 2, 2)),
            dma((2, 2, 2)),
            dma((2, 2, 2)),
            dma((2, 2, 2)),
            dma((3, 2)),
            dma((3, 2)),
            dma((2, 2, 2)),
            dma((2, 2, 2)),
        ]
        + work_shapes(),
        compiler_params=pltpu.CompilerParams(
            collective_id=0, has_side_effects=True, vmem_limit_bytes=60 * 1024 * 1024
        ),
        name="interferograms",
    )(partner, valid, slc, *tables)


def hand_on_kernel(done_coherence, done_filtered, coherence_hbm, filtered_hbm, coherence, filtered, in_sem, out_sem):
    ins, outs = [], []
    for rnd in range(4):
        for i in range(2):
            for n, (src, by, dst) in enumerate(
                [(done_filtered, filtered, filtered_hbm), (done_coherence, coherence, coherence_hbm)]
            ):
                ins.append(pltpu.make_async_copy(src.at[rnd, i], by.at[rnd, i], in_sem.at[n, rnd, i]))
                outs.append(pltpu.make_async_copy(by.at[rnd, i], dst.at[rnd, i], out_sem.at[n, rnd, i]))
    for copy in ins:
        copy.start()
    for copy_in, copy_out in zip(ins, outs):
        copy_in.wait()
        copy_out.start()
    for copy in outs:
        copy.wait()


def hand_on(coherence, filtered):
    hbm = pl.BlockSpec(memory_space=pltpu.HBM)
    dma = pltpu.SemaphoreType.DMA
    return pl.pallas_call(
        hand_on_kernel,
        out_shape=(
            jax.ShapeDtypeStruct(coherence.shape, F32),
            jax.ShapeDtypeStruct(filtered.shape, F32),
        ),
        in_specs=[hbm, hbm],
        out_specs=(hbm, hbm),
        scratch_shapes=[
            pltpu.VMEM(coherence.shape, F32),
            pltpu.VMEM(filtered.shape, F32),
            dma((2, 4, 2)),
            dma((2, 4, 2)),
        ],
        compiler_params=pltpu.CompilerParams(vmem_limit_bytes=60 * 1024 * 1024),
        name="hand_on",
    )(coherence, filtered)


def untile(array):
    lead = array.shape[:-3]
    array = array.reshape(lead + (4, 8, 8, LANES))
    n = len(lead)
    array = array.transpose(tuple(range(n)) + (n, n + 2, n + 1, n + 3))
    return array.reshape(lead + (ROWS, 8 * LANES))


def shards(slc, partner, valid):
    partner = partner.transpose(1, 2, 0)
    valid = valid.transpose(1, 2, 0)
    tables = [jnp.asarray(t) for t in make_tables()]
    coherence, filtered = hand_on(*exchange(partner, valid, slc, tables))
    return untile(coherence), untile(filtered)


def solution(mesh):
    in_specs = (P("date", None, "strip", None), P(None, "date", None), P(None, "date", None))
    out_specs = (P(None, "date", "strip", None), P(None, "date", None, "strip", None))
    return jax.shard_map(shards, mesh=mesh, in_specs=in_specs, out_specs=out_specs, check_vma=False)
```
